32 devices in a mesh: lon: 8 (over z, y), lat: 4 (over x, core).
Axes of the slice: x: 2, y: 2, z: 4, core: 2. Of those that a mesh axis runs over, the one named last changes fastest.
Arguments:
- obs_rows: bfloat16 [8, 4, 1024, 64], P('lon', 'lat'), may hold values from -6 to 6
- obs_cells: int32 [8, 4, 1024], P('lon', 'lat'), may hold values from 0 to 63
- obs_counts: int32 [8, 4], P('lon', 'lat'), may hold values from 128 to 1024, as said below
- enc_weight: bfloat16 [64, 1024], replicated, may hold values from -0.75 to 0.75
- near_kernel_weight: bfloat16 [3, 3, 64, 1024], replicated, may hold values from -0.25 to 0.25
- far_kernel_weight: bfloat16 [3, 3, 64, 1024], replicated, may hold values from -0.25 to 0.25
- mix_weight: bfloat16 [1024, 1024], replicated, may hold values from -0.1875 to 0.1875
Outputs:
- state: bfloat16 [64, 32, 1024], P('lon', 'lat')
The draws below stay inside these ranges and needn't reach their ends.
Inputs may be any that keep to these rules, and one draw needn't show every extreme that they name: `obs_cells`: cell index i * 8 + j within the sector and band; slots at or past the count are ignored. `obs_counts`: live slots come first; some sector and band has all 1024 slots live.
All inputs are finite; a program needn't handle non-finite values.
Results may differ from the reference program's by a relative error of at most 0.006.
Values may be sent and summed in bfloat16 or wider, within the bound.
No kernel may reach another device: no remote copies, remote signals or barrier semaphores. Data moves between devices by JAX's collectives and lax.ppermute only.
A program may use at most 128 MiB of HBM per device.

```python
import jax
import jax.numpy as jnp
from jax import lax

C = 1024
F_OBS = 64
FAR_DILATION = 8
BAND_LAT_CELLS = 8
R_CAP = 1024
SECTOR_LON_CELLS = 8
GW = 64
SECTORS = 8
BANDS = 4
NLON = 64
GRID_LAT_CELLS = 32


def draw_obs_counts(key, part):
    first_key = jax.random.fold_in(key, 11)
    second_key = jax.random.fold_in(key, 23)
    levels = jax.random.randint(first_key, (SECTORS, BANDS), 0, 4)
    counts = R_CAP // jnp.left_shift(jnp.ones_like(levels), levels)
    chosen = jax.random.randint(second_key, (), 0, SECTORS * BANDS)
    flat_index = jnp.arange(SECTORS * BANDS).reshape(SECTORS, BANDS)
    return jnp.where(flat_index == chosen, R_CAP, counts).astype(jnp.int32)


def with_ends(array, own_key, least, high):
    dims = array.shape
    spot = [jax.random.randint(jax.random.fold_in(own_key, axis), (), 0, dims[axis]) for axis in range(len(dims))]
    array = array.at[tuple(spot)].set(least)
    longest = dims.index(max(dims))
    spot[longest] = (spot[longest] + 1) % dims[longest]
    return array.at[tuple(spot)].set(high)


def block_levels(own_key, dims, shards, low, high):
    factor_of = 1.0
    for position, parts in shards:
        heights = jax.random.uniform(jax.random.fold_in(jax.random.fold_in(own_key, 6), position), (parts,), jnp.float32, low / len(shards), high / len(shards))
        factor_of = factor_of * jnp.repeat(jnp.exp(heights), dims[position] // parts).reshape((-1,) + (1,) * (len(dims) - 1 - position))
    return factor_of


def normal_values(stream_key, dims, scale, reach, cuts=(), kind=jnp.bfloat16):
    drawn = jax.random.normal(stream_key, dims, jnp.float32) * scale
    if len(cuts) > 0:
        drawn = block_levels(stream_key, dims, cuts, -0.22, 0.18) * drawn
    return jnp.clip(drawn, min=-reach, max=reach).astype(kind)


def setup_inputs(seed: int = 0) -> dict:
    keys = jax.random.split(jax.random.key(seed), 8)
    obs_rows = normal_values(keys[0], (SECTORS, BANDS, R_CAP, F_OBS), 1.0, 6.0, ((0, 8), (1, 4)))
    obs_cells = with_ends(jax.random.randint(keys[1], (SECTORS, BANDS, R_CAP), 0, SECTOR_LON_CELLS * BAND_LAT_CELLS), jax.random.fold_in(keys[1], 1), 0, (SECTOR_LON_CELLS * BAND_LAT_CELLS) - 1).astype(jnp.int32)
    obs_counts = draw_obs_counts(jax.random.fold_in(keys[7], 71), 0)
    enc_weight = normal_values(keys[3], (F_OBS, C), F_OBS ** -0.5, 0.75)
    near_kernel_weight = normal_values(keys[4], (3, 3, GW, C), (9 * GW) ** -0.5, 0.25)
    far_kernel_weight = normal_values(keys[5], (3, 3, GW, C), (9 * GW) ** -0.5, 0.25)
    mix_weight = normal_values(keys[6], (C, C), C ** -0.5, 0.1875)
    return {"obs_rows": obs_rows, "obs_cells": obs_cells, "obs_counts": obs_counts, "enc_weight": enc_weight, "near_kernel_weight": near_kernel_weight, "far_kernel_weight": far_kernel_weight, "mix_weight": mix_weight}


def grouped_filter(extended, lon_starts, lat_starts, rows, cols, weight):
    pieces = [extended[p:p + rows, q:q + cols] for p in lon_starts for q in lat_starts]
    stacked = jnp.stack(pieces, 0).astype(jnp.float32)
    channels = stacked.shape[-1]
    width = weight.shape[2]
    groups = channels // width
    taps = stacked.reshape(9, rows * cols, groups, width)
    kernel = weight.astype(jnp.float32).reshape(9, width, groups, width)
    return jnp.einsum('tngi,tigo->ngo', taps, kernel).reshape(rows, cols, channels)


def reference(obs_rows, obs_cells, obs_counts, enc_weight, near_kernel_weight, far_kernel_weight, mix_weight):
    slots = jnp.arange(R_CAP, dtype=jnp.int32)
    band_index = jnp.arange(BANDS, dtype=jnp.int32)[:, None]

    def encode_sector(sector):
        sector_rows = lax.dynamic_index_in_dim(obs_rows, sector, 0, keepdims=False)
        sector_cells = lax.dynamic_index_in_dim(obs_cells, sector, 0, keepdims=False)
        sector_counts = lax.dynamic_index_in_dim(obs_counts, sector, 0, keepdims=False)
        encoded = jnp.dot(sector_rows.reshape(BANDS * R_CAP, F_OBS), enc_weight,
                          preferred_element_type=jnp.float32).astype(jnp.bfloat16)
        live_slot = (slots[None, :] < sector_counts[:, None]).reshape(-1, 1)
        placed = (sector_cells // BAND_LAT_CELLS) * GRID_LAT_CELLS + band_index * BAND_LAT_CELLS + sector_cells % BAND_LAT_CELLS
        values = jnp.where(live_slot, encoded.astype(jnp.float32), jnp.zeros((), jnp.float32))
        summed = jax.ops.segment_sum(values, placed.reshape(-1).astype(jnp.int32), num_segments=SECTOR_LON_CELLS * GRID_LAT_CELLS)
        return summed.astype(jnp.bfloat16).reshape(SECTOR_LON_CELLS, GRID_LAT_CELLS, C)

    input_field = lax.map(encode_sector, jnp.arange(SECTORS, dtype=jnp.int32)).reshape(NLON, GRID_LAT_CELLS, C)
    wrapped_field = jnp.concatenate([input_field[NLON - SECTOR_LON_CELLS:], input_field, input_field[:SECTOR_LON_CELLS]], 0)
    padded_field = jnp.pad(wrapped_field, ((0, 0), (FAR_DILATION, FAR_DILATION), (0, 0)))

    def sector_out(sector):
        block_tile = lax.dynamic_slice_in_dim(padded_field, sector * SECTOR_LON_CELLS, 3 * SECTOR_LON_CELLS, 0)
        centre_cells = block_tile[SECTOR_LON_CELLS:2 * SECTOR_LON_CELLS, FAR_DILATION:FAR_DILATION + GRID_LAT_CELLS].astype(jnp.float32)
        near_output = grouped_filter(block_tile, [SECTOR_LON_CELLS - 1, SECTOR_LON_CELLS, SECTOR_LON_CELLS + 1], [FAR_DILATION - 1, FAR_DILATION, FAR_DILATION + 1], SECTOR_LON_CELLS, GRID_LAT_CELLS, near_kernel_weight)
        far_output = grouped_filter(block_tile, [0, SECTOR_LON_CELLS, 2 * SECTOR_LON_CELLS], [0, FAR_DILATION, 2 * FAR_DILATION], SECTOR_LON_CELLS, GRID_LAT_CELLS, far_kernel_weight)
        total = centre_cells + near_output + far_output
        activ = jax.nn.gelu(total, approximate=True).astype(jnp.bfloat16)
        mixed = jnp.dot(activ.reshape(SECTOR_LON_CELLS * GRID_LAT_CELLS, C), mix_weight,
                        preferred_element_type=jnp.float32).reshape(SECTOR_LON_CELLS, GRID_LAT_CELLS, C)
        return (total + mixed).astype(jnp.bfloat16)

    return lax.map(sector_out, jnp.arange(SECTORS, dtype=jnp.int32)).reshape(NLON, GRID_LAT_CELLS, C)
```

```python
import functools

import jax
import jax.numpy as jnp
from jax import lax
from jax.experimental import pallas as pl
from jax.experimental.pallas import tpu as pltpu
from jax.sharding import PartitionSpec as P

BAND_LAT_CELLS = 8
SECTOR_LON_CELLS = 8
CELLS = BAND_LAT_CELLS * SECTOR_LON_CELLS
BLOCK = 256
F32, BF16 = jnp.float32, jnp.bfloat16


def sums_kernel(rows_ref, cells_ref, count_ref, out_ref):
    slots = rows_ref.shape[0]
    slot = lax.broadcasted_iota(jnp.int32, (1, slots), 1)
    target = jnp.where(slot < count_ref[...], cells_ref[...], -1)
    cell = lax.broadcasted_iota(jnp.int32, (CELLS, slots), 0)
    onehot = jnp.where(cell == target, 1.0, 0.0).astype(BF16)
    sums = jnp.dot(onehot, rows_ref[...], preferred_element_type=F32)
    high = sums.astype(BF16).astype(F32)
    out_ref[...] = jnp.concatenate([high, sums - high], axis=1).astype(BF16)


def taps_kernel(enc_ref, near_ref, far_ref, out_ref):
    features, channels = enc_ref.shape
    width = near_ref.shape[2]
    lane = lax.broadcasted_iota(jnp.int32, (width, BLOCK), 1) // width
    for c in range(channels // BLOCK):
        cols = slice(c * BLOCK, (c + 1) * BLOCK)
        enc = enc_ref[:, cols]
        for t in range(18):
            source = near_ref if t < 9 else far_ref
            tap = source[t % 9 // 3, t % 3, :, cols]
            dense = jnp.concatenate(
                [jnp.where(lane == g, tap, jnp.zeros((), BF16)) for g in range(BLOCK // width)], axis=0
            )
            out_ref[t * features : (t + 1) * features, cols] = jnp.dot(
                enc, dense, preferred_element_type=F32
            ).astype(BF16)
        for t in (18, 19):
            out_ref[t * features : (t + 1) * features, cols] = enc


def mix_kernel(west_ref, own_ref, east_ref, taps_ref, mix_ref, out_ref, left_ref):
    features = taps_ref.shape[0] // 20
    wide = 2 * features
    shape = (SECTOR_LON_CELLS, BAND_LAT_CELLS, wide)
    row = lax.broadcasted_iota(jnp.int32, shape, 1)
    half = lax.broadcasted_iota(jnp.int32, (CELLS, wide), 1) < features
    blocks = [
        [ref[b].astype(F32).reshape(shape) for b in range(3)] for ref in (west_ref, own_ref, east_ref)
    ]
    shifted = []
    for a in range(3):
        before, own, after = blocks[a]
        down = jnp.where(row == 0, pltpu.roll(before, 1, 1), pltpu.roll(own, 1, 1))
        up = jnp.where(
            row == BAND_LAT_CELLS - 1,
            pltpu.roll(after, BAND_LAT_CELLS - 1, 1),
            pltpu.roll(own, BAND_LAT_CELLS - 1, 1),
        )
        shifted.append((down, own, up))
    pieces = []
    for a in range(3):
        for b in range(3):
            mid = shifted[1][b]
            if a == 0:
                mid = jnp.concatenate([shifted[0][b][-1:], mid[:-1]], axis=0)
            elif a == 2:
                mid = jnp.concatenate([mid[1:], shifted[2][b][:1]], axis=0)
            pieces.append(mid.reshape(CELLS, wide))
    for a in range(3):
        for b in range(3):
            pieces.append(blocks[a][b].reshape(CELLS, wide))
    for p in range(9):
        first, second = pieces[2 * p], pieces[2 * p + 1]
        lanes = slice(p * wide, (p + 1) * wide)
        left_ref[:CELLS, lanes] = jnp.where(half, first, pltpu.roll(second, features, 1)).astype(BF16)
        left_ref[CELLS:, lanes] = jnp.where(half, pltpu.roll(first, features, 1), second).astype(BF16)
    lanes = slice(9 * wide, 10 * wide)
    left_ref[:CELLS, lanes] = blocks[1][1].reshape(CELLS, wide).astype(BF16)
    left_ref[CELLS:, lanes] = jnp.zeros((CELLS, wide), BF16)
    channels = mix_ref.shape[0]
    totals, mixed = [], jnp.zeros((CELLS, channels), F32)
    for c in range(channels // BLOCK):
        cols = slice(c * BLOCK, (c + 1) * BLOCK)
        both = jnp.dot(left_ref[...], taps_ref[:, cols], preferred_element_type=F32)
        total = both[:CELLS] + both[CELLS:]
        activ = jax.nn.gelu(total, approximate=True).astype(BF16)
        mixed = mixed + jnp.dot(activ, mix_ref[cols, :], preferred_element_type=F32)
        totals.append(total)
    out_ref[...] = (jnp.concatenate(totals, axis=1) + mixed).astype(BF16)


def shifts(value, axis, wrap):
    count = lax.axis_size(axis)
    up = [(i, (i + 1) % count) for i in range(count if wrap else count - 1)]
    down = [(j, i) for i, j in up]
    return lax.ppermute(value, axis, up), lax.ppermute(value, axis, down)


def on_device(
    obs_rows, obs_cells, obs_counts, enc_weight, near_kernel_weight, far_kernel_weight, mix_weight
):
    slots, features = obs_rows.shape[2:]
    channels = mix_weight.shape[0]
    sums = pl.pallas_call(
        sums_kernel,
        out_shape=jax.ShapeDtypeStruct((CELLS, 2 * features), BF16),
        name="cell_sums",
    )(obs_rows.reshape(slots, features), obs_cells.reshape(1, slots), obs_counts)
    taps = pl.pallas_call(
        taps_kernel,
        out_shape=jax.ShapeDtypeStruct((20 * features, channels), BF16),
        cost_estimate=pl.CostEstimate(
            flops=2 * 72 * 64 * 256 * 256 * 4, bytes_accessed=5_000_000, transcendentals=0
        ),
        compiler_params=pltpu.CompilerParams(vmem_limit_bytes=24 << 20),
        name="encoded_taps",
    )(enc_weight, near_kernel_weight, far_kernel_weight)
    before, after = shifts(sums, "lat", False)
    own = jnp.stack([before, sums, after])
    west, east = shifts(own, "lon", True)
    mixed = pl.pallas_call(
        mix_kernel,
        out_shape=jax.ShapeDtypeStruct((CELLS, channels), BF16),
        scratch_shapes=[pltpu.VMEM((2 * CELLS, 20 * features), BF16)],
        compiler_params=pltpu.CompilerParams(vmem_limit_bytes=24 << 20),
        name="filter_and_mix",
    )(west, own, east, taps, mix_weight)
    return mixed.reshape(SECTOR_LON_CELLS, BAND_LAT_CELLS, channels)


def solution(mesh):
    return jax.shard_map(
        on_device,
        mesh=mesh,
        in_specs=(
            P("lon", "lat", None, None),
            P("lon", "lat", None),
            P("lon", "lat"),
            P(),
            P(),
            P(),
            P(),
        ),
        out_specs=P("lon", "lat", None),
        check_vma=False,
    )
```

```python
import functools

import jax
import jax.numpy as jnp
from jax import lax
from jax.experimental import pallas as pl
from jax.experimental.pallas import tpu as pltpu
from jax.sharding import PartitionSpec as P

BAND_LAT_CELLS = 8
SECTOR_LON_CELLS = 8
CELLS = BAND_LAT_CELLS * SECTOR_LON_CELLS
BLOCK = 256
F32, BF16 = jnp.float32, jnp.bfloat16


def sums_kernel(rows_ref, cells_ref, count_ref, out_ref):
    slots = rows_ref.shape[1]
    slot = lax.broadcasted_iota(jnp.int32, (1, slots), 1)
    target = jnp.where(slot < count_ref[...], cells_ref[...], -1)
    cell = lax.broadcasted_iota(jnp.int32, (CELLS, slots), 0)
    onehot = jnp.where(cell == target, 1.0, 0.0).astype(BF16)
    sums = lax.dot_general(
        onehot, rows_ref[...], (((1,), (1,)), ((), ())), preferred_element_type=F32
    )
    high = sums.astype(BF16).astype(F32)
    out_ref[...] = jnp.concatenate([high, sums - high], axis=1).astype(BF16)


def taps_kernel(enc_ref, near_ref, far_ref, out_ref):
    features, channels = enc_ref.shape
    width = near_ref.shape[2]
    lane = lax.broadcasted_iota(jnp.int32, (width, BLOCK), 1) // width
    for c in range(channels // BLOCK):
        cols = slice(c * BLOCK, (c + 1) * BLOCK)
        enc = enc_ref[:, cols]
        for t in range(18):
            source = near_ref if t < 9 else far_ref
            tap = source[t % 9 // 3, t % 3, :, cols]
            dense = jnp.concatenate(
                [jnp.where(lane == g, tap, jnp.zeros((), BF16)) for g in range(BLOCK // width)], axis=0
            )
            out_ref[t * features : (t + 1) * features, cols] = jnp.dot(
                enc, dense, preferred_element_type=F32
            ).astype(BF16)
        for t in (18, 19):
            out_ref[t * features : (t + 1) * features, cols] = enc


def mix_kernel(sums_ref, taps_ref, mix_ref, out_ref, left_ref):
    features = taps_ref.shape[0] // 20
    wide = 2 * features
    shape = (SECTOR_LON_CELLS, BAND_LAT_CELLS, wide)
    row = lax.broadcasted_iota(jnp.int32, shape, 1)
    half = lax.broadcasted_iota(jnp.int32, (CELLS, wide), 1) < features
    sectors, bands = sums_ref.shape[:2]
    sector, band = lax.axis_index("lon"), lax.axis_index("lat")
    blocks = []
    for a in (-1, 0, 1):
        lon = lax.rem(sector + a + sectors, sectors)
        line = []
        for b in (-1, 0, 1):
            lat = jnp.clip(band + b, 0, bands - 1)
            block = sums_ref[lon, lat].astype(F32)
            if b != 0:
                block = jnp.where(lat == band + b, block, 0.0)
            line.append(block.reshape(shape))
        blocks.append(line)
    shifted = []
    for a in range(3):
        before, own, after = blocks[a]
        down = jnp.where(row == 0, pltpu.roll(before, 1, 1), pltpu.roll(own, 1, 1))
        up = jnp.where(
            row == BAND_LAT_CELLS - 1,
            pltpu.roll(after, BAND_LAT_CELLS - 1, 1),
            pltpu.roll(own, BAND_LAT_CELLS - 1, 1),
        )
        shifted.append((down, own, up))
    pieces = []
    for a in range(3):
        for b in range(3):
            mid = shifted[1][b]
            if a == 0:
                mid = jnp.concatenate([shifted[0][b][-1:], mid[:-1]], axis=0)
            elif a == 2:
                mid = jnp.concatenate([mid[1:], shifted[2][b][:1]], axis=0)
            pieces.append(mid.reshape(CELLS, wide))
    for a in range(3):
        for b in range(3):
            pieces.append(blocks[a][b].reshape(CELLS, wide))
    for p in range(9):
        first, second = pieces[2 * p], pieces[2 * p + 1]
        lanes = slice(p * wide, (p + 1) * wide)
        left_ref[:CELLS, lanes] = jnp.where(half, first, pltpu.roll(second, features, 1)).astype(BF16)
        left_ref[CELLS:, lanes] = jnp.where(half, pltpu.roll(first, features, 1), second).astype(BF16)
    lanes = slice(9 * wide, 10 * wide)
    left_ref[:CELLS, lanes] = blocks[1][1].reshape(CELLS, wide).astype(BF16)
    left_ref[CELLS:, lanes] = jnp.zeros((CELLS, wide), BF16)
    channels = mix_ref.shape[0]
    totals, mixed = [], jnp.zeros((CELLS, channels), F32)
    for c in range(channels // BLOCK):
        cols = slice(c * BLOCK, (c + 1) * BLOCK)
        both = jnp.dot(left_ref[...], taps_ref[:, cols], preferred_element_type=F32)
        total = both[:CELLS] + both[CELLS:]
        activ = jax.nn.gelu(total, approximate=True).astype(BF16)
        mixed = mixed + jnp.dot(activ, mix_ref[cols, :], preferred_element_type=F32)
        totals.append(total)
    out_ref[...] = (jnp.concatenate(totals, axis=1) + mixed).astype(BF16)


def on_device(
    obs_rows, obs_cells, obs_counts, enc_weight, near_kernel_weight, far_kernel_weight, mix_weight
):
    slots, features = obs_rows.shape[2:]
    channels = mix_weight.shape[0]
    sums = pl.pallas_call(
        sums_kernel,
        out_shape=jax.ShapeDtypeStruct((CELLS, 2 * features), BF16),
        compiler_params=pltpu.CompilerParams(vmem_limit_bytes=8 << 20),
        name="cell_sums",
    )(obs_rows.reshape(slots, features).T, obs_cells.reshape(1, slots), obs_counts)
    taps = pl.pallas_call(
        taps_kernel,
        out_shape=jax.ShapeDtypeStruct((20 * features, channels), BF16),
        cost_estimate=pl.CostEstimate(
            flops=2 * 72 * 64 * 256 * 256 * 4, bytes_accessed=5_000_000, transcendentals=0
        ),
        compiler_params=pltpu.CompilerParams(vmem_limit_bytes=24 << 20),
        name="encoded_taps",
    )(enc_weight, near_kernel_weight, far_kernel_weight)
    gathered = lax.all_gather(sums, ("lon", "lat")).reshape(
        lax.axis_size("lon"), lax.axis_size("lat"), CELLS, 2 * features
    )
    mixed = pl.pallas_call(
        mix_kernel,
        out_shape=jax.ShapeDtypeStruct((CELLS, channels), BF16),
        scratch_shapes=[pltpu.VMEM((2 * CELLS, 20 * features), BF16)],
        compiler_params=pltpu.CompilerParams(vmem_limit_bytes=24 << 20),
        name="filter_and_mix",
    )(gathered, taps, mix_weight)
    return mixed.reshape(SECTOR_LON_CELLS, BAND_LAT_CELLS, channels)


def solution(mesh):
    return jax.shard_map(
        on_device,
        mesh=mesh,
        in_specs=(
            P("lon", "lat", None, None),
            P("lon", "lat", None),
            P("lon", "lat"),
            P(),
            P(),
            P(),
            P(),
        ),
        out_specs=P("lon", "lat", None),
        check_vma=False,
    )
```

```python
import functools

import jax
import jax.numpy as jnp
from jax import lax
from jax.experimental import pallas as pl
from jax.experimental.pallas import tpu as pltpu
from jax.sharding import PartitionSpec as P

BAND_LAT_CELLS = 8
SECTOR_LON_CELLS = 8
CELLS = BAND_LAT_CELLS * SECTOR_LON_CELLS
BLOCK = 256
F32, BF16 = jnp.float32, jnp.bfloat16


def sums_kernel(rows_hbm, cells_hbm, count_ref, out_ref, rows_ref, cells_ref, sems):
    copies = [
        pltpu.make_async_copy(cells_hbm, cells_ref, sems.at[0]),
        pltpu.make_async_copy(rows_hbm, rows_ref, sems.at[1]),
    ]
    for copy in copies:
        copy.start()
    slots = rows_ref.shape[1]
    slot = lax.broadcasted_iota(jnp.int32, (1, slots), 1)
    cell = lax.broadcasted_iota(jnp.int32, (CELLS, slots), 0)
    copies[0].wait()
    target = jnp.where(slot < count_ref[0, 0], cells_ref[...], -1)
    onehot = jnp.where(cell == target, 1.0, 0.0).astype(BF16)
    copies[1].wait()
    sums = lax.dot_general(
        onehot, rows_ref[...], (((1,), (1,)), ((), ())), preferred_element_type=F32
    )
    high = sums.astype(BF16).astype(F32)
    out_ref[...] = jnp.concatenate([high, sums - high], axis=1).astype(BF16)


def taps_kernel(enc_hbm, near_hbm, far_hbm, out_ref, enc_ref, near_ref, far_ref, sems):
    features, channels = enc_ref.shape
    width = near_ref.shape[2]
    enc_copy = pltpu.make_async_copy(enc_hbm, enc_ref, sems.at[6])
    enc_copy.start()
    copies = []
    for hbm, ref in ((near_hbm, near_ref), (far_hbm, far_ref)):
        for a in range(3):
            copies.append(pltpu.make_async_copy(hbm.at[a], ref.at[a], sems.at[len(copies)]))
            copies[-1].start()
    lane = lax.broadcasted_iota(jnp.int32, (width, BLOCK), 1) // width
    enc_copy.wait()
    for t in range(18):
        ref = near_ref if t < 9 else far_ref
        if t % 3 == 0:
            copies[t // 3].wait()
        for c in range(channels // BLOCK):
            cols = slice(c * BLOCK, (c + 1) * BLOCK)
            tap = ref[t % 9 // 3, t % 3, :, cols]
            dense = jnp.concatenate(
                [jnp.where(lane == g, tap, jnp.zeros((), BF16)) for g in range(BLOCK // width)], axis=0
            )
            out_ref[t * features : (t + 1) * features, cols] = jnp.dot(
                enc_ref[:, cols], dense, preferred_element_type=F32
            ).astype(BF16)
    for t in (18, 19):
        out_ref[t * features : (t + 1) * features] = enc_ref[...]


def mix_kernel(west_ref, own_ref, east_ref, taps_ref, mix_ref, out_ref, left_ref):
    features = taps_ref.shape[0] // 20
    wide = 2 * features
    shape = (SECTOR_LON_CELLS, BAND_LAT_CELLS, wide)
    row = lax.broadcasted_iota(jnp.int32, shape, 1)
    half = lax.broadcasted_iota(jnp.int32, (CELLS, wide), 1) < features
    blocks = [
        [ref[b].astype(F32).reshape(shape) for b in range(3)] for ref in (west_ref, own_ref, east_ref)
    ]
    shifted = []
    for a in range(3):
        before, own, after = blocks[a]
        down = jnp.where(row == 0, pltpu.roll(before, 1, 1), pltpu.roll(own, 1, 1))
        up = jnp.where(
            row == BAND_LAT_CELLS - 1,
            pltpu.roll(after, BAND_LAT_CELLS - 1, 1),
            pltpu.roll(own, BAND_LAT_CELLS - 1, 1),
        )
        shifted.append((down, own, up))
    pieces = []
    for a in range(3):
        for b in range(3):
            mid = shifted[1][b]
            if a == 0:
                mid = jnp.concatenate([shifted[0][b][-1:], mid[:-1]], axis=0)
            elif a == 2:
                mid = jnp.concatenate([mid[1:], shifted[2][b][:1]], axis=0)
            pieces.append(mid.reshape(CELLS, wide))
    for a in range(3):
        for b in range(3):
            pieces.append(blocks[a][b].reshape(CELLS, wide))
    for p in range(9):
        first, second = pieces[2 * p], pieces[2 * p + 1]
        lanes = slice(p * wide, (p + 1) * wide)
        left_ref[:CELLS, lanes] = jnp.where(half, first, pltpu.roll(second, features, 1)).astype(BF16)
        left_ref[CELLS:, lanes] = jnp.where(half, pltpu.roll(first, features, 1), second).astype(BF16)
    lanes = slice(9 * wide, 10 * wide)
    left_ref[:CELLS, lanes] = blocks[1][1].reshape(CELLS, wide).astype(BF16)
    left_ref[CELLS:, lanes] = jnp.zeros((CELLS, wide), BF16)
    channels = mix_ref.shape[0]
    totals, mixed = [], jnp.zeros((CELLS, channels), F32)
    for c in range(channels // BLOCK):
        cols = slice(c * BLOCK, (c + 1) * BLOCK)
        both = jnp.dot(left_ref[...], taps_ref[:, cols], preferred_element_type=F32)
        total = both[:CELLS] + both[CELLS:]
        activ = jax.nn.gelu(total, approximate=True).astype(BF16)
        mixed = mixed + jnp.dot(activ, mix_ref[cols, :], preferred_element_type=F32)
        totals.append(total)
    out_ref[...] = (jnp.concatenate(totals, axis=1) + mixed).astype(BF16)


def hbm(value):
    return pltpu.with_memory_space_constraint(value, pltpu.HBM)


def shifts(value, axis, wrap):
    count = lax.axis_size(axis)
    up = [(i, (i + 1) % count) for i in range(count if wrap else count - 1)]
    down = [(j, i) for i, j in up]
    return lax.ppermute(value, axis, up), lax.ppermute(value, axis, down)


def on_device(
    obs_rows, obs_cells, obs_counts, enc_weight, near_kernel_weight, far_kernel_weight, mix_weight
):
    slots, features = obs_rows.shape[2:]
    channels = mix_weight.shape[0]
    sums = pl.pallas_call(
        sums_kernel,
        out_shape=pltpu.VMEM((CELLS, 2 * features), BF16),
        in_specs=[pl.BlockSpec(memory_space=pltpu.HBM)] * 2 + [pl.BlockSpec(memory_space=pltpu.SMEM)],
        scratch_shapes=[
            pltpu.VMEM((features, slots), BF16),
            pltpu.VMEM((1, slots), jnp.int32),
            pltpu.SemaphoreType.DMA((2,)),
        ],
        compiler_params=pltpu.CompilerParams(vmem_limit_bytes=8 << 20),
        name="cell_sums",
    )(hbm(obs_rows.reshape(slots, features).T), hbm(obs_cells.reshape(1, slots)), obs_counts)
    taps = pl.pallas_call(
        taps_kernel,
        out_shape=pltpu.VMEM((20 * features, channels), BF16),
        in_specs=[pl.BlockSpec(memory_space=pltpu.HBM)] * 3,
        scratch_shapes=[
            pltpu.VMEM(enc_weight.shape, BF16),
            pltpu.VMEM(near_kernel_weight.shape, BF16),
            pltpu.VMEM(far_kernel_weight.shape, BF16),
            pltpu.SemaphoreType.DMA((7,)),
        ],
        cost_estimate=pl.CostEstimate(
            flops=2 * 72 * 64 * 256 * 256 * 4, bytes_accessed=5_000_000, transcendentals=0
        ),
        compiler_params=pltpu.CompilerParams(vmem_limit_bytes=24 << 20),
        name="encoded_taps",
    )(hbm(enc_weight), hbm(near_kernel_weight), hbm(far_kernel_weight))
    before, after = shifts(sums, "lat", False)
    own = jnp.stack([before, sums, after])
    west, east = shifts(own, "lon", True)
    mixed = pl.pallas_call(
        mix_kernel,
        out_shape=jax.ShapeDtypeStruct((CELLS, channels), BF16),
        scratch_shapes=[pltpu.VMEM((2 * CELLS, 20 * features), BF16)],
        compiler_params=pltpu.CompilerParams(vmem_limit_bytes=24 << 20),
        name="filter_and_mix",
    )(west, own, east, taps, mix_weight)
    return mixed.reshape(SECTOR_LON_CELLS, BAND_LAT_CELLS, channels)


def solution(mesh):
    return jax.shard_map(
        on_device,
        mesh=mesh,
        in_specs=(
            P("lon", "lat", None, None),
            P("lon", "lat", None),
            P("lon", "lat"),
            P(),
            P(),
            P(),
            P(),
        ),
        out_specs=P("lon", "lat", None),
        check_vma=False,
    )
```

```python
import functools

import jax
import jax.numpy as jnp
from jax import lax
from jax.experimental import pallas as pl
from jax.experimental.pallas import tpu as pltpu
from jax.sharding import PartitionSpec as P

BAND_LAT_CELLS = 8
SECTOR_LON_CELLS = 8
CELLS = BAND_LAT_CELLS * SECTOR_LON_CELLS
BLOCK = 256
F32, BF16 = jnp.float32, jnp.bfloat16


def sums_kernel(rows_hbm, cells_hbm, count_ref, out_ref, rows_ref, cells_ref, sems):
    copies = [
        pltpu.make_async_copy(cells_hbm, cells_ref, sems.at[0]),
        pltpu.make_async_copy(rows_hbm, rows_ref, sems.at[1]),
    ]
    for copy in copies:
        copy.start()
    slots = rows_ref.shape[1]
    slot = lax.broadcasted_iota(jnp.int32, (1, slots), 1)
    cell = lax.broadcasted_iota(jnp.int32, (CELLS, slots), 0)
    copies[0].wait()
    target = jnp.where(slot < count_ref[0, 0], cells_ref[...], -1)
    onehot = jnp.where(cell == target, 1.0, 0.0).astype(BF16)
    copies[1].wait()
    sums = lax.dot_general(
        onehot, rows_ref[...], (((1,), (1,)), ((), ())), preferred_element_type=F32
    )
    high = sums.astype(BF16).astype(F32)
    out_ref[...] = jnp.concatenate([high, sums - high], axis=1).astype(BF16)


def taps_kernel(enc_hbm, near_hbm, far_hbm, out_ref, enc_ref, near_ref, far_ref, sems):
    features, channels = enc_ref.shape
    width = near_ref.shape[2]
    enc_copy = pltpu.make_async_copy(enc_hbm, enc_ref, sems.at[18])
    enc_copy.start()
    copies = []
    for hbm, ref in ((near_hbm, near_ref), (far_hbm, far_ref)):
        for tap in range(9):
            at = (tap // 3, tap % 3)
            copies.append(pltpu.make_async_copy(hbm.at[at], ref.at[at], sems.at[len(copies)]))
            copies[-1].start()
    lane = lax.broadcasted_iota(jnp.int32, (width, BLOCK), 1) // width
    enc_copy.wait()
    for t in range(18):
        ref = near_ref if t < 9 else far_ref
        copies[t].wait()
        for c in range(channels // BLOCK):
            cols = slice(c * BLOCK, (c + 1) * BLOCK)
            tap = ref[t % 9 // 3, t % 3, :, cols]
            dense = jnp.concatenate(
                [jnp.where(lane == g, tap, jnp.zeros((), BF16)) for g in range(BLOCK // width)], axis=0
            )
            out_ref[t * features : (t + 1) * features, cols] = jnp.dot(
                enc_ref[:, cols], dense, preferred_element_type=F32
            ).astype(BF16)
    for t in (18, 19):
        out_ref[t * features : (t + 1) * features] = enc_ref[...]


def mix_kernel(*refs):
    sums_refs = refs[:9]
    taps_ref, mix_ref, out_ref, left_ref = refs[9:]
    features = taps_ref.shape[0] // 20
    wide = 2 * features
    shape = (SECTOR_LON_CELLS, BAND_LAT_CELLS, wide)
    row = lax.broadcasted_iota(jnp.int32, shape, 1)
    half = lax.broadcasted_iota(jnp.int32, (CELLS, wide), 1) < features
    band = lax.axis_index("lat")
    inside = (band > 0, None, band < lax.axis_size("lat") - 1)
    blocks = []
    for a in range(3):
        line = []
        for b in range(3):
            block = sums_refs[8 - 3 * a - b][...].astype(F32)
            if b != 1:
                block = jnp.where(inside[b], block, 0.0)
            line.append(block.reshape(shape))
        blocks.append(line)
    shifted = []
    for a in range(3):
        before, own, after = blocks[a]
        down = jnp.where(row == 0, pltpu.roll(before, 1, 1), pltpu.roll(own, 1, 1))
        up = jnp.where(
            row == BAND_LAT_CELLS - 1,
            pltpu.roll(after, BAND_LAT_CELLS - 1, 1),
            pltpu.roll(own, BAND_LAT_CELLS - 1, 1),
        )
        shifted.append((down, own, up))
    pieces = []
    for a in range(3):
        for b in range(3):
            mid = shifted[1][b]
            if a == 0:
                mid = jnp.concatenate([shifted[0][b][-1:], mid[:-1]], axis=0)
            elif a == 2:
                mid = jnp.concatenate([mid[1:], shifted[2][b][:1]], axis=0)
            pieces.append(mid.reshape(CELLS, wide))
    for a in range(3):
        for b in range(3):
            pieces.append(blocks[a][b].reshape(CELLS, wide))
    for p in range(9):
        first, second = pieces[2 * p], pieces[2 * p + 1]
        lanes = slice(p * wide, (p + 1) * wide)
        left_ref[:CELLS, lanes] = jnp.where(half, first, pltpu.roll(second, features, 1)).astype(BF16)
        left_ref[CELLS:, lanes] = jnp.where(half, pltpu.roll(first, features, 1), second).astype(BF16)
    lanes = slice(9 * wide, 10 * wide)
    left_ref[:CELLS, lanes] = blocks[1][1].reshape(CELLS, wide).astype(BF16)
    left_ref[CELLS:, lanes] = jnp.zeros((CELLS, wide), BF16)
    channels = mix_ref.shape[0]
    totals, mixed = [], jnp.zeros((CELLS, channels), F32)
    for c in range(channels // BLOCK):
        cols = slice(c * BLOCK, (c + 1) * BLOCK)
        both = jnp.dot(left_ref[...], taps_ref[:, cols], preferred_element_type=F32)
        total = both[:CELLS] + both[CELLS:]
        activ = jax.nn.gelu(total, approximate=True).astype(BF16)
        mixed = mixed + jnp.dot(activ, mix_ref[cols, :], preferred_element_type=F32)
        totals.append(total)
    out_ref[...] = (jnp.concatenate(totals, axis=1) + mixed).astype(BF16)


def hbm(value):
    return pltpu.with_memory_space_constraint(value, pltpu.HBM)


def from_neighbour(value, lon_step, lat_step):
    sectors, bands = lax.axis_size("lon"), lax.axis_size("lat")
    pairs = [
        ((lon + lon_step) % sectors * bands + (lat + lat_step) % bands, lon * bands + lat)
        for lon in range(sectors)
        for lat in range(bands)
    ]
    return lax.ppermute(value, ("lon", "lat"), pairs)


def on_device(
    obs_rows, obs_cells, obs_counts, enc_weight, near_kernel_weight, far_kernel_weight, mix_weight
):
    slots, features = obs_rows.shape[2:]
    channels = mix_weight.shape[0]
    sums = pl.pallas_call(
        sums_kernel,
        out_shape=pltpu.VMEM((CELLS, 2 * features), BF16),
        in_specs=[pl.BlockSpec(memory_space=pltpu.HBM)] * 2 + [pl.BlockSpec(memory_space=pltpu.SMEM)],
        scratch_shapes=[
            pltpu.VMEM((features, slots), BF16),
            pltpu.VMEM((1, slots), jnp.int32),
            pltpu.SemaphoreType.DMA((2,)),
        ],
        compiler_params=pltpu.CompilerParams(vmem_limit_bytes=8 << 20),
        name="cell_sums",
    )(hbm(obs_rows.reshape(slots, features).T), hbm(obs_cells.reshape(1, slots)), obs_counts)
    taps = pl.pallas_call(
        taps_kernel,
        out_shape=pltpu.VMEM((20 * features, channels), BF16),
        in_specs=[pl.BlockSpec(memory_space=pltpu.HBM)] * 3,
        scratch_shapes=[
            pltpu.VMEM(enc_weight.shape, BF16),
            pltpu.VMEM(near_kernel_weight.shape, BF16),
            pltpu.VMEM(far_kernel_weight.shape, BF16),
            pltpu.SemaphoreType.DMA((19,)),
        ],
        cost_estimate=pl.CostEstimate(
            flops=2 * 72 * 64 * 256 * 256 * 4, bytes_accessed=5_000_000, transcendentals=0
        ),
        compiler_params=pltpu.CompilerParams(vmem_limit_bytes=24 << 20),
        name="encoded_taps",
    )(hbm(enc_weight), hbm(near_kernel_weight), hbm(far_kernel_weight))
    blocks = {(0, 0): sums}
    for lon_step in (1, 0, -1):
        for lat_step in (1, 0, -1):
            if lon_step or lat_step:
                blocks[lon_step, lat_step] = from_neighbour(sums, lon_step, lat_step)
    mixed = pl.pallas_call(
        mix_kernel,
        out_shape=jax.ShapeDtypeStruct((CELLS, channels), BF16),
        scratch_shapes=[pltpu.VMEM((2 * CELLS, 20 * features), BF16)],
        compiler_params=pltpu.CompilerParams(vmem_limit_bytes=24 << 20),
        name="filter_and_mix",
    )(*[blocks[a, b] for a in (1, 0, -1) for b in (1, 0, -1)], taps, mix_weight)
    return mixed.reshape(SECTOR_LON_CELLS, BAND_LAT_CELLS, channels)


def solution(mesh):
    return jax.shard_map(
        on_device,
        mesh=mesh,
        in_specs=(
            P("lon", "lat", None, None),
            P("lon", "lat", None),
            P("lon", "lat"),
            P(),
            P(),
            P(),
            P(),
        ),
        out_specs=P("lon", "lat", None),
        check_vma=False,
    )
```

```python
import functools

import jax
import jax.numpy as jnp
from jax import lax
from jax.experimental import pallas as pl
from jax.experimental.pallas import tpu as pltpu
from jax.sharding import PartitionSpec as P

BAND_LAT_CELLS = 8
SECTOR_LON_CELLS = 8
CELLS = BAND_LAT_CELLS * SECTOR_LON_CELLS
BLOCK = 256
F32, BF16 = jnp.float32, jnp.bfloat16


def early():
    return lax.axis_index("lon") < lax.axis_size("lon") // 2


def weight_copies(sources, scratch):
    sems = scratch[-1]
    return [pltpu.make_async_copy(src, dst, sems.at[i]) for i, (src, dst) in enumerate(zip(sources, scratch))]


def encode_taps(enc_ref, near_ref, far_ref, out_ref):
    features, channels = enc_ref.shape
    width = near_ref.shape[2]
    lane = lax.broadcasted_iota(jnp.int32, (width, BLOCK), 1) // width
    for t in range(18):
        ref = near_ref if t < 9 else far_ref
        for c in range(channels // BLOCK):
            cols = slice(c * BLOCK, (c + 1) * BLOCK)
            tap = ref[t % 9 // 3, t % 3, :, cols]
            dense = jnp.concatenate(
                [jnp.where(lane == g, tap, jnp.zeros((), BF16)) for g in range(BLOCK // width)], axis=0
            )
            out_ref[t * features : (t + 1) * features, cols] = jnp.dot(
                enc_ref[:, cols], dense, preferred_element_type=F32
            ).astype(BF16)
    for t in (18, 19):
        out_ref[t * features : (t + 1) * features] = enc_ref[...]


def sums_kernel(rows_hbm, cells_hbm, count_ref, *refs):
    weights, (out_ref, taps_ref), (rows_ref, cells_ref, sems), scratch = refs[:3], refs[3:5], refs[5:8], refs[8:]
    copies = [
        pltpu.make_async_copy(cells_hbm, cells_ref, sems.at[0]),
        pltpu.make_async_copy(rows_hbm, rows_ref, sems.at[1]),
    ]
    for copy in copies:
        copy.start()

    @pl.when(early())
    def _():
        for copy in weight_copies(weights, scratch):
            copy.start()

    slots = rows_ref.shape[1]
    slot = lax.broadcasted_iota(jnp.int32, (1, slots), 1)
    cell = lax.broadcasted_iota(jnp.int32, (CELLS, slots), 0)
    copies[0].wait()
    target = jnp.where(slot < count_ref[0, 0], cells_ref[...], -1)
    onehot = jnp.where(cell == target, 1.0, 0.0).astype(BF16)
    copies[1].wait()
    sums = lax.dot_general(
        onehot, rows_ref[...], (((1,), (1,)), ((), ())), preferred_element_type=F32
    )
    high = sums.astype(BF16).astype(F32)
    out_ref[...] = jnp.concatenate([high, sums - high], axis=1).astype(BF16)

    @pl.when(early())
    def _():
        for copy in weight_copies(weights, scratch):
            copy.wait()
        encode_taps(*scratch[:3], taps_ref)


def taps_kernel(enc_hbm, near_hbm, far_hbm, held_ref, out_ref, *scratch):
    del held_ref

    @pl.when(jnp.logical_not(early()))
    def _():
        copies = weight_copies((enc_hbm, near_hbm, far_hbm), scratch)
        for copy in copies:
            copy.start()
        for copy in copies:
            copy.wait()
        encode_taps(*scratch[:3], out_ref)


def mix_kernel(own_ref, near_lat_ref, other_lat_ref, taps_ref, mix_ref, out_ref, left_ref):
    features = taps_ref.shape[0] // 20
    wide = 2 * features
    shape = (SECTOR_LON_CELLS, BAND_LAT_CELLS, wide)
    row = lax.broadcasted_iota(jnp.int32, shape, 1)
    half = lax.broadcasted_iota(jnp.int32, (CELLS, wide), 1) < features
    sector, band = lax.axis_index("lon"), lax.axis_index("lat")
    even_lon, even_lat = lax.rem(sector, 2) == 0, lax.rem(band, 2) == 0
    blocks = []
    for slot in (jnp.where(even_lon, 1, 2), 0, jnp.where(even_lon, 2, 1)):
        one, two = (ref[slot].astype(F32) for ref in (near_lat_ref, other_lat_ref))
        before = jnp.where(band > 0, jnp.where(even_lat, two, one), 0.0)
        after = jnp.where(band < lax.axis_size("lat") - 1, jnp.where(even_lat, one, two), 0.0)
        blocks.append([block.reshape(shape) for block in (before, own_ref[slot].astype(F32), after)])
    shifted = []
    for a in range(3):
        before, own, after = blocks[a]
        down = jnp.where(row == 0, pltpu.roll(before, 1, 1), pltpu.roll(own, 1, 1))
        up = jnp.where(
            row == BAND_LAT_CELLS - 1,
            pltpu.roll(after, BAND_LAT_CELLS - 1, 1),
            pltpu.roll(own, BAND_LAT_CELLS - 1, 1),
        )
        shifted.append((down, own, up))
    pieces = []
    for a in range(3):
        for b in range(3):
            mid = shifted[1][b]
            if a == 0:
                mid = jnp.concatenate([shifted[0][b][-1:], mid[:-1]], axis=0)
            elif a == 2:
                mid = jnp.concatenate([mid[1:], shifted[2][b][:1]], axis=0)
            pieces.append(mid.reshape(CELLS, wide))
    for a in range(3):
        for b in range(3):
            pieces.append(blocks[a][b].reshape(CELLS, wide))
    for p in range(9):
        first, second = pieces[2 * p], pieces[2 * p + 1]
        lanes = slice(p * wide, (p + 1) * wide)
        left_ref[:CELLS, lanes] = jnp.where(half, first, pltpu.roll(second, features, 1)).astype(BF16)
        left_ref[CELLS:, lanes] = jnp.where(half, pltpu.roll(first, features, 1), second).astype(BF16)
    lanes = slice(9 * wide, 10 * wide)
    left_ref[:CELLS, lanes] = blocks[1][1].reshape(CELLS, wide).astype(BF16)
    left_ref[CELLS:, lanes] = jnp.zeros((CELLS, wide), BF16)
    channels = mix_ref.shape[0]
    totals, mixed = [], jnp.zeros((CELLS, channels), F32)
    for c in range(channels // BLOCK):
        cols = slice(c * BLOCK, (c + 1) * BLOCK)
        both = jnp.dot(left_ref[...], taps_ref[:, cols], preferred_element_type=F32)
        total = both[:CELLS] + both[CELLS:]
        activ = jax.nn.gelu(total, approximate=True).astype(BF16)
        mixed = mixed + jnp.dot(activ, mix_ref[cols, :], preferred_element_type=F32)
        totals.append(total)
    out_ref[...] = (jnp.concatenate(totals, axis=1) + mixed).astype(BF16)


def hbm(value):
    return pltpu.with_memory_space_constraint(value, pltpu.HBM)


def swapped(value, axis, first):
    count = lax.axis_size(axis)
    pairs = [(i, (i + 1 if i % 2 == first else i - 1) % count) for i in range(count)]
    return lax.ppermute(value, axis, pairs)


def on_device(
    obs_rows, obs_cells, obs_counts, enc_weight, near_kernel_weight, far_kernel_weight, mix_weight
):
    slots, features = obs_rows.shape[2:]
    channels = mix_weight.shape[0]
    weights = [hbm(weight) for weight in (enc_weight, near_kernel_weight, far_kernel_weight)]
    weight_scratch = [pltpu.VMEM(weight.shape, BF16) for weight in weights] + [pltpu.SemaphoreType.DMA((3,))]
    params = pltpu.CompilerParams(vmem_limit_bytes=24 << 20)
    in_hbm, in_vmem = pl.BlockSpec(memory_space=pltpu.HBM), pl.BlockSpec(memory_space=pltpu.VMEM)
    sums, taps = pl.pallas_call(
        sums_kernel,
        out_shape=(pltpu.VMEM((CELLS, 2 * features), BF16), pltpu.VMEM((20 * features, channels), BF16)),
        in_specs=[in_hbm] * 2 + [pl.BlockSpec(memory_space=pltpu.SMEM)] + [in_hbm] * 3,
        scratch_shapes=[
            pltpu.VMEM((features, slots), BF16),
            pltpu.VMEM((1, slots), jnp.int32),
            pltpu.SemaphoreType.DMA((2,)),
        ]
        + weight_scratch,
        compiler_params=params,
        name="cell_sums",
    )(hbm(obs_rows.reshape(slots, features).T), hbm(obs_cells.reshape(1, slots)), obs_counts, *weights)
    taps = pl.pallas_call(
        taps_kernel,
        out_shape=pltpu.VMEM((20 * features, channels), BF16),
        in_specs=[in_hbm] * 3 + [in_vmem],
        scratch_shapes=weight_scratch,
        input_output_aliases={3: 0},
        cost_estimate=pl.CostEstimate(
            flops=2 * 72 * 64 * 256 * 256 * 4, bytes_accessed=5_000_000, transcendentals=0
        ),
        compiler_params=params,
        name="encoded_taps",
    )(*weights, taps)
    own = jnp.stack([sums, swapped(sums, "lon", 1), swapped(sums, "lon", 0)])
    own, taps = lax.optimization_barrier((own, taps))
    near_lat, other_lat = swapped(own, "lat", 0), swapped(own, "lat", 1)
    mixed = pl.pallas_call(
        mix_kernel,
        out_shape=jax.ShapeDtypeStruct((CELLS, channels), BF16),
        scratch_shapes=[pltpu.VMEM((2 * CELLS, 20 * features), BF16)],
        compiler_params=pltpu.CompilerParams(vmem_limit_bytes=24 << 20),
        name="filter_and_mix",
    )(own, near_lat, other_lat, taps, mix_weight)
    return mixed.reshape(SECTOR_LON_CELLS, BAND_LAT_CELLS, channels)


def solution(mesh):
    return jax.shard_map(
        on_device,
        mesh=mesh,
        in_specs=(
            P("lon", "lat", None, None),
            P("lon", "lat", None),
            P("lon", "lat"),
            P(),
            P(),
            P(),
            P(),
        ),
        out_specs=P("lon", "lat", None),
        check_vma=False,
    )
```

```python
import functools

import jax
import jax.numpy as jnp
from jax import lax
from jax.experimental import pallas as pl
from jax.experimental.pallas import tpu as pltpu
from jax.sharding import PartitionSpec as P

BAND_LAT_CELLS = 8
SECTOR_LON_CELLS = 8
CELLS = BAND_LAT_CELLS * SECTOR_LON_CELLS
BLOCK = 256
F32, BF16 = jnp.float32, jnp.bfloat16


def early():
    return lax.axis_index("lon") < lax.axis_size("lon") // 2


def weight_copies(sources, scratch):
    sems = scratch[-1]
    return [pltpu.make_async_copy(src, dst, sems.at[i]) for i, (src, dst) in enumerate(zip(sources, scratch))]


def encode_taps(copies, enc_ref, near_ref, far_ref, out_ref):
    copies = copies[:2], copies[2:]
    features, channels = enc_ref.shape
    width = near_ref.shape[2]
    lane = lax.broadcasted_iota(jnp.int32, (width, BLOCK), 1) // width
    for t in range(18):
        ref = near_ref if t < 9 else far_ref
        if t % 9 == 0:
            for copy in copies[t // 9]:
                copy.wait()
        for c in range(channels // BLOCK):
            cols = slice(c * BLOCK, (c + 1) * BLOCK)
            tap = ref[t % 9 // 3, t % 3, :, cols]
            dense = jnp.concatenate(
                [jnp.where(lane == g, tap, jnp.zeros((), BF16)) for g in range(BLOCK // width)], axis=0
            )
            out_ref[t * features : (t + 1) * features, cols] = jnp.dot(
                enc_ref[:, cols], dense, preferred_element_type=F32
            ).astype(BF16)
    for t in (18, 19):
        out_ref[t * features : (t + 1) * features] = enc_ref[...]


def sums_kernel(rows_hbm, cells_hbm, count_ref, *refs):
    weights, (sent_ref, own_ref, taps_ref), (rows_ref, cells_ref, sems) = refs[:3], refs[3:6], refs[6:9]
    scratch = refs[9:]
    copies = [
        pltpu.make_async_copy(cells_hbm, cells_ref, sems.at[0]),
        pltpu.make_async_copy(rows_hbm, rows_ref, sems.at[1]),
    ]
    for copy in copies:
        copy.start()

    @pl.when(early())
    def _():
        for copy in weight_copies(weights, scratch):
            copy.start()

    slots = rows_ref.shape[1]
    slot = lax.broadcasted_iota(jnp.int32, (1, slots), 1)
    cell = lax.broadcasted_iota(jnp.int32, (CELLS, slots), 0)
    copies[0].wait()
    target = jnp.where(slot < count_ref[0, 0], cells_ref[...], -1)
    onehot = jnp.where(cell == target, 1.0, 0.0).astype(BF16)
    copies[1].wait()
    sums = lax.dot_general(
        onehot, rows_ref[...], (((1,), (1,)), ((), ())), preferred_element_type=F32
    )
    high = sums.astype(BF16).astype(F32)
    sent_ref[...] = jnp.concatenate([high[: CELLS // 2], high[CELLS // 2 :]], axis=1).astype(BF16)
    own_ref[...] = jnp.concatenate([high, sums - high], axis=1).astype(BF16)

    @pl.when(early())
    def _():
        encode_taps(weight_copies(weights, scratch), *scratch[:3], taps_ref)


def taps_kernel(enc_hbm, near_hbm, far_hbm, held_ref, out_ref, *scratch):
    del held_ref

    @pl.when(jnp.logical_not(early()))
    def _():
        copies = weight_copies((enc_hbm, near_hbm, far_hbm), scratch)
        for copy in copies:
            copy.start()
        encode_taps(copies, *scratch[:3], out_ref)


def mix_kernel(own_ref, line_ref, near_lat_ref, other_lat_ref, taps_ref, mix_ref, out_ref, left_ref):
    features = taps_ref.shape[0] // 20
    wide = 2 * features
    packed = (SECTOR_LON_CELLS // 2, BAND_LAT_CELLS, wide)
    shape = (SECTOR_LON_CELLS, BAND_LAT_CELLS, wide)
    row = lax.broadcasted_iota(jnp.int32, shape, 1)
    half = lax.broadcasted_iota(jnp.int32, packed, 2) < features
    low_half = lax.broadcasted_iota(jnp.int32, (CELLS, wide), 1) < features
    sector, band = lax.axis_index("lon"), lax.axis_index("lat")
    even_lon, even_lat = lax.rem(sector, 2) == 0, lax.rem(band, 2) == 0

    def doubled(block):
        turned = pltpu.roll(block, features, 1).reshape(packed)
        block = block.reshape(packed)
        return jnp.concatenate([jnp.where(half, block, turned), jnp.where(half, turned, block)], axis=0)

    blocks = []
    for slot in (jnp.where(even_lon, 2, 1), 0, jnp.where(even_lon, 1, 2)):
        one, two = (ref[slot].astype(F32) for ref in (near_lat_ref, other_lat_ref))
        before = jnp.where(band > 0, jnp.where(even_lat, two, one), 0.0)
        after = jnp.where(band < lax.axis_size("lat") - 1, jnp.where(even_lat, one, two), 0.0)
        blocks.append([doubled(block) for block in (before, line_ref[slot].astype(F32), after)])
    shifted = []
    for a in range(3):
        before, own, after = blocks[a]
        down = jnp.where(row == 0, pltpu.roll(before, 1, 1), pltpu.roll(own, 1, 1))
        up = jnp.where(
            row == BAND_LAT_CELLS - 1,
            pltpu.roll(after, BAND_LAT_CELLS - 1, 1),
            pltpu.roll(own, BAND_LAT_CELLS - 1, 1),
        )
        shifted.append((down, own, up))
    pieces = []
    for a in range(3):
        for b in range(3):
            mid = shifted[1][b]
            if a == 0:
                mid = jnp.concatenate([shifted[0][b][-1:], mid[:-1]], axis=0)
            elif a == 2:
                mid = jnp.concatenate([mid[1:], shifted[2][b][:1]], axis=0)
            pieces.append(mid.reshape(CELLS, wide))
    for a in range(3):
        for b in range(3):
            pieces.append(blocks[a][b].reshape(CELLS, wide))
    for p in range(9):
        left_ref[:, p * wide : (p + 1) * wide] = jnp.where(low_half, pieces[2 * p], pieces[2 * p + 1]).astype(BF16)
    left_ref[:, 9 * wide :] = own_ref[...]
    channels = mix_ref.shape[0]
    totals, mixed = [], jnp.zeros((CELLS, channels), F32)
    for c in range(channels // BLOCK):
        cols = slice(c * BLOCK, (c + 1) * BLOCK)
        total = jnp.dot(left_ref[...], taps_ref[:, cols], preferred_element_type=F32)
        activ = jax.nn.gelu(total, approximate=True).astype(BF16)
        mixed = mixed + jnp.dot(activ, mix_ref[cols, :], preferred_element_type=F32)
        totals.append(total)
    out_ref[...] = (jnp.concatenate(totals, axis=1) + mixed).astype(BF16)


def hbm(value):
    return pltpu.with_memory_space_constraint(value, pltpu.HBM)


def swapped(value, axis, first):
    count = lax.axis_size(axis)
    pairs = [(i, (i + 1 if i % 2 == first else i - 1) % count) for i in range(count)]
    return lax.ppermute(value, axis, pairs)


def on_device(
    obs_rows, obs_cells, obs_counts, enc_weight, near_kernel_weight, far_kernel_weight, mix_weight
):
    slots, features = obs_rows.shape[2:]
    channels = mix_weight.shape[0]
    weights = [hbm(weight) for weight in (enc_weight, near_kernel_weight, far_kernel_weight)]
    weight_scratch = [pltpu.VMEM(weight.shape, BF16) for weight in weights] + [pltpu.SemaphoreType.DMA((3,))]
    params = pltpu.CompilerParams(vmem_limit_bytes=24 << 20)
    in_hbm, in_vmem = pl.BlockSpec(memory_space=pltpu.HBM), pl.BlockSpec(memory_space=pltpu.VMEM)
    sent, own, taps = pl.pallas_call(
        sums_kernel,
        out_shape=(
            pltpu.VMEM((CELLS // 2, 2 * features), BF16),
            pltpu.VMEM((CELLS, 2 * features), BF16),
            pltpu.VMEM((20 * features, channels), BF16),
        ),
        in_specs=[in_hbm] * 2 + [pl.BlockSpec(memory_space=pltpu.SMEM)] + [in_hbm] * 3,
        scratch_shapes=[
            pltpu.VMEM((features, slots), BF16),
            pltpu.VMEM((1, slots), jnp.int32),
            pltpu.SemaphoreType.DMA((2,)),
        ]
        + weight_scratch,
        compiler_params=params,
        name="cell_sums",
    )(hbm(obs_rows.reshape(slots, features).T), hbm(obs_cells.reshape(1, slots)), obs_counts, *weights)
    taps = pl.pallas_call(
        taps_kernel,
        out_shape=pltpu.VMEM((20 * features, channels), BF16),
        in_specs=[in_hbm] * 3 + [in_vmem],
        scratch_shapes=weight_scratch,
        input_output_aliases={3: 0},
        cost_estimate=pl.CostEstimate(
            flops=2 * 72 * 64 * 256 * 256 * 4, bytes_accessed=5_000_000, transcendentals=0
        ),
        compiler_params=params,
        name="encoded_taps",
    )(*weights, taps)
    even_first, odd_first = swapped(sent, "lon", 0), swapped(sent, "lon", 1)
    line = jnp.stack([sent, even_first, odd_first])
    line, taps = lax.optimization_barrier((line, taps))
    near_lat, other_lat = swapped(line, "lat", 0), swapped(line, "lat", 1)
    mixed = pl.pallas_call(
        mix_kernel,
        out_shape=jax.ShapeDtypeStruct((CELLS, channels), BF16),
        scratch_shapes=[pltpu.VMEM((CELLS, 20 * features), BF16)],
        compiler_params=pltpu.CompilerParams(vmem_limit_bytes=24 << 20),
        name="filter_and_mix",
    )(own, line, near_lat, other_lat, taps, mix_weight)
    return mixed.reshape(SECTOR_LON_CELLS, BAND_LAT_CELLS, channels)


def solution(mesh):
    return jax.shard_map(
        on_device,
        mesh=mesh,
        in_specs=(
            P("lon", "lat", None, None),
            P("lon", "lat", None),
            P("lon", "lat"),
            P(),
            P(),
            P(),
            P(),
        ),
        out_specs=P("lon", "lat", None),
        check_vma=False,
    )
```

```python
import functools

import jax
import jax.numpy as jnp
from jax import lax
from jax.experimental import pallas as pl
from jax.experimental.pallas import tpu as pltpu
from jax.sharding import PartitionSpec as P

BAND_LAT_CELLS = 8
SECTOR_LON_CELLS = 8
CELLS = BAND_LAT_CELLS * SECTOR_LON_CELLS
BLOCK = 256
F32, BF16 = jnp.float32, jnp.bfloat16


def taps_kernel(enc_ref, near_ref, far_ref, out_ref):
    features, channels = enc_ref.shape
    width = near_ref.shape[2]
    lane = lax.broadcasted_iota(jnp.int32, (width, BLOCK), 1) // width
    for t in range(18):
        ref = near_ref if t < 9 else far_ref
        for c in range(channels // BLOCK):
            cols = slice(c * BLOCK, (c + 1) * BLOCK)
            tap = ref[t % 9 // 3, t % 3, :, cols]
            dense = jnp.concatenate(
                [jnp.where(lane == g, tap, jnp.zeros((), BF16)) for g in range(BLOCK // width)], axis=0
            )
            out_ref[t * features : (t + 1) * features, cols] = jnp.dot(
                enc_ref[:, cols], dense, preferred_element_type=F32
            ).astype(BF16)
    for t in (18, 19):
        out_ref[t * features : (t + 1) * features] = enc_ref[...]


def sums_kernel(rows_hbm, cells_hbm, count_ref, sent_ref, own_ref, rows_ref, cells_ref, sems):
    copies = [
        pltpu.make_async_copy(cells_hbm, cells_ref, sems.at[0]),
        pltpu.make_async_copy(rows_hbm, rows_ref, sems.at[1]),
    ]
    for copy in copies:
        copy.start()

    slots = rows_ref.shape[1]
    slot = lax.broadcasted_iota(jnp.int32, (1, slots), 1)
    cell = lax.broadcasted_iota(jnp.int32, (CELLS, slots), 0)
    copies[0].wait()
    target = jnp.where(slot < count_ref[0, 0], cells_ref[...], -1)
    onehot = jnp.where(cell == target, 1.0, 0.0).astype(BF16)
    copies[1].wait()
    sums = lax.dot_general(
        onehot, rows_ref[...], (((1,), (1,)), ((), ())), preferred_element_type=F32
    )
    high = sums.astype(BF16).astype(F32)
    sent_ref[...] = jnp.concatenate([high[: CELLS // 2], high[CELLS // 2 :]], axis=1).astype(BF16)
    own_ref[...] = jnp.concatenate([high, sums - high], axis=1).astype(BF16)


def mix_kernel(own_ref, line_ref, near_lat_ref, other_lat_ref, taps_ref, mix_ref, out_ref, left_ref):
    features = taps_ref.shape[0] // 20
    wide = 2 * features
    packed = (SECTOR_LON_CELLS // 2, BAND_LAT_CELLS, wide)
    shape = (SECTOR_LON_CELLS, BAND_LAT_CELLS, wide)
    row = lax.broadcasted_iota(jnp.int32, shape, 1)
    half = lax.broadcasted_iota(jnp.int32, packed, 2) < features
    low_half = lax.broadcasted_iota(jnp.int32, (CELLS, wide), 1) < features
    band = lax.axis_index("lat")
    even_lat = lax.rem(band, 2) == 0

    def doubled(block):
        turned = pltpu.roll(block, features, 1).reshape(packed)
        block = block.reshape(packed)
        return jnp.concatenate([jnp.where(half, block, turned), jnp.where(half, turned, block)], axis=0)

    blocks = []
    for slot in (2, 0, 1):
        one, two = (ref[slot].astype(F32) for ref in (near_lat_ref, other_lat_ref))
        before = jnp.where(band > 0, jnp.where(even_lat, two, one), 0.0)
        after = jnp.where(band < lax.axis_size("lat") - 1, jnp.where(even_lat, one, two), 0.0)
        blocks.append([doubled(block) for block in (before, line_ref[slot].astype(F32), after)])
    shifted = []
    for a in range(3):
        before, own, after = blocks[a]
        down = jnp.where(row == 0, pltpu.roll(before, 1, 1), pltpu.roll(own, 1, 1))
        up = jnp.where(
            row == BAND_LAT_CELLS - 1,
            pltpu.roll(after, BAND_LAT_CELLS - 1, 1),
            pltpu.roll(own, BAND_LAT_CELLS - 1, 1),
        )
        shifted.append((down, own, up))
    pieces = []
    for a in range(3):
        for b in range(3):
            mid = shifted[1][b]
            if a == 0:
                mid = jnp.concatenate([shifted[0][b][-1:], mid[:-1]], axis=0)
            elif a == 2:
                mid = jnp.concatenate([mid[1:], shifted[2][b][:1]], axis=0)
            pieces.append(mid.reshape(CELLS, wide))
    for a in range(3):
        for b in range(3):
            pieces.append(blocks[a][b].reshape(CELLS, wide))
    for p in range(9):
        left_ref[:, p * wide : (p + 1) * wide] = jnp.where(low_half, pieces[2 * p], pieces[2 * p + 1]).astype(BF16)
    left_ref[:, 9 * wide :] = own_ref[...]
    channels = mix_ref.shape[0]
    totals, mixed = [], jnp.zeros((CELLS, channels), F32)
    for c in range(channels // BLOCK):
        cols = slice(c * BLOCK, (c + 1) * BLOCK)
        total = jnp.dot(left_ref[...], taps_ref[:, cols], preferred_element_type=F32)
        activ = jax.nn.gelu(total, approximate=True).astype(BF16)
        mixed = mixed + jnp.dot(activ, mix_ref[cols, :], preferred_element_type=F32)
        totals.append(total)
    out_ref[...] = (jnp.concatenate(totals, axis=1) + mixed).astype(BF16)


def hbm(value):
    return pltpu.with_memory_space_constraint(value, pltpu.HBM)


def from_neighbour(value, axis, step):
    count = lax.axis_size(axis)
    return lax.ppermute(value, axis, [((i + step) % count, i) for i in range(count)])


def swapped(value, axis, first):
    count = lax.axis_size(axis)
    pairs = [(i, (i + 1 if i % 2 == first else i - 1) % count) for i in range(count)]
    return lax.ppermute(value, axis, pairs)


def on_device(
    obs_rows, obs_cells, obs_counts, enc_weight, near_kernel_weight, far_kernel_weight, mix_weight
):
    slots, features = obs_rows.shape[2:]
    channels = mix_weight.shape[0]
    params = pltpu.CompilerParams(vmem_limit_bytes=24 << 20)
    sent, own = pl.pallas_call(
        sums_kernel,
        out_shape=(pltpu.VMEM((CELLS // 2, 2 * features), BF16), pltpu.VMEM((CELLS, 2 * features), BF16)),
        in_specs=[pl.BlockSpec(memory_space=pltpu.HBM)] * 2 + [pl.BlockSpec(memory_space=pltpu.SMEM)],
        scratch_shapes=[
            pltpu.VMEM((features, slots), BF16),
            pltpu.VMEM((1, slots), jnp.int32),
            pltpu.SemaphoreType.DMA((2,)),
        ],
        cost_estimate=pl.CostEstimate(flops=4_000_000_000, bytes_accessed=12_000_000, transcendentals=0),
        compiler_params=params,
        name="cell_sums",
    )(hbm(obs_rows.reshape(slots, features).T), hbm(obs_cells.reshape(1, slots)), obs_counts)
    taps = pl.pallas_call(
        taps_kernel,
        out_shape=pltpu.VMEM((20 * features, channels), BF16),
        cost_estimate=pl.CostEstimate(
            flops=2 * 72 * 64 * 256 * 256 * 4, bytes_accessed=5_000_000, transcendentals=0
        ),
        compiler_params=params,
        name="encoded_taps",
    )(enc_weight, near_kernel_weight, far_kernel_weight)
    line = jnp.stack([sent, from_neighbour(sent, "lon", 1), from_neighbour(sent, "lon", -1)])
    near_lat, other_lat = swapped(line, "lat", 0), swapped(line, "lat", 1)
    mixed = pl.pallas_call(
        mix_kernel,
        out_shape=jax.ShapeDtypeStruct((CELLS, channels), BF16),
        scratch_shapes=[pltpu.VMEM((CELLS, 20 * features), BF16)],
        compiler_params=pltpu.CompilerParams(vmem_limit_bytes=24 << 20),
        name="filter_and_mix",
    )(own, line, near_lat, other_lat, taps, mix_weight)
    return mixed.reshape(SECTOR_LON_CELLS, BAND_LAT_CELLS, channels)


def solution(mesh):
    return jax.shard_map(
        on_device,
        mesh=mesh,
        in_specs=(
            P("lon", "lat", None, None),
            P("lon", "lat", None),
            P("lon", "lat"),
            P(),
            P(),
            P(),
            P(),
        ),
        out_specs=P("lon", "lat", None),
        check_vma=False,
    )
```

```python
import functools

import jax
import jax.numpy as jnp
from jax import lax
from jax.experimental import pallas as pl
from jax.experimental.pallas import tpu as pltpu
from jax.sharding import PartitionSpec as P

BAND_LAT_CELLS = 8
SECTOR_LON_CELLS = 8
CELLS = BAND_LAT_CELLS * SECTOR_LON_CELLS
BLOCK = 256
TAPS_BEFORE = 12
F32, BF16 = jnp.float32, jnp.bfloat16


def taps_kernel(first, last, enc_ref, near_ref, far_ref, *refs):
    out_ref = refs[-1]
    features, channels = enc_ref.shape
    width = near_ref.shape[2]
    lane = lax.broadcasted_iota(jnp.int32, (width, BLOCK), 1) // width
    for t in range(first, min(last, 18)):
        rows = slice((t - first) * features, (t - first + 1) * features)
        ref = near_ref if t < 9 else far_ref
        for c in range(channels // BLOCK):
            cols = slice(c * BLOCK, (c + 1) * BLOCK)
            tap = ref[t % 9 // 3, t % 3, :, cols]
            dense = jnp.concatenate(
                [jnp.where(lane == g, tap, jnp.zeros((), BF16)) for g in range(BLOCK // width)], axis=0
            )
            out_ref[rows, cols] = jnp.dot(
                enc_ref[:, cols], dense, preferred_element_type=F32
            ).astype(BF16)
    for t in range(18, last):
        out_ref[(t - first) * features : (t - first + 1) * features] = enc_ref[...]


def ready_kernel(out_ref):
    out_ref[...] = jnp.zeros(out_ref.shape, F32)


def sums_kernel(_, count_ref, rows_ref, cells_ref, sent_ref, own_ref):
    slots = rows_ref.shape[1]
    slot = lax.broadcasted_iota(jnp.int32, (1, slots), 1)
    cell = lax.broadcasted_iota(jnp.int32, (CELLS, slots), 0)
    target = jnp.where(slot < count_ref[0, 0], cells_ref[...], -1)
    onehot = jnp.where(cell == target, 1.0, 0.0).astype(BF16)
    sums = lax.dot_general(
        onehot, rows_ref[...], (((1,), (1,)), ((), ())), preferred_element_type=F32
    )
    high = sums.astype(BF16).astype(F32)
    sent_ref[...] = jnp.concatenate([high[: CELLS // 2], high[CELLS // 2 :]], axis=1).astype(BF16)
    own_ref[...] = jnp.concatenate([high, sums - high], axis=1).astype(BF16)


def mix_kernel(own_ref, line_ref, near_lat_ref, other_lat_ref, taps_ref, rest_ref, mix_ref, out_ref, left_ref):
    split = taps_ref.shape[0]
    features = left_ref.shape[1] // 20
    wide = 2 * features
    packed = (SECTOR_LON_CELLS // 2, BAND_LAT_CELLS, wide)
    shape = (SECTOR_LON_CELLS, BAND_LAT_CELLS, wide)
    row = lax.broadcasted_iota(jnp.int32, shape, 1)
    half = lax.broadcasted_iota(jnp.int32, packed, 2) < features
    low_half = lax.broadcasted_iota(jnp.int32, (CELLS, wide), 1) < features
    band = lax.axis_index("lat")
    even_lat = lax.rem(band, 2) == 0

    def doubled(block):
        turned = pltpu.roll(block, features, 1).reshape(packed)
        block = block.reshape(packed)
        return jnp.concatenate([jnp.where(half, block, turned), jnp.where(half, turned, block)], axis=0)

    blocks = []
    for slot in (2, 0, 1):
        one, two = (ref[slot].astype(F32) for ref in (near_lat_ref, other_lat_ref))
        before = jnp.where(band > 0, jnp.where(even_lat, two, one), 0.0)
        after = jnp.where(band < lax.axis_size("lat") - 1, jnp.where(even_lat, one, two), 0.0)
        blocks.append([doubled(block) for block in (before, line_ref[slot].astype(F32), after)])
    shifted = []
    for a in range(3):
        before, own, after = blocks[a]
        down = jnp.where(row == 0, pltpu.roll(before, 1, 1), pltpu.roll(own, 1, 1))
        up = jnp.where(
            row == BAND_LAT_CELLS - 1,
            pltpu.roll(after, BAND_LAT_CELLS - 1, 1),
            pltpu.roll(own, BAND_LAT_CELLS - 1, 1),
        )
        shifted.append((down, own, up))
    pieces = []
    for a in range(3):
        for b in range(3):
            mid = shifted[1][b]
            if a == 0:
                mid = jnp.concatenate([shifted[0][b][-1:], mid[:-1]], axis=0)
            elif a == 2:
                mid = jnp.concatenate([mid[1:], shifted[2][b][:1]], axis=0)
            pieces.append(mid.reshape(CELLS, wide))
    for a in range(3):
        for b in range(3):
            pieces.append(blocks[a][b].reshape(CELLS, wide))
    for p in range(9):
        left_ref[:, p * wide : (p + 1) * wide] = jnp.where(low_half, pieces[2 * p], pieces[2 * p + 1]).astype(BF16)
    left_ref[:, 9 * wide :] = own_ref[...]
    channels = mix_ref.shape[0]
    totals, mixed = [], jnp.zeros((CELLS, channels), F32)
    for c in range(channels // BLOCK):
        cols = slice(c * BLOCK, (c + 1) * BLOCK)
        total = jnp.dot(left_ref[:, :split], taps_ref[:, cols], preferred_element_type=F32)
        total = total + jnp.dot(left_ref[:, split:], rest_ref[:, cols], preferred_element_type=F32)
        activ = jax.nn.gelu(total, approximate=True).astype(BF16)
        mixed = mixed + jnp.dot(activ, mix_ref[cols, :], preferred_element_type=F32)
        totals.append(total)
    out_ref[...] = (jnp.concatenate(totals, axis=1) + mixed).astype(BF16)


def from_neighbour(value, axis, step):
    count = lax.axis_size(axis)
    return lax.ppermute(value, axis, [((i + step) % count, i) for i in range(count)])


def swapped(value, axis, first):
    count = lax.axis_size(axis)
    pairs = [(i, (i + 1 if i % 2 == first else i - 1) % count) for i in range(count)]
    return lax.ppermute(value, axis, pairs)


def on_device(
    obs_rows, obs_cells, obs_counts, enc_weight, near_kernel_weight, far_kernel_weight, mix_weight
):
    slots, features = obs_rows.shape[2:]
    channels = mix_weight.shape[0]
    params = pltpu.CompilerParams(vmem_limit_bytes=24 << 20)
    in_vmem = pl.BlockSpec(memory_space=pltpu.VMEM)
    early = pl.pallas_call(
        ready_kernel,
        out_shape=pltpu.VMEM((8, 128), F32),
        cost_estimate=pl.CostEstimate(flops=4_000_000_000, bytes_accessed=12_000_000, transcendentals=0),
        compiler_params=params,
        name="ready",
    )()
    count, early = lax.optimization_barrier((obs_counts, early))
    sent, own = pl.pallas_call(
        sums_kernel,
        out_shape=(pltpu.VMEM((CELLS // 2, 2 * features), BF16), pltpu.VMEM((CELLS, 2 * features), BF16)),
        in_specs=[in_vmem, pl.BlockSpec(memory_space=pltpu.SMEM), in_vmem, in_vmem],
        cost_estimate=pl.CostEstimate(flops=4_000_000_000, bytes_accessed=12_000_000, transcendentals=0),
        compiler_params=params,
        name="cell_sums",
    )(early, count, obs_rows.reshape(slots, features).T, obs_cells.reshape(1, slots))
    def taps_of(first, last):
        return pl.pallas_call(
            functools.partial(taps_kernel, first, last),
            out_shape=pltpu.VMEM(((last - first) * features, channels), BF16),
            cost_estimate=pl.CostEstimate(
                flops=2 * 4 * (last - first) * 64 * 256 * 256 * 4, bytes_accessed=2_500_000, transcendentals=0
            ),
            compiler_params=params,
            name="encoded_taps",
        )(enc_weight, near_kernel_weight, far_kernel_weight)

    taps, rest = taps_of(0, TAPS_BEFORE), taps_of(TAPS_BEFORE, 20)
    line = jnp.stack([sent, from_neighbour(sent, "lon", 1), from_neighbour(sent, "lon", -1)])
    line, taps = lax.optimization_barrier((line, taps))
    near_lat, other_lat = swapped(line, "lat", 0), swapped(line, "lat", 1)
    mixed = pl.pallas_call(
        mix_kernel,
        out_shape=jax.ShapeDtypeStruct((CELLS, channels), BF16),
        scratch_shapes=[pltpu.VMEM((CELLS, 20 * features), BF16)],
        compiler_params=pltpu.CompilerParams(vmem_limit_bytes=24 << 20),
        name="filter_and_mix",
    )(own, line, near_lat, other_lat, taps, rest, mix_weight)
    return mixed.reshape(SECTOR_LON_CELLS, BAND_LAT_CELLS, channels)


def solution(mesh):
    return jax.shard_map(
        on_device,
        mesh=mesh,
        in_specs=(
            P("lon", "lat", None, None),
            P("lon", "lat", None),
            P("lon", "lat"),
            P(),
            P(),
            P(),
            P(),
        ),
        out_specs=P("lon", "lat", None),
        check_vma=False,
    )
```

```python
import jax
import jax.numpy as jnp
from jax import lax
from jax.experimental import pallas as pl
from jax.experimental.pallas import tpu as pltpu
from jax.sharding import PartitionSpec as P

BAND_LAT_CELLS = 8
SECTOR_LON_CELLS = 8
CELLS = BAND_LAT_CELLS * SECTOR_LON_CELLS
BLOCK = 256
INNER_TAPS = [(far, a, 1) for far in (0, 1) for a in range(3)]
OUTER_TAPS = [(far, a, b) for far in (0, 1) for b in (0, 2) for a in range(3)]
LON_SLOTS = (2, 0, 1)
F32, BF16 = jnp.float32, jnp.bfloat16


def encode(taps, enc_ref, near_ref, far_ref, out_ref):
    features, channels = enc_ref.shape
    width = near_ref.shape[2]
    lane = lax.broadcasted_iota(jnp.int32, (width, BLOCK), 1) // width
    for t, (far, a, b) in enumerate(taps):
        for c in range(channels // BLOCK):
            cols = slice(c * BLOCK, (c + 1) * BLOCK)
            tap = (far_ref if far else near_ref)[a, b, :, cols]
            dense = jnp.concatenate(
                [jnp.where(lane == g, tap, jnp.zeros((), BF16)) for g in range(BLOCK // width)], axis=0
            )
            out_ref[t * features : (t + 1) * features, cols] = jnp.dot(
                enc_ref[:, cols], dense, preferred_element_type=F32
            ).astype(BF16)


def taps_kernel(enc_ref, near_ref, far_ref, out_ref):
    encode(OUTER_TAPS, enc_ref, near_ref, far_ref, out_ref)


def doubled(block):
    rows, wide = block.shape
    packed = (SECTOR_LON_CELLS // 2, BAND_LAT_CELLS, wide)
    half = lax.broadcasted_iota(jnp.int32, packed, 2) < wide // 2
    turned = pltpu.roll(block, wide // 2, 1).reshape(packed)
    block = block.reshape(packed)
    return jnp.concatenate([jnp.where(half, block, turned), jnp.where(half, turned, block)], axis=0)


def along_lon(west, own, east):
    return (
        jnp.concatenate([west[-1:], own[:-1]], axis=0),
        own,
        jnp.concatenate([own[1:], east[:1]], axis=0),
    )


def store_pairs(pieces, left_ref):
    wide = pieces[0].shape[-1]
    low_half = lax.broadcasted_iota(jnp.int32, (CELLS, wide), 1) < wide // 2
    for p in range(len(pieces) // 2):
        first, second = (piece.reshape(CELLS, wide) for piece in pieces[2 * p : 2 * p + 2])
        left_ref[:, p * wide : (p + 1) * wide] = jnp.where(low_half, first, second).astype(BF16)


def inner_kernel(own_ref, line_ref, enc_ref, near_ref, far_ref, out_ref, taps_ref, left_ref):
    features, channels = enc_ref.shape
    west, own, east = (doubled(line_ref[slot].astype(F32)) for slot in LON_SLOTS)
    store_pairs([*along_lon(west, own, east), west, own, east], left_ref)
    left_ref[:, 6 * features :] = own_ref[...]
    encode(INNER_TAPS, enc_ref, near_ref, far_ref, taps_ref)
    for t in (6, 7):
        taps_ref[t * features : (t + 1) * features] = enc_ref[...]
    for c in range(channels // BLOCK):
        cols = slice(c * BLOCK, (c + 1) * BLOCK)
        out_ref[:, cols] = jnp.dot(left_ref[...], taps_ref[:, cols], preferred_element_type=F32)


def ready_kernel(out_ref):
    out_ref[...] = jnp.zeros(out_ref.shape, F32)


def sums_kernel(_, count_ref, rows_ref, cells_ref, sent_ref, own_ref):
    slots = rows_ref.shape[1]
    slot = lax.broadcasted_iota(jnp.int32, (1, slots), 1)
    cell = lax.broadcasted_iota(jnp.int32, (CELLS, slots), 0)
    target = jnp.where(slot < count_ref[0, 0], cells_ref[...], -1)
    onehot = jnp.where(cell == target, 1.0, 0.0).astype(BF16)
    sums = lax.dot_general(
        onehot, rows_ref[...], (((1,), (1,)), ((), ())), preferred_element_type=F32
    )
    high = sums.astype(BF16).astype(F32)
    sent_ref[...] = jnp.concatenate([high[: CELLS // 2], high[CELLS // 2 :]], axis=1).astype(BF16)
    own_ref[...] = jnp.concatenate([high, sums - high], axis=1).astype(BF16)


def mix_kernel(line_ref, before_ref, after_ref, taps_ref, inner_ref, mix_ref, out_ref, left_ref):
    wide = line_ref.shape[2]
    row = lax.broadcasted_iota(jnp.int32, (SECTOR_LON_CELLS, BAND_LAT_CELLS, wide), 1)
    band = lax.axis_index("lat")
    has_before, has_after = band > 0, band < lax.axis_size("lat") - 1
    befores, afters, downs, ups = [], [], [], []
    for slot in LON_SLOTS:
        before = doubled(jnp.where(has_before, before_ref[slot].astype(F32), 0.0))
        own = doubled(line_ref[slot].astype(F32))
        after = doubled(jnp.where(has_after, after_ref[slot].astype(F32), 0.0))
        befores.append(before)
        afters.append(after)
        downs.append(jnp.where(row == 0, pltpu.roll(before, 1, 1), pltpu.roll(own, 1, 1)))
        last = BAND_LAT_CELLS - 1
        ups.append(jnp.where(row == last, pltpu.roll(after, last, 1), pltpu.roll(own, last, 1)))
    store_pairs([*along_lon(*downs), *along_lon(*ups), *befores, *afters], left_ref)
    channels = mix_ref.shape[0]
    totals, mixed = [], jnp.zeros((CELLS, channels), F32)
    for c in range(channels // BLOCK):
        cols = slice(c * BLOCK, (c + 1) * BLOCK)
        total = inner_ref[:, cols] + jnp.dot(left_ref[...], taps_ref[:, cols], preferred_element_type=F32)
        activ = jax.nn.gelu(total, approximate=True).astype(BF16)
        mixed = mixed + jnp.dot(activ, mix_ref[cols, :], preferred_element_type=F32)
        totals.append(total)
    out_ref[...] = (jnp.concatenate(totals, axis=1) + mixed).astype(BF16)


def from_neighbour(value, axis, step):
    count = lax.axis_size(axis)
    return lax.ppermute(value, axis, [((i + step) % count, i) for i in range(count)])


def on_device(
    obs_rows, obs_cells, obs_counts, enc_weight, near_kernel_weight, far_kernel_weight, mix_weight
):
    slots, features = obs_rows.shape[2:]
    channels = mix_weight.shape[0]
    params = pltpu.CompilerParams(vmem_limit_bytes=24 << 20)
    in_vmem = pl.BlockSpec(memory_space=pltpu.VMEM)
    early = pl.pallas_call(
        ready_kernel,
        out_shape=pltpu.VMEM((8, 128), F32),
        cost_estimate=pl.CostEstimate(flops=4_000_000_000, bytes_accessed=12_000_000, transcendentals=0),
        compiler_params=params,
        name="ready",
    )()
    count, early = lax.optimization_barrier((obs_counts, early))
    sent, own = pl.pallas_call(
        sums_kernel,
        out_shape=(pltpu.VMEM((CELLS // 2, 2 * features), BF16), pltpu.VMEM((CELLS, 2 * features), BF16)),
        in_specs=[in_vmem, pl.BlockSpec(memory_space=pltpu.SMEM), in_vmem, in_vmem],
        cost_estimate=pl.CostEstimate(flops=4_000_000_000, bytes_accessed=12_000_000, transcendentals=0),
        compiler_params=params,
        name="cell_sums",
    )(early, count, obs_rows.reshape(slots, features).T, obs_cells.reshape(1, slots))
    weights = (enc_weight, near_kernel_weight, far_kernel_weight)
    taps = pl.pallas_call(
        taps_kernel,
        out_shape=pltpu.VMEM((len(OUTER_TAPS) * features, channels), BF16),
        cost_estimate=pl.CostEstimate(flops=1_600_000_000, bytes_accessed=2_500_000, transcendentals=0),
        compiler_params=params,
        name="outer_taps",
    )(*weights)
    line = jnp.stack([sent, from_neighbour(sent, "lon", 1), from_neighbour(sent, "lon", -1)])
    line, taps = lax.optimization_barrier((line, taps))
    inner = pl.pallas_call(
        inner_kernel,
        out_shape=pltpu.VMEM((CELLS, channels), F32),
        scratch_shapes=[pltpu.VMEM((8 * features, channels), BF16), pltpu.VMEM((CELLS, 8 * features), BF16)],
        cost_estimate=pl.CostEstimate(flops=1_000_000_000, bytes_accessed=2_500_000, transcendentals=0),
        compiler_params=params,
        name="inner_taps",
    )(own, line, *weights)
    mixed = pl.pallas_call(
        mix_kernel,
        out_shape=jax.ShapeDtypeStruct((CELLS, channels), BF16),
        scratch_shapes=[pltpu.VMEM((CELLS, len(OUTER_TAPS) * features), BF16)],
        compiler_params=params,
        name="filter_and_mix",
    )(line, from_neighbour(line, "lat", -1), from_neighbour(line, "lat", 1), taps, inner, mix_weight)
    return mixed.reshape(SECTOR_LON_CELLS, BAND_LAT_CELLS, channels)


def solution(mesh):
    return jax.shard_map(
        on_device,
        mesh=mesh,
        in_specs=(
            P("lon", "lat", None, None),
            P("lon", "lat", None),
            P("lon", "lat"),
            P(),
            P(),
            P(),
            P(),
        ),
        out_specs=P("lon", "lat", None),
        check_vma=False,
    )
```

```python
import jax
import jax.numpy as jnp
from jax import lax
from jax.experimental import pallas as pl
from jax.experimental.pallas import tpu as pltpu
from jax.sharding import PartitionSpec as P

BAND_LAT_CELLS = 8
SECTOR_LON_CELLS = 8
CELLS = BAND_LAT_CELLS * SECTOR_LON_CELLS
BLOCK = 256
INNER_TAPS = [(far, a, 1) for far in (0, 1) for a in range(3)]
OUTER_TAPS = [(far, a, b) for far in (0, 1) for b in (0, 2) for a in range(3)]
LON_SLOTS = (2, 0, 1)
F32, BF16 = jnp.float32, jnp.bfloat16


def encode(taps, enc_ref, near_ref, far_ref, out_ref):
    features, channels = enc_ref.shape
    width = near_ref.shape[2]
    lane = lax.broadcasted_iota(jnp.int32, (width, BLOCK), 1) // width
    for t, (far, a, b) in enumerate(taps):
        for c in range(channels // BLOCK):
            cols = slice(c * BLOCK, (c + 1) * BLOCK)
            tap = (far_ref if far else near_ref)[a, b, :, cols]
            dense = jnp.concatenate(
                [jnp.where(lane == g, tap, jnp.zeros((), BF16)) for g in range(BLOCK // width)], axis=0
            )
            out_ref[t * features : (t + 1) * features, cols] = jnp.dot(
                enc_ref[:, cols], dense, preferred_element_type=F32
            ).astype(BF16)


def taps_kernel(enc_ref, near_ref, far_ref, out_ref):
    encode(OUTER_TAPS, enc_ref, near_ref, far_ref, out_ref)


def doubled(block):
    rows, wide = block.shape
    packed = (SECTOR_LON_CELLS // 2, BAND_LAT_CELLS, wide)
    half = lax.broadcasted_iota(jnp.int32, packed, 2) < wide // 2
    turned = pltpu.roll(block, wide // 2, 1).reshape(packed)
    block = block.reshape(packed)
    return jnp.concatenate([jnp.where(half, block, turned), jnp.where(half, turned, block)], axis=0)


def along_lon(west, own, east):
    return (
        jnp.concatenate([west[-1:], own[:-1]], axis=0),
        own,
        jnp.concatenate([own[1:], east[:1]], axis=0),
    )


def store_pairs(pieces, left_ref):
    wide = pieces[0].shape[-1]
    low_half = lax.broadcasted_iota(jnp.int32, (CELLS, wide), 1) < wide // 2
    for p in range(len(pieces) // 2):
        first, second = (piece.reshape(CELLS, wide) for piece in pieces[2 * p : 2 * p + 2])
        left_ref[:, p * wide : (p + 1) * wide] = jnp.where(low_half, first, second).astype(BF16)


def inner_kernel(own_ref, line_ref, enc_ref, near_ref, far_ref, out_ref, taps_ref, left_ref):
    features, channels = enc_ref.shape
    west, own, east = (doubled(line_ref[slot].astype(F32)) for slot in LON_SLOTS)
    store_pairs([*along_lon(west, own, east), west, own, east], left_ref)
    left_ref[:, 6 * features :] = own_ref[...]
    encode(INNER_TAPS, enc_ref, near_ref, far_ref, taps_ref)
    for t in (6, 7):
        taps_ref[t * features : (t + 1) * features] = enc_ref[...]
    for c in range(channels // BLOCK):
        cols = slice(c * BLOCK, (c + 1) * BLOCK)
        out_ref[:, cols] = jnp.dot(left_ref[...], taps_ref[:, cols], preferred_element_type=F32)


def ready_kernel(out_ref):
    out_ref[...] = jnp.zeros(out_ref.shape, F32)


def sums_kernel(_, count_ref, rows_ref, cells_ref, sent_ref, own_ref):
    slots = rows_ref.shape[1]
    slot = lax.broadcasted_iota(jnp.int32, (1, slots), 1)
    cell = lax.broadcasted_iota(jnp.int32, (CELLS, slots), 0)
    target = jnp.where(slot < count_ref[0, 0], cells_ref[...], -1)
    onehot = jnp.where(cell == target, 1.0, 0.0).astype(BF16)
    sums = lax.dot_general(
        onehot, rows_ref[...], (((1,), (1,)), ((), ())), preferred_element_type=F32
    )
    high = sums.astype(BF16).astype(F32)
    sent_ref[...] = jnp.concatenate([high[: CELLS // 2], high[CELLS // 2 :]], axis=1).astype(BF16)
    own_ref[...] = jnp.concatenate([high, sums - high], axis=1).astype(BF16)


def mix_kernel(line_ref, before_ref, after_ref, taps_ref, inner_ref, mix_ref, out_ref, *scratch):
    left_ref, activ_ref, total_ref, state_ref, sems = scratch
    wide = line_ref.shape[2]
    row = lax.broadcasted_iota(jnp.int32, (SECTOR_LON_CELLS, BAND_LAT_CELLS, wide), 1)
    band = lax.axis_index("lat")
    has_before, has_after = band > 0, band < lax.axis_size("lat") - 1
    befores, afters, downs, ups = [], [], [], []
    for slot in LON_SLOTS:
        before = doubled(jnp.where(has_before, before_ref[slot].astype(F32), 0.0))
        own = doubled(line_ref[slot].astype(F32))
        after = doubled(jnp.where(has_after, after_ref[slot].astype(F32), 0.0))
        befores.append(before)
        afters.append(after)
        downs.append(jnp.where(row == 0, pltpu.roll(before, 1, 1), pltpu.roll(own, 1, 1)))
        last = BAND_LAT_CELLS - 1
        ups.append(jnp.where(row == last, pltpu.roll(after, last, 1), pltpu.roll(own, last, 1)))
    store_pairs([*along_lon(*downs), *along_lon(*ups), *befores, *afters], left_ref)
    channels = mix_ref.shape[0]
    chunks = [slice(c * BLOCK, (c + 1) * BLOCK) for c in range(channels // BLOCK)]
    for cols in chunks:
        total = inner_ref[:, cols] + jnp.dot(left_ref[...], taps_ref[:, cols], preferred_element_type=F32)
        activ_ref[:, cols] = jax.nn.gelu(total, approximate=True).astype(BF16)
        total_ref[:, cols] = total
    copies = []
    for c, cols in enumerate(chunks):
        mixed = jnp.dot(activ_ref[...], mix_ref[:, cols], preferred_element_type=F32)
        state_ref[:, cols] = (total_ref[:, cols] + mixed).astype(BF16)
        copies.append(pltpu.make_async_copy(state_ref.at[:, cols], out_ref.at[:, cols], sems.at[c]))
        copies[-1].start()
    for copy in copies:
        copy.wait()


def from_neighbour(value, axis, step):
    count = lax.axis_size(axis)
    return lax.ppermute(value, axis, [((i + step) % count, i) for i in range(count)])


def on_device(
    obs_rows, obs_cells, obs_counts, enc_weight, near_kernel_weight, far_kernel_weight, mix_weight
):
    slots, features = obs_rows.shape[2:]
    channels = mix_weight.shape[0]
    params = pltpu.CompilerParams(vmem_limit_bytes=24 << 20)
    in_vmem = pl.BlockSpec(memory_space=pltpu.VMEM)
    early = pl.pallas_call(
        ready_kernel,
        out_shape=pltpu.VMEM((8, 128), F32),
        cost_estimate=pl.CostEstimate(flops=4_000_000_000, bytes_accessed=12_000_000, transcendentals=0),
        compiler_params=params,
        name="ready",
    )()
    count, early = lax.optimization_barrier((obs_counts, early))
    sent, own = pl.pallas_call(
        sums_kernel,
        out_shape=(pltpu.VMEM((CELLS // 2, 2 * features), BF16), pltpu.VMEM((CELLS, 2 * features), BF16)),
        in_specs=[in_vmem, pl.BlockSpec(memory_space=pltpu.SMEM), in_vmem, in_vmem],
        cost_estimate=pl.CostEstimate(flops=4_000_000_000, bytes_accessed=12_000_000, transcendentals=0),
        compiler_params=params,
        name="cell_sums",
    )(early, count, obs_rows.reshape(slots, features).T, obs_cells.reshape(1, slots))
    weights = (enc_weight, near_kernel_weight, far_kernel_weight)
    taps = pl.pallas_call(
        taps_kernel,
        out_shape=pltpu.VMEM((len(OUTER_TAPS) * features, channels), BF16),
        cost_estimate=pl.CostEstimate(flops=1_600_000_000, bytes_accessed=2_500_000, transcendentals=0),
        compiler_params=params,
        name="outer_taps",
    )(*weights)
    line = jnp.stack([sent, from_neighbour(sent, "lon", 1), from_neighbour(sent, "lon", -1)])
    line, taps = lax.optimization_barrier((line, taps))
    inner = pl.pallas_call(
        inner_kernel,
        out_shape=pltpu.VMEM((CELLS, channels), F32),
        scratch_shapes=[pltpu.VMEM((8 * features, channels), BF16), pltpu.VMEM((CELLS, 8 * features), BF16)],
        cost_estimate=pl.CostEstimate(flops=1_000_000_000, bytes_accessed=2_500_000, transcendentals=0),
        compiler_params=params,
        name="inner_taps",
    )(own, line, *weights)
    mixed = pl.pallas_call(
        mix_kernel,
        out_shape=jax.ShapeDtypeStruct((CELLS, channels), BF16),
        in_specs=[in_vmem] * 6,
        out_specs=pl.BlockSpec(memory_space=pltpu.HBM),
        scratch_shapes=[
            pltpu.VMEM((CELLS, len(OUTER_TAPS) * features), BF16),
            pltpu.VMEM((CELLS, channels), BF16),
            pltpu.VMEM((CELLS, channels), F32),
            pltpu.VMEM((CELLS, channels), BF16),
            pltpu.SemaphoreType.DMA((channels // BLOCK,)),
        ],
        compiler_params=params,
        name="filter_and_mix",
    )(line, from_neighbour(line, "lat", -1), from_neighbour(line, "lat", 1), taps, inner, mix_weight)
    return mixed.reshape(SECTOR_LON_CELLS, BAND_LAT_CELLS, channels)


def solution(mesh):
    return jax.shard_map(
        on_device,
        mesh=mesh,
        in_specs=(
            P("lon", "lat", None, None),
            P("lon", "lat", None),
            P("lon", "lat"),
            P(),
            P(),
            P(),
            P(),
        ),
        out_specs=P("lon", "lat", None),
        check_vma=False,
    )
```

```python
import jax
import jax.numpy as jnp
from jax import lax
from jax.experimental import pallas as pl
from jax.experimental.pallas import tpu as pltpu
from jax.sharding import PartitionSpec as P

BAND_LAT_CELLS = 8
SECTOR_LON_CELLS = 8
CELLS = BAND_LAT_CELLS * SECTOR_LON_CELLS
BLOCK = 256
INNER_TAPS = [(far, a, 1) for far in (0, 1) for a in range(3)]
OUTER_TAPS = [(far, a, b) for far in (0, 1) for b in (0, 2) for a in range(3)]
LON_SLOTS = (2, 0, 1)
F32, BF16 = jnp.float32, jnp.bfloat16


def encode(taps, enc_ref, near_ref, far_ref, out_ref):
    features, channels = enc_ref.shape
    width = near_ref.shape[2]
    lane = lax.broadcasted_iota(jnp.int32, (width, BLOCK), 1) // width
    for t, (far, a, b) in enumerate(taps):
        for c in range(channels // BLOCK):
            cols = slice(c * BLOCK, (c + 1) * BLOCK)
            tap = (far_ref if far else near_ref)[a, b, :, cols]
            dense = jnp.concatenate(
                [jnp.where(lane == g, tap, jnp.zeros((), BF16)) for g in range(BLOCK // width)], axis=0
            )
            out_ref[t * features : (t + 1) * features, cols] = jnp.dot(
                enc_ref[:, cols], dense, preferred_element_type=F32
            ).astype(BF16)


def taps_kernel(enc_ref, near_ref, far_ref, out_ref):
    encode(OUTER_TAPS, enc_ref, near_ref, far_ref, out_ref)


def doubled(block):
    rows, wide = block.shape
    packed = (SECTOR_LON_CELLS // 2, BAND_LAT_CELLS, wide)
    half = lax.broadcasted_iota(jnp.int32, packed, 2) < wide // 2
    turned = pltpu.roll(block, wide // 2, 1).reshape(packed)
    block = block.reshape(packed)
    return jnp.concatenate([jnp.where(half, block, turned), jnp.where(half, turned, block)], axis=0)


def along_lon(west, own, east):
    return (
        jnp.concatenate([west[-1:], own[:-1]], axis=0),
        own,
        jnp.concatenate([own[1:], east[:1]], axis=0),
    )


def store_pairs(pieces, left_ref):
    wide = pieces[0].shape[-1]
    low_half = lax.broadcasted_iota(jnp.int32, (CELLS, wide), 1) < wide // 2
    for p in range(len(pieces) // 2):
        first, second = (piece.reshape(CELLS, wide) for piece in pieces[2 * p : 2 * p + 2])
        left_ref[:, p * wide : (p + 1) * wide] = jnp.where(low_half, first, second).astype(BF16)


def inner_kernel(own_ref, line_ref, enc_ref, near_ref, far_ref, out_ref, taps_ref, left_ref):
    features, channels = enc_ref.shape
    west, own, east = (doubled(line_ref[slot].astype(F32)) for slot in LON_SLOTS)
    store_pairs([*along_lon(west, own, east), west, own, east], left_ref)
    left_ref[:, 6 * features :] = own_ref[...]
    encode(INNER_TAPS, enc_ref, near_ref, far_ref, taps_ref)
    for t in (6, 7):
        taps_ref[t * features : (t + 1) * features] = enc_ref[...]
    for c in range(channels // BLOCK):
        cols = slice(c * BLOCK, (c + 1) * BLOCK)
        out_ref[:, cols] = jnp.dot(left_ref[...], taps_ref[:, cols], preferred_element_type=F32)


def ready_kernel(out_ref):
    out_ref[...] = jnp.zeros(out_ref.shape, F32)


def sums_kernel(_, count_ref, rows_ref, cells_ref, sent_ref, own_ref):
    slots = rows_ref.shape[1]
    slot = lax.broadcasted_iota(jnp.int32, (1, slots), 1)
    cell = lax.broadcasted_iota(jnp.int32, (CELLS, slots), 0)
    target = jnp.where(slot < count_ref[0, 0], cells_ref[...], -1)
    onehot = jnp.where(cell == target, 1.0, 0.0).astype(BF16)
    sums = lax.dot_general(
        onehot, rows_ref[...], (((1,), (1,)), ((), ())), preferred_element_type=F32
    )
    high = sums.astype(BF16).astype(F32)
    sent_ref[...] = jnp.concatenate([high[: CELLS // 2], high[CELLS // 2 :]], axis=1).astype(BF16)
    own_ref[...] = jnp.concatenate([high, sums - high], axis=1).astype(BF16)


def mix_kernel(line_ref, even_ref, odd_ref, taps_ref, inner_ref, mix_ref, out_ref, *scratch):
    left_ref, activ_ref, total_ref, state_ref, sems = scratch
    wide = line_ref.shape[2]
    row = lax.broadcasted_iota(jnp.int32, (SECTOR_LON_CELLS, BAND_LAT_CELLS, wide), 1)
    band = lax.axis_index("lat")
    even = lax.rem(band, 2) == 0
    has_before, has_after = band > 0, band < lax.axis_size("lat") - 1
    befores, afters, downs, ups = [], [], [], []
    for slot in LON_SLOTS:
        from_even, from_odd = even_ref[slot].astype(F32), odd_ref[slot].astype(F32)
        before = doubled(jnp.where(has_before, jnp.where(even, from_odd, from_even), 0.0))
        own = doubled(line_ref[slot].astype(F32))
        after = doubled(jnp.where(has_after, jnp.where(even, from_even, from_odd), 0.0))
        befores.append(before)
        afters.append(after)
        downs.append(jnp.where(row == 0, pltpu.roll(before, 1, 1), pltpu.roll(own, 1, 1)))
        last = BAND_LAT_CELLS - 1
        ups.append(jnp.where(row == last, pltpu.roll(after, last, 1), pltpu.roll(own, last, 1)))
    store_pairs([*along_lon(*downs), *along_lon(*ups), *befores, *afters], left_ref)
    channels = mix_ref.shape[0]
    chunks = [slice(c * BLOCK, (c + 1) * BLOCK) for c in range(channels // BLOCK)]
    for cols in chunks:
        total = inner_ref[:, cols] + jnp.dot(left_ref[...], taps_ref[:, cols], preferred_element_type=F32)
        activ_ref[:, cols] = jax.nn.gelu(total, approximate=True).astype(BF16)
        total_ref[:, cols] = total
    copies = []
    for c, cols in enumerate(chunks):
        mixed = jnp.dot(activ_ref[...], mix_ref[:, cols], preferred_element_type=F32)
        state_ref[:, cols] = (total_ref[:, cols] + mixed).astype(BF16)
        copies.append(pltpu.make_async_copy(state_ref.at[:, cols], out_ref.at[:, cols], sems.at[c]))
        copies[-1].start()
    for copy in copies:
        copy.wait()


def from_neighbour(value, axis, step):
    count = lax.axis_size(axis)
    return lax.ppermute(value, axis, [((i + step) % count, i) for i in range(count)])


def swapped(value, axis, first):
    count = lax.axis_size(axis)
    pairs = [(i, (i + 1 if i % 2 == first else i - 1) % count) for i in range(count)]
    return lax.ppermute(value, axis, pairs)


def on_device(
    obs_rows, obs_cells, obs_counts, enc_weight, near_kernel_weight, far_kernel_weight, mix_weight
):
    slots, features = obs_rows.shape[2:]
    channels = mix_weight.shape[0]
    params = pltpu.CompilerParams(vmem_limit_bytes=24 << 20)
    in_vmem = pl.BlockSpec(memory_space=pltpu.VMEM)
    early = pl.pallas_call(
        ready_kernel,
        out_shape=pltpu.VMEM((8, 128), F32),
        cost_estimate=pl.CostEstimate(flops=4_000_000_000, bytes_accessed=12_000_000, transcendentals=0),
        compiler_params=params,
        name="ready",
    )()
    count, early = lax.optimization_barrier((obs_counts, early))
    sent, own = pl.pallas_call(
        sums_kernel,
        out_shape=(pltpu.VMEM((CELLS // 2, 2 * features), BF16), pltpu.VMEM((CELLS, 2 * features), BF16)),
        in_specs=[in_vmem, pl.BlockSpec(memory_space=pltpu.SMEM), in_vmem, in_vmem],
        cost_estimate=pl.CostEstimate(flops=4_000_000_000, bytes_accessed=12_000_000, transcendentals=0),
        compiler_params=params,
        name="cell_sums",
    )(early, count, obs_rows.reshape(slots, features).T, obs_cells.reshape(1, slots))
    weights = (enc_weight, near_kernel_weight, far_kernel_weight)
    taps = pl.pallas_call(
        taps_kernel,
        out_shape=pltpu.VMEM((len(OUTER_TAPS) * features, channels), BF16),
        cost_estimate=pl.CostEstimate(flops=1_600_000_000, bytes_accessed=2_500_000, transcendentals=0),
        compiler_params=params,
        name="outer_taps",
    )(*weights)
    line = jnp.stack([sent, from_neighbour(sent, "lon", 1), from_neighbour(sent, "lon", -1)])
    line, taps = lax.optimization_barrier((line, taps))
    inner = pl.pallas_call(
        inner_kernel,
        out_shape=pltpu.VMEM((CELLS, channels), F32),
        scratch_shapes=[pltpu.VMEM((8 * features, channels), BF16), pltpu.VMEM((CELLS, 8 * features), BF16)],
        cost_estimate=pl.CostEstimate(flops=1_000_000_000, bytes_accessed=2_500_000, transcendentals=0),
        compiler_params=params,
        name="inner_taps",
    )(own, line, *weights)
    mixed = pl.pallas_call(
        mix_kernel,
        out_shape=jax.ShapeDtypeStruct((CELLS, channels), BF16),
        in_specs=[in_vmem] * 6,
        out_specs=pl.BlockSpec(memory_space=pltpu.HBM),
        scratch_shapes=[
            pltpu.VMEM((CELLS, len(OUTER_TAPS) * features), BF16),
            pltpu.VMEM((CELLS, channels), BF16),
            pltpu.VMEM((CELLS, channels), F32),
            pltpu.VMEM((CELLS, channels), BF16),
            pltpu.SemaphoreType.DMA((channels // BLOCK,)),
        ],
        compiler_params=params,
        name="filter_and_mix",
    )(line, swapped(line, "lat", 0), swapped(line, "lat", 1), taps, inner, mix_weight)
    return mixed.reshape(SECTOR_LON_CELLS, BAND_LAT_CELLS, channels)


def solution(mesh):
    return jax.shard_map(
        on_device,
        mesh=mesh,
        in_specs=(
            P("lon", "lat", None, None),
            P("lon", "lat", None),
            P("lon", "lat"),
            P(),
            P(),
            P(),
            P(),
        ),
        out_specs=P("lon", "lat", None),
        check_vma=False,
    )
```

```python
import jax
import jax.numpy as jnp
from jax import lax
from jax.experimental import pallas as pl
from jax.experimental.pallas import tpu as pltpu
from jax.sharding import PartitionSpec as P

BAND_LAT_CELLS = 8
SECTOR_LON_CELLS = 8
CELLS = BAND_LAT_CELLS * SECTOR_LON_CELLS
BLOCK = 256
INNER_TAPS = [(far, a, 1) for far in (0, 1) for a in range(3)]
OUTER_TAPS = [(far, a, b) for far in (0, 1) for b in (0, 2) for a in range(3)]
LON_SLOTS = (2, 0, 1)
F32, BF16 = jnp.float32, jnp.bfloat16


def encode(taps, enc_ref, near_ref, far_ref, out_ref):
    features, channels = enc_ref.shape
    width = near_ref.shape[2]
    lane = lax.broadcasted_iota(jnp.int32, (width, BLOCK), 1) // width
    for t, (far, a, b) in enumerate(taps):
        for c in range(channels // BLOCK):
            cols = slice(c * BLOCK, (c + 1) * BLOCK)
            tap = (far_ref if far else near_ref)[a, b, :, cols]
            dense = jnp.concatenate(
                [jnp.where(lane == g, tap, jnp.zeros((), BF16)) for g in range(BLOCK // width)], axis=0
            )
            out_ref[t * features : (t + 1) * features, cols] = jnp.dot(
                enc_ref[:, cols], dense, preferred_element_type=F32
            ).astype(BF16)


def taps_kernel(enc_ref, near_ref, far_ref, out_ref):
    encode(OUTER_TAPS, enc_ref, near_ref, far_ref, out_ref)


def doubled(block):
    rows, wide = block.shape
    packed = (SECTOR_LON_CELLS // 2, BAND_LAT_CELLS, wide)
    half = lax.broadcasted_iota(jnp.int32, packed, 2) < wide // 2
    turned = pltpu.roll(block, wide // 2, 1).reshape(packed)
    block = block.reshape(packed)
    return jnp.concatenate([jnp.where(half, block, turned), jnp.where(half, turned, block)], axis=0)


def along_lon(west, own, east):
    return (
        jnp.concatenate([west[-1:], own[:-1]], axis=0),
        own,
        jnp.concatenate([own[1:], east[:1]], axis=0),
    )


def store_pairs(pieces, left_ref):
    wide = pieces[0].shape[-1]
    low_half = lax.broadcasted_iota(jnp.int32, (CELLS, wide), 1) < wide // 2
    for p in range(len(pieces) // 2):
        first, second = (piece.reshape(CELLS, wide) for piece in pieces[2 * p : 2 * p + 2])
        left_ref[:, p * wide : (p + 1) * wide] = jnp.where(low_half, first, second).astype(BF16)


def inner_kernel(own_ref, line_ref, enc_ref, near_ref, far_ref, out_ref, taps_ref, left_ref):
    features, channels = enc_ref.shape
    west, own, east = (doubled(line_ref[slot].astype(F32)) for slot in LON_SLOTS)
    store_pairs([*along_lon(west, own, east), west, own, east], left_ref)
    left_ref[:, 6 * features :] = own_ref[...]
    encode(INNER_TAPS, enc_ref, near_ref, far_ref, taps_ref)
    for t in (6, 7):
        taps_ref[t * features : (t + 1) * features] = enc_ref[...]
    for c in range(channels // BLOCK):
        cols = slice(c * BLOCK, (c + 1) * BLOCK)
        out_ref[:, cols] = jnp.dot(left_ref[...], taps_ref[:, cols], preferred_element_type=F32)


def ready_kernel(out_ref):
    out_ref[...] = jnp.zeros(out_ref.shape, F32)


def sums_kernel(_, count_ref, cells_ref, rows_ref, sent_ref, own_ref):
    slots = rows_ref.shape[1]
    slot = lax.broadcasted_iota(jnp.int32, (1, slots), 1)
    cell = lax.broadcasted_iota(jnp.int32, (CELLS, slots), 0)
    target = jnp.where(slot < count_ref[0, 0], cells_ref[...], -1)
    onehot = jnp.where(cell == target, 1.0, 0.0).astype(BF16)
    sums = lax.dot_general(
        onehot, rows_ref[...], (((1,), (1,)), ((), ())), preferred_element_type=F32
    )
    high = sums.astype(BF16).astype(F32)
    sent_ref[...] = jnp.concatenate([high[: CELLS // 2], high[CELLS // 2 :]], axis=1).astype(BF16)
    own_ref[...] = jnp.concatenate([high, sums - high], axis=1).astype(BF16)


def mix_kernel(line_ref, even_ref, odd_ref, taps_ref, inner_ref, mix_ref, out_ref, *scratch):
    left_ref, activ_ref, total_ref, state_ref, sems = scratch
    wide = line_ref.shape[2]
    row = lax.broadcasted_iota(jnp.int32, (SECTOR_LON_CELLS, BAND_LAT_CELLS, wide), 1)
    band = lax.axis_index("lat")
    even = lax.rem(band, 2) == 0
    has_before, has_after = band > 0, band < lax.axis_size("lat") - 1
    befores, afters, downs, ups = [], [], [], []
    for slot in LON_SLOTS:
        from_even, from_odd = even_ref[slot].astype(F32), odd_ref[slot].astype(F32)
        before = doubled(jnp.where(has_before, jnp.where(even, from_odd, from_even), 0.0))
        own = doubled(line_ref[slot].astype(F32))
        after = doubled(jnp.where(has_after, jnp.where(even, from_even, from_odd), 0.0))
        befores.append(before)
        afters.append(after)
        downs.append(jnp.where(row == 0, pltpu.roll(before, 1, 1), pltpu.roll(own, 1, 1)))
        last = BAND_LAT_CELLS - 1
        ups.append(jnp.where(row == last, pltpu.roll(after, last, 1), pltpu.roll(own, last, 1)))
    store_pairs([*along_lon(*downs), *along_lon(*ups), *befores, *afters], left_ref)
    channels = mix_ref.shape[0]
    chunks = [slice(c * BLOCK, (c + 1) * BLOCK) for c in range(channels // BLOCK)]
    for cols in chunks:
        total = inner_ref[:, cols] + jnp.dot(left_ref[...], taps_ref[:, cols], preferred_element_type=F32)
        activ_ref[:, cols] = jax.nn.gelu(total, approximate=True).astype(BF16)
        total_ref[:, cols] = total
    copies = []
    for c, cols in enumerate(chunks):
        mixed = jnp.dot(activ_ref[...], mix_ref[:, cols], preferred_element_type=F32)
        state_ref[:, cols] = (total_ref[:, cols] + mixed).astype(BF16)
        copies.append(pltpu.make_async_copy(state_ref.at[:, cols], out_ref.at[:, cols], sems.at[c]))
        copies[-1].start()
    for copy in copies:
        copy.wait()


def from_neighbour(value, axis, step):
    count = lax.axis_size(axis)
    return lax.ppermute(value, axis, [((i + step) % count, i) for i in range(count)])


def swapped(value, axis, first):
    count = lax.axis_size(axis)
    partner = [i + 1 if i % 2 == first else i - 1 for i in range(count)]
    return lax.ppermute(value, axis, [(i, p if 0 <= p < count else i) for i, p in enumerate(partner)])


def on_device(
    obs_rows, obs_cells, obs_counts, enc_weight, near_kernel_weight, far_kernel_weight, mix_weight
):
    slots, features = obs_rows.shape[2:]
    channels = mix_weight.shape[0]
    params = pltpu.CompilerParams(vmem_limit_bytes=24 << 20)
    in_vmem = pl.BlockSpec(memory_space=pltpu.VMEM)
    early = pl.pallas_call(
        ready_kernel,
        out_shape=pltpu.VMEM((8, 128), F32),
        cost_estimate=pl.CostEstimate(flops=4_000_000_000, bytes_accessed=12_000_000, transcendentals=0),
        compiler_params=params,
        name="ready",
    )()
    count, early = lax.optimization_barrier((obs_counts, early))
    sent, own = pl.pallas_call(
        sums_kernel,
        out_shape=(pltpu.VMEM((CELLS // 2, 2 * features), BF16), pltpu.VMEM((CELLS, 2 * features), BF16)),
        in_specs=[in_vmem, pl.BlockSpec(memory_space=pltpu.SMEM), in_vmem, in_vmem],
        cost_estimate=pl.CostEstimate(flops=4_000_000_000, bytes_accessed=12_000_000, transcendentals=0),
        compiler_params=params,
        name="cell_sums",
    )(early, count, obs_cells.reshape(1, slots), obs_rows.reshape(slots, features).T)
    weights = (enc_weight, near_kernel_weight, far_kernel_weight)
    taps = pl.pallas_call(
        taps_kernel,
        out_shape=pltpu.VMEM((len(OUTER_TAPS) * features, channels), BF16),
        cost_estimate=pl.CostEstimate(flops=1_600_000_000, bytes_accessed=2_500_000, transcendentals=0),
        compiler_params=params,
        name="outer_taps",
    )(*weights)
    line = jnp.stack([sent, from_neighbour(sent, "lon", 1), from_neighbour(sent, "lon", -1)])
    line, taps = lax.optimization_barrier((line, taps))
    inner = pl.pallas_call(
        inner_kernel,
        out_shape=pltpu.VMEM((CELLS, channels), F32),
        scratch_shapes=[pltpu.VMEM((8 * features, channels), BF16), pltpu.VMEM((CELLS, 8 * features), BF16)],
        cost_estimate=pl.CostEstimate(flops=1_000_000_000, bytes_accessed=2_500_000, transcendentals=0),
        compiler_params=params,
        name="inner_taps",
    )(own, line, *weights)
    mixed = pl.pallas_call(
        mix_kernel,
        out_shape=jax.ShapeDtypeStruct((CELLS, channels), BF16),
        in_specs=[in_vmem] * 6,
        out_specs=pl.BlockSpec(memory_space=pltpu.HBM),
        scratch_shapes=[
            pltpu.VMEM((CELLS, len(OUTER_TAPS) * features), BF16),
            pltpu.VMEM((CELLS, channels), BF16),
            pltpu.VMEM((CELLS, channels), F32),
            pltpu.VMEM((CELLS, channels), BF16),
            pltpu.SemaphoreType.DMA((channels // BLOCK,)),
        ],
        compiler_params=params,
        name="filter_and_mix",
    )(line, swapped(line, "lat", 0), swapped(line, "lat", 1), taps, inner, mix_weight)
    return mixed.reshape(SECTOR_LON_CELLS, BAND_LAT_CELLS, channels)


def solution(mesh):
    return jax.shard_map(
        on_device,
        mesh=mesh,
        in_specs=(
            P("lon", "lat", None, None),
            P("lon", "lat", None),
            P("lon", "lat"),
            P(),
            P(),
            P(),
            P(),
        ),
        out_specs=P("lon", "lat", None),
        check_vma=False,
    )
```

```python
import jax
import jax.numpy as jnp
from jax import lax
from jax.experimental import pallas as pl
from jax.experimental.pallas import tpu as pltpu
from jax.sharding import PartitionSpec as P

BAND_LAT_CELLS = 8
SECTOR_LON_CELLS = 8
CELLS = BAND_LAT_CELLS * SECTOR_LON_CELLS
BLOCK = 256
INNER_TAPS = [(far, a, 1) for far in (0, 1) for a in range(3)]
OUTER_TAPS = [(far, a, b) for far in (0, 1) for b in (0, 2) for a in range(3)]
LON_SLOTS = (2, 0, 1)
F32, BF16 = jnp.float32, jnp.bfloat16


def encode(taps, enc_ref, near_ref, far_ref, out_ref):
    features, channels = enc_ref.shape
    width = near_ref.shape[2]
    lane = lax.broadcasted_iota(jnp.int32, (width, BLOCK), 1) // width
    for t, (far, a, b) in enumerate(taps):
        for c in range(channels // BLOCK):
            cols = slice(c * BLOCK, (c + 1) * BLOCK)
            tap = (far_ref if far else near_ref)[a, b, :, cols]
            dense = jnp.concatenate(
                [jnp.where(lane == g, tap, jnp.zeros((), BF16)) for g in range(BLOCK // width)], axis=0
            )
            out_ref[t * features : (t + 1) * features, cols] = jnp.dot(
                enc_ref[:, cols], dense, preferred_element_type=F32
            ).astype(BF16)


def taps_kernel(enc_ref, near_ref, far_ref, out_ref):
    encode(OUTER_TAPS, enc_ref, near_ref, far_ref, out_ref)


def doubled(block):
    rows, wide = block.shape
    packed = (SECTOR_LON_CELLS // 2, BAND_LAT_CELLS, wide)
    half = lax.broadcasted_iota(jnp.int32, packed, 2) < wide // 2
    turned = pltpu.roll(block, wide // 2, 1).reshape(packed)
    block = block.reshape(packed)
    return jnp.concatenate([jnp.where(half, block, turned), jnp.where(half, turned, block)], axis=0)


def along_lon(west, own, east):
    return (
        jnp.concatenate([west[-1:], own[:-1]], axis=0),
        own,
        jnp.concatenate([own[1:], east[:1]], axis=0),
    )


def store_pairs(pieces, left_ref):
    wide = pieces[0].shape[-1]
    low_half = lax.broadcasted_iota(jnp.int32, (CELLS, wide), 1) < wide // 2
    for p in range(len(pieces) // 2):
        first, second = (piece.reshape(CELLS, wide) for piece in pieces[2 * p : 2 * p + 2])
        left_ref[:, p * wide : (p + 1) * wide] = jnp.where(low_half, first, second).astype(BF16)


def inner_kernel(own_ref, line_ref, enc_ref, near_ref, far_ref, out_ref, taps_ref, left_ref):
    features, channels = enc_ref.shape
    west, own, east = (doubled(line_ref[slot].astype(F32)) for slot in LON_SLOTS)
    store_pairs([*along_lon(west, own, east), west, own, east], left_ref)
    left_ref[:, 6 * features :] = own_ref[...]
    encode(INNER_TAPS, enc_ref, near_ref, far_ref, taps_ref)
    for t in (6, 7):
        taps_ref[t * features : (t + 1) * features] = enc_ref[...]
    for c in range(channels // BLOCK):
        cols = slice(c * BLOCK, (c + 1) * BLOCK)
        out_ref[:, cols] = jnp.dot(left_ref[...], taps_ref[:, cols], preferred_element_type=F32)


def ready_kernel(out_ref):
    out_ref[...] = jnp.zeros(out_ref.shape, F32)


def sums_kernel(_, count_ref, rows_ref, cells_ref, sent_ref, own_ref):
    slots = rows_ref.shape[1]
    slot = lax.broadcasted_iota(jnp.int32, (1, slots), 1)
    cell = lax.broadcasted_iota(jnp.int32, (CELLS, slots), 0)
    target = jnp.where(slot < count_ref[0, 0], cells_ref[...], -1)
    onehot = jnp.where(cell == target, 1.0, 0.0).astype(BF16)
    sums = lax.dot_general(
        onehot, rows_ref[...], (((1,), (1,)), ((), ())), preferred_element_type=F32
    )
    high = sums.astype(BF16).astype(F32)
    sent_ref[...] = jnp.concatenate([high[: CELLS // 2], high[CELLS // 2 :]], axis=1).astype(BF16)
    own_ref[...] = jnp.concatenate([high, sums - high], axis=1).astype(BF16)


def mix_kernel(line_ref, even_ref, odd_ref, taps_ref, inner_ref, mix_ref, out_ref, *scratch):
    left_ref, activ_ref, total_ref, state_ref, sems = scratch
    wide = line_ref.shape[2]
    row = lax.broadcasted_iota(jnp.int32, (SECTOR_LON_CELLS, BAND_LAT_CELLS, wide), 1)
    band = lax.axis_index("lat")
    even = lax.rem(band, 2) == 0
    has_before, has_after = band > 0, band < lax.axis_size("lat") - 1
    befores, afters, downs, ups = [], [], [], []
    for slot in LON_SLOTS:
        from_even, from_odd = even_ref[slot].astype(F32), odd_ref[slot].astype(F32)
        before = doubled(jnp.where(has_before, jnp.where(even, from_odd, from_even), 0.0))
        own = doubled(line_ref[slot].astype(F32))
        after = doubled(jnp.where(has_after, jnp.where(even, from_even, from_odd), 0.0))
        befores.append(before)
        afters.append(after)
        downs.append(jnp.where(row == 0, pltpu.roll(before, 1, 1), pltpu.roll(own, 1, 1)))
        last = BAND_LAT_CELLS - 1
        ups.append(jnp.where(row == last, pltpu.roll(after, last, 1), pltpu.roll(own, last, 1)))
    store_pairs([*along_lon(*downs), *along_lon(*ups), *befores, *afters], left_ref)
    channels = mix_ref.shape[0]
    chunks = [slice(c * BLOCK, (c + 1) * BLOCK) for c in range(channels // BLOCK)]
    for cols in chunks:
        total = inner_ref[:, cols] + jnp.dot(left_ref[...], taps_ref[:, cols], preferred_element_type=F32)
        activ_ref[:, cols] = jax.nn.gelu(total, approximate=True).astype(BF16)
        total_ref[:, cols] = total
    copies = []
    half = CELLS // 2
    for cols in chunks[:-1] + [slice(channels - BLOCK, channels - BLOCK // 2), slice(channels - BLOCK // 2, channels)]:
        mixed = jnp.dot(activ_ref[...], mix_ref[:, cols], preferred_element_type=F32)
        state_ref[:, cols] = (total_ref[:, cols] + mixed).astype(BF16)
        for rows in (slice(0, half), slice(half, CELLS)):
            copy = pltpu.make_async_copy(state_ref.at[rows, cols], out_ref.at[rows, cols], sems.at[len(copies)])
            copy.start()
            copies.append(copy)
    for copy in copies:
        copy.wait()


def from_neighbour(value, axis, step):
    count = lax.axis_size(axis)
    return lax.ppermute(value, axis, [((i + step) % count, i) for i in range(count)])


def lat_swapped(value, first):
    sectors, bands = lax.axis_size("lon"), lax.axis_size("lat")
    pairs = []
    for lon in range(sectors):
        for lat in range(bands):
            partner = lat + 1 if lat % 2 == first else lat - 1
            inside = 0 <= partner < bands
            other = lon if inside else (lon + 1 if lon % 2 == 0 else lon - 1) % sectors
            pairs.append((lon * bands + lat, other * bands + (partner if inside else lat)))
    return lax.ppermute(value, ("lon", "lat"), pairs)


def on_device(
    obs_rows, obs_cells, obs_counts, enc_weight, near_kernel_weight, far_kernel_weight, mix_weight
):
    slots, features = obs_rows.shape[2:]
    channels = mix_weight.shape[0]
    params = pltpu.CompilerParams(vmem_limit_bytes=24 << 20)
    in_vmem = pl.BlockSpec(memory_space=pltpu.VMEM)
    early = pl.pallas_call(
        ready_kernel,
        out_shape=pltpu.VMEM((8, 128), F32),
        cost_estimate=pl.CostEstimate(flops=4_000_000_000, bytes_accessed=12_000_000, transcendentals=0),
        compiler_params=params,
        name="ready",
    )()
    count, early = lax.optimization_barrier((obs_counts, early))
    sent, own = pl.pallas_call(
        sums_kernel,
        out_shape=(pltpu.VMEM((CELLS // 2, 2 * features), BF16), pltpu.VMEM((CELLS, 2 * features), BF16)),
        in_specs=[in_vmem, pl.BlockSpec(memory_space=pltpu.SMEM), in_vmem, in_vmem],
        cost_estimate=pl.CostEstimate(flops=4_000_000_000, bytes_accessed=12_000_000, transcendentals=0),
        compiler_params=params,
        name="cell_sums",
    )(early, count, obs_rows.reshape(slots, features).T, obs_cells.reshape(1, slots))
    weights = (enc_weight, near_kernel_weight, far_kernel_weight)
    taps = pl.pallas_call(
        taps_kernel,
        out_shape=pltpu.VMEM((len(OUTER_TAPS) * features, channels), BF16),
        cost_estimate=pl.CostEstimate(flops=1_600_000_000, bytes_accessed=2_500_000, transcendentals=0),
        compiler_params=params,
        name="outer_taps",
    )(*weights)
    line = jnp.stack([sent, from_neighbour(sent, "lon", 1), from_neighbour(sent, "lon", -1)])
    line, taps = lax.optimization_barrier((line, taps))
    inner = pl.pallas_call(
        inner_kernel,
        out_shape=pltpu.VMEM((CELLS, channels), F32),
        scratch_shapes=[pltpu.VMEM((8 * features, channels), BF16), pltpu.VMEM((CELLS, 8 * features), BF16)],
        cost_estimate=pl.CostEstimate(flops=1_000_000_000, bytes_accessed=2_500_000, transcendentals=0),
        compiler_params=params,
        name="inner_taps",
    )(own, line, *weights)
    mixed = pl.pallas_call(
        mix_kernel,
        out_shape=jax.ShapeDtypeStruct((CELLS, channels), BF16),
        in_specs=[in_vmem] * 6,
        out_specs=pl.BlockSpec(memory_space=pltpu.HBM),
        scratch_shapes=[
            pltpu.VMEM((CELLS, len(OUTER_TAPS) * features), BF16),
            pltpu.VMEM((CELLS, channels), BF16),
            pltpu.VMEM((CELLS, channels), F32),
            pltpu.VMEM((CELLS, channels), BF16),
            pltpu.SemaphoreType.DMA((2 * (channels // BLOCK + 1),)),
        ],
        compiler_params=params,
        name="filter_and_mix",
    )(line, lat_swapped(line, 0), lat_swapped(line, 1), taps, inner, mix_weight)
    return mixed.reshape(SECTOR_LON_CELLS, BAND_LAT_CELLS, channels)


def solution(mesh):
    return jax.shard_map(
        on_device,
        mesh=mesh,
        in_specs=(
            P("lon", "lat", None, None),
            P("lon", "lat", None),
            P("lon", "lat"),
            P(),
            P(),
            P(),
            P(),
        ),
        out_specs=P("lon", "lat", None),
        check_vma=False,
    )
```

```python
import jax
import jax.numpy as jnp
from jax import lax
from jax.experimental import pallas as pl
from jax.experimental.pallas import tpu as pltpu
from jax.sharding import PartitionSpec as P

BAND_LAT_CELLS = 8
SECTOR_LON_CELLS = 8
CELLS = BAND_LAT_CELLS * SECTOR_LON_CELLS
BLOCK = 256
INNER_TAPS = [(far, a, 1) for far in (0, 1) for a in range(3)]
OUTER_TAPS = [(far, a, b) for far in (0, 1) for b in (0, 2) for a in range(3)]
LON_SLOTS = (2, 0, 1)
F32, BF16 = jnp.float32, jnp.bfloat16


def encode(taps, enc_ref, near_ref, far_ref, out_ref):
    features, channels = enc_ref.shape
    width = near_ref.shape[2]
    lane = lax.broadcasted_iota(jnp.int32, (width, BLOCK), 1) // width
    for t, (far, a, b) in enumerate(taps):
        for c in range(channels // BLOCK):
            cols = slice(c * BLOCK, (c + 1) * BLOCK)
            tap = (far_ref if far else near_ref)[a, b, :, cols]
            dense = jnp.concatenate(
                [jnp.where(lane == g, tap, jnp.zeros((), BF16)) for g in range(BLOCK // width)], axis=0
            )
            out_ref[t * features : (t + 1) * features, cols] = jnp.dot(
                enc_ref[:, cols], dense, preferred_element_type=F32
            ).astype(BF16)


def taps_kernel(enc_ref, near_ref, far_ref, out_ref):
    encode(OUTER_TAPS, enc_ref, near_ref, far_ref, out_ref)


def doubled(block):
    rows, wide = block.shape
    packed = (SECTOR_LON_CELLS // 2, BAND_LAT_CELLS, wide)
    half = lax.broadcasted_iota(jnp.int32, packed, 2) < wide // 2
    turned = pltpu.roll(block, wide // 2, 1).reshape(packed)
    block = block.reshape(packed)
    return jnp.concatenate([jnp.where(half, block, turned), jnp.where(half, turned, block)], axis=0)


def along_lon(west, own, east):
    return (
        jnp.concatenate([west[-1:], own[:-1]], axis=0),
        own,
        jnp.concatenate([own[1:], east[:1]], axis=0),
    )


def store_pairs(pieces, left_ref):
    wide = pieces[0].shape[-1]
    low_half = lax.broadcasted_iota(jnp.int32, (CELLS, wide), 1) < wide // 2
    for p in range(len(pieces) // 2):
        first, second = (piece.reshape(CELLS, wide) for piece in pieces[2 * p : 2 * p + 2])
        left_ref[:, p * wide : (p + 1) * wide] = jnp.where(low_half, first, second).astype(BF16)


def inner_kernel(own_ref, line_ref, enc_ref, near_ref, far_ref, out_ref, taps_ref, left_ref):
    features, channels = enc_ref.shape
    west, own, east = (doubled(line_ref[slot].astype(F32)) for slot in LON_SLOTS)
    store_pairs([*along_lon(west, own, east), west, own, east], left_ref)
    left_ref[:, 6 * features :] = own_ref[...]
    encode(INNER_TAPS, enc_ref, near_ref, far_ref, taps_ref)
    for t in (6, 7):
        taps_ref[t * features : (t + 1) * features] = enc_ref[...]
    for c in range(channels // BLOCK):
        cols = slice(c * BLOCK, (c + 1) * BLOCK)
        out_ref[:, cols] = jnp.dot(left_ref[...], taps_ref[:, cols], preferred_element_type=F32)


def ready_kernel(out_ref):
    out_ref[...] = jnp.zeros(out_ref.shape, F32)


def sums_kernel(_, count_ref, rows_ref, cells_ref, sent_ref, own_ref):
    slots = rows_ref.shape[1]
    slot = lax.broadcasted_iota(jnp.int32, (1, slots), 1)
    cell = lax.broadcasted_iota(jnp.int32, (CELLS, slots), 0)
    target = jnp.where(slot < count_ref[0, 0], cells_ref[...], -1)
    onehot = jnp.where(cell == target, 1.0, 0.0).astype(BF16)
    sums = lax.dot_general(
        onehot, rows_ref[...], (((1,), (1,)), ((), ())), preferred_element_type=F32
    )
    high = sums.astype(BF16).astype(F32)
    sent_ref[...] = jnp.concatenate([high[: CELLS // 2], high[CELLS // 2 :]], axis=1).astype(BF16)
    own_ref[...] = jnp.concatenate([high, sums - high], axis=1).astype(BF16)


def mix_kernel(line_ref, odd_ref, even_ref, taps_ref, inner_ref, mix_ref, out_ref, *scratch):
    left_ref, activ_ref, total_ref, state_ref, sems = scratch
    wide = line_ref.shape[2]
    row = lax.broadcasted_iota(jnp.int32, (SECTOR_LON_CELLS, BAND_LAT_CELLS, wide), 1)
    band = lax.axis_index("lat")
    even = lax.rem(band, 2) == 0
    has_before, has_after = band > 0, band < lax.axis_size("lat") - 1
    befores, afters, downs, ups = [], [], [], []
    for slot in LON_SLOTS:
        from_even, from_odd = even_ref[slot].astype(F32), odd_ref[slot].astype(F32)
        before = doubled(jnp.where(has_before, jnp.where(even, from_odd, from_even), 0.0))
        own = doubled(line_ref[slot].astype(F32))
        after = doubled(jnp.where(has_after, jnp.where(even, from_even, from_odd), 0.0))
        befores.append(before)
        afters.append(after)
        downs.append(jnp.where(row == 0, pltpu.roll(before, 1, 1), pltpu.roll(own, 1, 1)))
        last = BAND_LAT_CELLS - 1
        ups.append(jnp.where(row == last, pltpu.roll(after, last, 1), pltpu.roll(own, last, 1)))
    store_pairs([*along_lon(*downs), *along_lon(*ups), *befores, *afters], left_ref)
    channels = mix_ref.shape[0]
    chunks = [slice(c * BLOCK, (c + 1) * BLOCK) for c in range(channels // BLOCK)]
    for cols in chunks:
        total = inner_ref[:, cols] + jnp.dot(left_ref[...], taps_ref[:, cols], preferred_element_type=F32)
        activ_ref[:, cols] = jax.nn.gelu(total, approximate=True).astype(BF16)
        total_ref[:, cols] = total
    copies = []
    for c, cols in enumerate(chunks):
        mixed = jnp.dot(activ_ref[...], mix_ref[:, cols], preferred_element_type=F32)
        state_ref[:, cols] = (total_ref[:, cols] + mixed).astype(BF16)
        copies.append(pltpu.make_async_copy(state_ref.at[:, cols], out_ref.at[:, cols], sems.at[c]))
        copies[-1].start()
    for copy in copies:
        copy.wait()


def from_neighbour(value, axis, step):
    count = lax.axis_size(axis)
    return lax.ppermute(value, axis, [((i + step) % count, i) for i in range(count)])


def swapped(value, axis, first):
    count = lax.axis_size(axis)
    pairs = [(i, (i + 1 if i % 2 == first else i - 1) % count) for i in range(count)]
    return lax.ppermute(value, axis, pairs)


def on_device(
    obs_rows, obs_cells, obs_counts, enc_weight, near_kernel_weight, far_kernel_weight, mix_weight
):
    slots, features = obs_rows.shape[2:]
    channels = mix_weight.shape[0]
    params = pltpu.CompilerParams(vmem_limit_bytes=24 << 20)
    in_vmem = pl.BlockSpec(memory_space=pltpu.VMEM)
    early = pl.pallas_call(
        ready_kernel,
        out_shape=pltpu.VMEM((8, 128), F32),
        cost_estimate=pl.CostEstimate(flops=4_000_000_000, bytes_accessed=12_000_000, transcendentals=0),
        compiler_params=params,
        name="ready",
    )()
    count, early = lax.optimization_barrier((obs_counts, early))
    sent, own = pl.pallas_call(
        sums_kernel,
        out_shape=(pltpu.VMEM((CELLS // 2, 2 * features), BF16), pltpu.VMEM((CELLS, 2 * features), BF16)),
        in_specs=[in_vmem, pl.BlockSpec(memory_space=pltpu.SMEM), in_vmem, in_vmem],
        cost_estimate=pl.CostEstimate(flops=4_000_000_000, bytes_accessed=12_000_000, transcendentals=0),
        compiler_params=params,
        name="cell_sums",
    )(early, count, obs_rows.reshape(slots, features).T, obs_cells.reshape(1, slots))
    weights = (enc_weight, near_kernel_weight, far_kernel_weight)
    taps = pl.pallas_call(
        taps_kernel,
        out_shape=pltpu.VMEM((len(OUTER_TAPS) * features, channels), BF16),
        cost_estimate=pl.CostEstimate(flops=1_600_000_000, bytes_accessed=2_500_000, transcendentals=0),
        compiler_params=params,
        name="outer_taps",
    )(*weights)
    line = jnp.stack([sent, from_neighbour(sent, "lon", 1), from_neighbour(sent, "lon", -1)])
    line, taps = lax.optimization_barrier((line, taps))
    inner = pl.pallas_call(
        inner_kernel,
        out_shape=pltpu.VMEM((CELLS, channels), F32),
        scratch_shapes=[pltpu.VMEM((8 * features, channels), BF16), pltpu.VMEM((CELLS, 8 * features), BF16)],
        cost_estimate=pl.CostEstimate(flops=1_000_000_000, bytes_accessed=2_500_000, transcendentals=0),
        compiler_params=params,
        name="inner_taps",
    )(own, line, *weights)
    mixed = pl.pallas_call(
        mix_kernel,
        out_shape=jax.ShapeDtypeStruct((CELLS, channels), BF16),
        in_specs=[in_vmem] * 6,
        out_specs=pl.BlockSpec(memory_space=pltpu.HBM),
        scratch_shapes=[
            pltpu.VMEM((CELLS, len(OUTER_TAPS) * features), BF16),
            pltpu.VMEM((CELLS, channels), BF16),
            pltpu.VMEM((CELLS, channels), F32),
            pltpu.VMEM((CELLS, channels), BF16),
            pltpu.SemaphoreType.DMA((channels // BLOCK,)),
        ],
        compiler_params=params,
        name="filter_and_mix",
    )(line, swapped(line, "lat", 1), swapped(line, "lat", 0), taps, inner, mix_weight)
    return mixed.reshape(SECTOR_LON_CELLS, BAND_LAT_CELLS, channels)


def solution(mesh):
    return jax.shard_map(
        on_device,
        mesh=mesh,
        in_specs=(
            P("lon", "lat", None, None),
            P("lon", "lat", None),
            P("lon", "lat"),
            P(),
            P(),
            P(),
            P(),
        ),
        out_specs=P("lon", "lat", None),
        check_vma=False,
    )
```

```python
import jax
import jax.numpy as jnp
from jax import lax
from jax.experimental import pallas as pl
from jax.experimental.pallas import tpu as pltpu
from jax.sharding import PartitionSpec as P

BAND_LAT_CELLS = 8
SECTOR_LON_CELLS = 8
CELLS = BAND_LAT_CELLS * SECTOR_LON_CELLS
BLOCK = 256
INNER_TAPS = [(far, a, 1) for far in (0, 1) for a in range(3)]
OUTER_TAPS = [(far, a, b) for b in (0, 2) for far in (0, 1) for a in range(3)]
LON_SLOTS = (1, 0, 2)
F32, BF16 = jnp.float32, jnp.bfloat16


def encode(taps, enc_ref, near_ref, far_ref, out_ref):
    features, channels = enc_ref.shape
    width = near_ref.shape[2]
    lane = lax.broadcasted_iota(jnp.int32, (width, BLOCK), 1) // width
    for t, (far, a, b) in enumerate(taps):
        for c in range(channels // BLOCK):
            cols = slice(c * BLOCK, (c + 1) * BLOCK)
            tap = (far_ref if far else near_ref)[a, b, :, cols]
            dense = jnp.concatenate(
                [jnp.where(lane == g, tap, jnp.zeros((), BF16)) for g in range(BLOCK // width)], axis=0
            )
            out_ref[t * features : (t + 1) * features, cols] = jnp.dot(
                enc_ref[:, cols], dense, preferred_element_type=F32
            ).astype(BF16)


def taps_kernel(enc_ref, near_ref, far_ref, out_ref):
    encode(OUTER_TAPS, enc_ref, near_ref, far_ref, out_ref)


def doubled(block):
    rows, wide = block.shape
    packed = (SECTOR_LON_CELLS // 2, BAND_LAT_CELLS, wide)
    half = lax.broadcasted_iota(jnp.int32, packed, 2) < wide // 2
    turned = pltpu.roll(block, wide // 2, 1).reshape(packed)
    block = block.reshape(packed)
    return jnp.concatenate([jnp.where(half, block, turned), jnp.where(half, turned, block)], axis=0)


def along_lon(west, own, east):
    return (
        jnp.concatenate([west[-1:], own[:-1]], axis=0),
        own,
        jnp.concatenate([own[1:], east[:1]], axis=0),
    )


def store_pairs(pieces, left_ref):
    wide = pieces[0].shape[-1]
    low_half = lax.broadcasted_iota(jnp.int32, (CELLS, wide), 1) < wide // 2
    for p in range(len(pieces) // 2):
        first, second = (piece.reshape(CELLS, wide) for piece in pieces[2 * p : 2 * p + 2])
        left_ref[:, p * wide : (p + 1) * wide] = jnp.where(low_half, first, second).astype(BF16)


def inner_kernel(own_ref, line_ref, enc_ref, near_ref, far_ref, mix_ref, out_ref, taps_ref, left_ref):
    del mix_ref
    features, channels = enc_ref.shape
    west, own, east = (doubled(line_ref[slot].astype(F32)) for slot in LON_SLOTS)
    store_pairs([*along_lon(west, own, east), west, own, east], left_ref)
    left_ref[:, 6 * features :] = own_ref[...]
    encode(INNER_TAPS, enc_ref, near_ref, far_ref, taps_ref)
    for t in (6, 7):
        taps_ref[t * features : (t + 1) * features] = enc_ref[...]
    for c in range(channels // BLOCK):
        cols = slice(c * BLOCK, (c + 1) * BLOCK)
        out_ref[:, cols] = jnp.dot(left_ref[...], taps_ref[:, cols], preferred_element_type=F32)


def ready_kernel(out_ref):
    out_ref[...] = jnp.zeros(out_ref.shape, F32)


def sums_kernel(_, count_ref, rows_ref, cells_ref, sent_ref, own_ref):
    slots = rows_ref.shape[1]
    slot = lax.broadcasted_iota(jnp.int32, (1, slots), 1)
    cell = lax.broadcasted_iota(jnp.int32, (CELLS, slots), 0)
    target = jnp.where(slot < count_ref[0, 0], cells_ref[...], -1)
    onehot = jnp.where(cell == target, 1.0, 0.0).astype(BF16)
    sums = lax.dot_general(
        onehot, rows_ref[...], (((1,), (1,)), ((), ())), preferred_element_type=F32
    )
    high = sums.astype(BF16).astype(F32)
    sent_ref[...] = jnp.concatenate([high[: CELLS // 2], high[CELLS // 2 :]], axis=1).astype(BF16)
    own_ref[...] = jnp.concatenate([high, sums - high], axis=1).astype(BF16)


def other_band(line_ref, other_ref, taps_ref, left_ref, is_before, inside):
    wide = line_ref.shape[2]
    row = lax.broadcasted_iota(jnp.int32, (SECTOR_LON_CELLS, BAND_LAT_CELLS, wide), 1)
    last = BAND_LAT_CELLS - 1
    others, steps = [], []
    for slot in LON_SLOTS:
        own = doubled(line_ref[slot].astype(F32))
        other = doubled(jnp.where(inside, other_ref[slot].astype(F32), 0.0))
        down = jnp.where(row == 0, pltpu.roll(other, 1, 1), pltpu.roll(own, 1, 1))
        up = jnp.where(row == last, pltpu.roll(other, last, 1), pltpu.roll(own, last, 1))
        others.append(other)
        steps.append(jnp.where(is_before, down, up))
    store_pairs([*along_lon(*steps), *others], left_ref)
    depth = taps_ref.shape[0] // 2
    rows = pl.ds(pl.multiple_of(jnp.where(is_before, 0, depth), depth), depth)
    for c in range(taps_ref.shape[1] // BLOCK):
        cols = slice(c * BLOCK, (c + 1) * BLOCK)
        yield cols, jnp.dot(left_ref[...], taps_ref[rows, cols], preferred_element_type=F32)


def is_even():
    return lax.rem(lax.axis_index("lat"), 2) == 0


def pair_kernel(line_ref, other_ref, taps_ref, inner_ref, out_ref, left_ref):
    for cols, added in other_band(line_ref, other_ref, taps_ref, left_ref, jnp.logical_not(is_even()), True):
        out_ref[:, cols] = inner_ref[:, cols] + added


def mix_kernel(line_ref, other_ref, taps_ref, inner_ref, mix_ref, out_ref, *scratch):
    left_ref, activ_ref, total_ref, state_ref, sems = scratch
    band = lax.axis_index("lat")
    inside = (band > 0) & (band < lax.axis_size("lat") - 1)
    for cols, added in other_band(line_ref, other_ref, taps_ref, left_ref, is_even(), inside):
        total = inner_ref[:, cols] + added
        activ_ref[:, cols] = jax.nn.gelu(total, approximate=True).astype(BF16)
        total_ref[:, cols] = total
    copies = []
    for c in range(mix_ref.shape[1] // BLOCK):
        cols = slice(c * BLOCK, (c + 1) * BLOCK)
        mixed = jnp.dot(activ_ref[...], mix_ref[:, cols], preferred_element_type=F32)
        state_ref[:, cols] = (total_ref[:, cols] + mixed).astype(BF16)
        copies.append(pltpu.make_async_copy(state_ref.at[:, cols], out_ref.at[:, cols], sems.at[c]))
        copies[-1].start()
    for copy in copies:
        copy.wait()


def from_neighbour(value, axis, step):
    count = lax.axis_size(axis)
    return lax.ppermute(value, axis, [((i + step) % count, i) for i in range(count)])


def swapped(value, axis, first):
    count = lax.axis_size(axis)
    pairs = [(i, (i + 1 if i % 2 == first else i - 1) % count) for i in range(count)]
    return lax.ppermute(value, axis, pairs)


def on_device(
    obs_rows, obs_cells, obs_counts, enc_weight, near_kernel_weight, far_kernel_weight, mix_weight
):
    slots, features = obs_rows.shape[2:]
    channels = mix_weight.shape[0]
    params = pltpu.CompilerParams(vmem_limit_bytes=24 << 20)
    in_vmem = pl.BlockSpec(memory_space=pltpu.VMEM)
    early = pl.pallas_call(
        ready_kernel,
        out_shape=pltpu.VMEM((8, 128), F32),
        cost_estimate=pl.CostEstimate(flops=4_000_000_000, bytes_accessed=12_000_000, transcendentals=0),
        compiler_params=params,
        name="ready",
    )()
    count, early = lax.optimization_barrier((obs_counts, early))
    sent, own = pl.pallas_call(
        sums_kernel,
        out_shape=(pltpu.VMEM((CELLS // 2, 2 * features), BF16), pltpu.VMEM((CELLS, 2 * features), BF16)),
        in_specs=[in_vmem, pl.BlockSpec(memory_space=pltpu.SMEM), in_vmem, in_vmem],
        cost_estimate=pl.CostEstimate(flops=4_000_000_000, bytes_accessed=12_000_000, transcendentals=0),
        compiler_params=params,
        name="cell_sums",
    )(early, count, obs_rows.reshape(slots, features).T, obs_cells.reshape(1, slots))
    weights = (enc_weight, near_kernel_weight, far_kernel_weight)
    taps = pl.pallas_call(
        taps_kernel,
        out_shape=pltpu.VMEM((len(OUTER_TAPS) * features, channels), BF16),
        cost_estimate=pl.CostEstimate(flops=1_600_000_000, bytes_accessed=2_500_000, transcendentals=0),
        compiler_params=params,
        name="outer_taps",
    )(*weights)
    line = jnp.stack([sent, from_neighbour(sent, "lon", -1), from_neighbour(sent, "lon", 1)])
    line, taps = lax.optimization_barrier((line, taps))
    inner = pl.pallas_call(
        inner_kernel,
        out_shape=pltpu.VMEM((CELLS, channels), F32),
        scratch_shapes=[pltpu.VMEM((8 * features, channels), BF16), pltpu.VMEM((CELLS, 8 * features), BF16)],
        cost_estimate=pl.CostEstimate(flops=1_000_000_000, bytes_accessed=2_500_000, transcendentals=0),
        compiler_params=params,
        name="inner_taps",
    )(own, line, *weights, mix_weight)
    left = pltpu.VMEM((CELLS, len(INNER_TAPS) * features), BF16)
    paired = pl.pallas_call(
        pair_kernel,
        out_shape=pltpu.VMEM((CELLS, channels), F32),
        scratch_shapes=[left],
        cost_estimate=pl.CostEstimate(flops=1_000_000, bytes_accessed=10_000, transcendentals=0),
        compiler_params=params,
        name="pair_taps",
    )(line, swapped(line, "lat", 0), taps, inner)
    mixed = pl.pallas_call(
        mix_kernel,
        out_shape=jax.ShapeDtypeStruct((CELLS, channels), BF16),
        in_specs=[in_vmem] * 5,
        out_specs=pl.BlockSpec(memory_space=pltpu.HBM),
        scratch_shapes=[
            left,
            pltpu.VMEM((CELLS, channels), BF16),
            pltpu.VMEM((CELLS, channels), F32),
            pltpu.VMEM((CELLS, channels), BF16),
            pltpu.SemaphoreType.DMA((channels // BLOCK,)),
        ],
        compiler_params=params,
        name="filter_and_mix",
    )(line, swapped(line, "lat", 1), taps, paired, mix_weight)
    return mixed.reshape(SECTOR_LON_CELLS, BAND_LAT_CELLS, channels)


def solution(mesh):
    return jax.shard_map(
        on_device,
        mesh=mesh,
        in_specs=(
            P("lon", "lat", None, None),
            P("lon", "lat", None),
            P("lon", "lat"),
            P(),
            P(),
            P(),
            P(),
        ),
        out_specs=P("lon", "lat", None),
        check_vma=False,
    )
```

```python
import jax
import jax.numpy as jnp
from jax import lax
from jax.experimental import pallas as pl
from jax.experimental.pallas import tpu as pltpu
from jax.sharding import PartitionSpec as P

BAND_LAT_CELLS = 8
SECTOR_LON_CELLS = 8
CELLS = BAND_LAT_CELLS * SECTOR_LON_CELLS
BLOCK = 256
INNER_TAPS = [(far, a, 1) for far in (0, 1) for a in range(3)]
OUTER_TAPS = [(far, a, b) for b in (0, 2) for far in (0, 1) for a in range(3)]
LON_SLOTS = (1, 0, 2)
F32, BF16 = jnp.float32, jnp.bfloat16


def encode(taps, enc_ref, near_ref, far_ref, out_ref):
    features, channels = enc_ref.shape
    width = near_ref.shape[2]
    lane = lax.broadcasted_iota(jnp.int32, (width, BLOCK), 1) // width
    for t, (far, a, b) in enumerate(taps):
        for c in range(channels // BLOCK):
            cols = slice(c * BLOCK, (c + 1) * BLOCK)
            tap = (far_ref if far else near_ref)[a, b, :, cols]
            dense = jnp.concatenate(
                [jnp.where(lane == g, tap, jnp.zeros((), BF16)) for g in range(BLOCK // width)], axis=0
            )
            out_ref[t * features : (t + 1) * features, cols] = jnp.dot(
                enc_ref[:, cols], dense, preferred_element_type=F32
            ).astype(BF16)


def taps_kernel(enc_ref, near_ref, far_ref, out_ref):
    encode(OUTER_TAPS, enc_ref, near_ref, far_ref, out_ref)


def doubled(block):
    rows, wide = block.shape
    packed = (SECTOR_LON_CELLS // 2, BAND_LAT_CELLS, wide)
    half = lax.broadcasted_iota(jnp.int32, packed, 2) < wide // 2
    turned = pltpu.roll(block, wide // 2, 1).reshape(packed)
    block = block.reshape(packed)
    return jnp.concatenate([jnp.where(half, block, turned), jnp.where(half, turned, block)], axis=0)


def along_lon(west, own, east):
    return (
        jnp.concatenate([west[-1:], own[:-1]], axis=0),
        own,
        jnp.concatenate([own[1:], east[:1]], axis=0),
    )


def store_pairs(pieces, left_ref):
    wide = pieces[0].shape[-1]
    low_half = lax.broadcasted_iota(jnp.int32, (CELLS, wide), 1) < wide // 2
    for p in range(len(pieces) // 2):
        first, second = (piece.reshape(CELLS, wide) for piece in pieces[2 * p : 2 * p + 2])
        left_ref[:, p * wide : (p + 1) * wide] = jnp.where(low_half, first, second).astype(BF16)


def inner_kernel(own_ref, line_ref, enc_ref, near_ref, far_ref, mix_ref, out_ref, taps_ref, left_ref):
    del mix_ref
    features, channels = enc_ref.shape
    west, own, east = (doubled(line_ref[slot].astype(F32)) for slot in LON_SLOTS)
    store_pairs([*along_lon(west, own, east), west, own, east], left_ref)
    left_ref[:, 6 * features :] = own_ref[...]
    encode(INNER_TAPS, enc_ref, near_ref, far_ref, taps_ref)
    for t in (6, 7):
        taps_ref[t * features : (t + 1) * features] = enc_ref[...]
    for c in range(channels // BLOCK):
        cols = slice(c * BLOCK, (c + 1) * BLOCK)
        out_ref[:, cols] = jnp.dot(left_ref[...], taps_ref[:, cols], preferred_element_type=F32)


def ready_kernel(out_ref):
    out_ref[...] = jnp.zeros(out_ref.shape, F32)


def sums_kernel(_, count_ref, rows_ref, cells_ref, sent_ref, own_ref):
    slots = rows_ref.shape[1]
    slot = lax.broadcasted_iota(jnp.int32, (1, slots), 1)
    cell = lax.broadcasted_iota(jnp.int32, (CELLS, slots), 0)
    target = jnp.where(slot < count_ref[0, 0], cells_ref[...], -1)
    onehot = jnp.where(cell == target, 1.0, 0.0).astype(BF16)
    sums = lax.dot_general(
        onehot, rows_ref[...], (((1,), (1,)), ((), ())), preferred_element_type=F32
    )
    high = sums.astype(BF16).astype(F32)
    sent_ref[...] = jnp.concatenate([high[: CELLS // 2], high[CELLS // 2 :]], axis=1).astype(BF16)
    own_ref[...] = jnp.concatenate([high, sums - high], axis=1).astype(BF16)


def other_band(line_ref, other_ref, taps_ref, left_ref, is_before, inside):
    wide = line_ref.shape[2]
    row = lax.broadcasted_iota(jnp.int32, (SECTOR_LON_CELLS, BAND_LAT_CELLS, wide), 1)
    last = BAND_LAT_CELLS - 1
    others, steps = [], []
    for slot in LON_SLOTS:
        own = doubled(line_ref[slot].astype(F32))
        other = doubled(jnp.where(inside, other_ref[slot].astype(F32), 0.0))
        down = jnp.where(row == 0, pltpu.roll(other, 1, 1), pltpu.roll(own, 1, 1))
        up = jnp.where(row == last, pltpu.roll(other, last, 1), pltpu.roll(own, last, 1))
        others.append(other)
        steps.append(jnp.where(is_before, down, up))
    store_pairs([*along_lon(*steps), *others], left_ref)
    depth = taps_ref.shape[0] // 2
    rows = pl.ds(pl.multiple_of(jnp.where(is_before, 0, depth), depth), depth)
    for c in range(taps_ref.shape[1] // BLOCK):
        cols = slice(c * BLOCK, (c + 1) * BLOCK)
        yield cols, jnp.dot(left_ref[...], taps_ref[rows, cols], preferred_element_type=F32)


def is_even():
    return lax.rem(lax.axis_index("lat"), 2) == 0


def pair_kernel(line_ref, other_ref, taps_ref, inner_ref, out_ref, left_ref):
    for cols, added in other_band(line_ref, other_ref, taps_ref, left_ref, jnp.logical_not(is_even()), True):
        out_ref[:, cols] = inner_ref[:, cols] + added


def mix_kernel(line_ref, other_ref, taps_ref, inner_ref, mix_ref, out_ref, *scratch):
    left_ref, activ_ref, total_ref, state_ref, sems = scratch
    band = lax.axis_index("lat")
    inside = (band > 0) & (band < lax.axis_size("lat") - 1)
    for cols, added in other_band(line_ref, other_ref, taps_ref, left_ref, is_even(), inside):
        total = inner_ref[:, cols] + added
        activ_ref[:, cols] = jax.nn.gelu(total, approximate=True).astype(BF16)
        total_ref[:, cols] = total
    copies = []
    for c in range(mix_ref.shape[1] // BLOCK):
        cols = slice(c * BLOCK, (c + 1) * BLOCK)
        mixed = jnp.dot(activ_ref[...], mix_ref[:, cols], preferred_element_type=F32)
        state_ref[:, cols] = (total_ref[:, cols] + mixed).astype(BF16)
        copies.append(pltpu.make_async_copy(state_ref.at[:, cols], out_ref.at[:, cols], sems.at[c]))
        copies[-1].start()
    for copy in copies:
        copy.wait()


def from_neighbour(value, axis, step):
    count = lax.axis_size(axis)
    return lax.ppermute(value, axis, [((i + step) % count, i) for i in range(count)])


def lat_swapped(value, first):
    sectors, bands = lax.axis_size("lon"), lax.axis_size("lat")
    step = 2 if sectors % 4 == 0 else 1
    pairs = []
    for lon in range(sectors):
        for lat in range(bands):
            partner = lat + 1 if lat % 2 == first else lat - 1
            inside = 0 <= partner < bands
            other = lon if inside else lon ^ step
            pairs.append((lon * bands + lat, other * bands + (partner if inside else lat)))
    return lax.ppermute(value, ("lon", "lat"), pairs)


def on_device(
    obs_rows, obs_cells, obs_counts, enc_weight, near_kernel_weight, far_kernel_weight, mix_weight
):
    slots, features = obs_rows.shape[2:]
    channels = mix_weight.shape[0]
    params = pltpu.CompilerParams(vmem_limit_bytes=24 << 20)
    in_vmem = pl.BlockSpec(memory_space=pltpu.VMEM)
    early = pl.pallas_call(
        ready_kernel,
        out_shape=pltpu.VMEM((8, 128), F32),
        cost_estimate=pl.CostEstimate(flops=4_000_000_000, bytes_accessed=12_000_000, transcendentals=0),
        compiler_params=params,
        name="ready",
    )()
    count, early = lax.optimization_barrier((obs_counts, early))
    sent, own = pl.pallas_call(
        sums_kernel,
        out_shape=(pltpu.VMEM((CELLS // 2, 2 * features), BF16), pltpu.VMEM((CELLS, 2 * features), BF16)),
        in_specs=[in_vmem, pl.BlockSpec(memory_space=pltpu.SMEM), in_vmem, in_vmem],
        cost_estimate=pl.CostEstimate(flops=4_000_000_000, bytes_accessed=12_000_000, transcendentals=0),
        compiler_params=params,
        name="cell_sums",
    )(early, count, obs_rows.reshape(slots, features).T, obs_cells.reshape(1, slots))
    weights = (enc_weight, near_kernel_weight, far_kernel_weight)
    taps = pl.pallas_call(
        taps_kernel,
        out_shape=pltpu.VMEM((len(OUTER_TAPS) * features, channels), BF16),
        cost_estimate=pl.CostEstimate(flops=1_600_000_000, bytes_accessed=2_500_000, transcendentals=0),
        compiler_params=params,
        name="outer_taps",
    )(*weights)
    line = jnp.stack([sent, from_neighbour(sent, "lon", -1), from_neighbour(sent, "lon", 1)])
    line, taps = lax.optimization_barrier((line, taps))
    inner = pl.pallas_call(
        inner_kernel,
        out_shape=pltpu.VMEM((CELLS, channels), F32),
        scratch_shapes=[pltpu.VMEM((8 * features, channels), BF16), pltpu.VMEM((CELLS, 8 * features), BF16)],
        cost_estimate=pl.CostEstimate(flops=1_000_000_000, bytes_accessed=2_500_000, transcendentals=0),
        compiler_params=params,
        name="inner_taps",
    )(own, line, *weights, mix_weight)
    left = pltpu.VMEM((CELLS, len(INNER_TAPS) * features), BF16)
    paired = pl.pallas_call(
        pair_kernel,
        out_shape=pltpu.VMEM((CELLS, channels), F32),
        scratch_shapes=[left],
        cost_estimate=pl.CostEstimate(flops=1_000_000, bytes_accessed=10_000, transcendentals=0),
        compiler_params=params,
        name="pair_taps",
    )(line, lat_swapped(line, 0), taps, inner)
    mixed = pl.pallas_call(
        mix_kernel,
        out_shape=jax.ShapeDtypeStruct((CELLS, channels), BF16),
        in_specs=[in_vmem] * 5,
        out_specs=pl.BlockSpec(memory_space=pltpu.HBM),
        scratch_shapes=[
            left,
            pltpu.VMEM((CELLS, channels), BF16),
            pltpu.VMEM((CELLS, channels), F32),
            pltpu.VMEM((CELLS, channels), BF16),
            pltpu.SemaphoreType.DMA((channels // BLOCK,)),
        ],
        compiler_params=params,
        name="filter_and_mix",
    )(line, lat_swapped(line, 1), taps, paired, mix_weight)
    return mixed.reshape(SECTOR_LON_CELLS, BAND_LAT_CELLS, channels)


def solution(mesh):
    return jax.shard_map(
        on_device,
        mesh=mesh,
        in_specs=(
            P("lon", "lat", None, None),
            P("lon", "lat", None),
            P("lon", "lat"),
            P(),
            P(),
            P(),
            P(),
        ),
        out_specs=P("lon", "lat", None),
        check_vma=False,
    )
```

```python
import jax
import jax.numpy as jnp
from jax import lax
from jax.experimental import pallas as pl
from jax.experimental.pallas import tpu as pltpu
from jax.sharding import PartitionSpec as P

BAND_LAT_CELLS = 8
SECTOR_LON_CELLS = 8
CELLS = BAND_LAT_CELLS * SECTOR_LON_CELLS
BLOCK = 256
INNER_TAPS = [(far, a, 1) for far in (0, 1) for a in range(3)]
OUTER_TAPS = [(far, a, b) for b in (0, 2) for far in (0, 1) for a in range(3)]
LON_SLOTS = (1, 0, 2)
F32, BF16 = jnp.float32, jnp.bfloat16


def encode(taps, enc_ref, near_ref, far_ref, out_ref):
    features, channels = enc_ref.shape
    width = near_ref.shape[2]
    lane = lax.broadcasted_iota(jnp.int32, (width, BLOCK), 1) // width
    for t, (far, a, b) in enumerate(taps):
        for c in range(channels // BLOCK):
            cols = slice(c * BLOCK, (c + 1) * BLOCK)
            tap = (far_ref if far else near_ref)[a, b, :, cols]
            dense = jnp.concatenate(
                [jnp.where(lane == g, tap, jnp.zeros((), BF16)) for g in range(BLOCK // width)], axis=0
            )
            out_ref[t * features : (t + 1) * features, cols] = jnp.dot(
                enc_ref[:, cols], dense, preferred_element_type=F32
            ).astype(BF16)


def taps_kernel(enc_ref, near_ref, far_ref, out_ref):
    encode(OUTER_TAPS, enc_ref, near_ref, far_ref, out_ref)


def doubled(block):
    rows, wide = block.shape
    packed = (SECTOR_LON_CELLS // 2, BAND_LAT_CELLS, wide)
    half = lax.broadcasted_iota(jnp.int32, packed, 2) < wide // 2
    turned = pltpu.roll(block, wide // 2, 1).reshape(packed)
    block = block.reshape(packed)
    return jnp.concatenate([jnp.where(half, block, turned), jnp.where(half, turned, block)], axis=0)


def along_lon(west, own, east):
    return (
        jnp.concatenate([west[-1:], own[:-1]], axis=0),
        own,
        jnp.concatenate([own[1:], east[:1]], axis=0),
    )


def store_pairs(pieces, left_ref):
    wide = pieces[0].shape[-1]
    low_half = lax.broadcasted_iota(jnp.int32, (CELLS, wide), 1) < wide // 2
    for p in range(len(pieces) // 2):
        first, second = (piece.reshape(CELLS, wide) for piece in pieces[2 * p : 2 * p + 2])
        left_ref[:, p * wide : (p + 1) * wide] = jnp.where(low_half, first, second).astype(BF16)


def inner_kernel(own_ref, line_ref, enc_ref, near_ref, far_ref, mix_ref, out_ref, taps_ref, left_ref):
    del mix_ref
    features, channels = enc_ref.shape
    west, own, east = (doubled(line_ref[slot].astype(F32)) for slot in LON_SLOTS)
    store_pairs([*along_lon(west, own, east), west, own, east], left_ref)
    left_ref[:, 6 * features :] = own_ref[...]
    encode(INNER_TAPS, enc_ref, near_ref, far_ref, taps_ref)
    for t in (6, 7):
        taps_ref[t * features : (t + 1) * features] = enc_ref[...]
    for c in range(channels // BLOCK):
        cols = slice(c * BLOCK, (c + 1) * BLOCK)
        out_ref[:, cols] = jnp.dot(left_ref[...], taps_ref[:, cols], preferred_element_type=F32)


def ready_kernel(out_ref):
    out_ref[...] = jnp.zeros(out_ref.shape, F32)


def sums_kernel(_, count_ref, rows_ref, cells_ref, sent_ref, own_ref):
    slots = rows_ref.shape[1]
    slot = lax.broadcasted_iota(jnp.int32, (1, slots), 1)
    cell = lax.broadcasted_iota(jnp.int32, (CELLS, slots), 0)
    target = jnp.where(slot < count_ref[0, 0], cells_ref[...], -1)
    onehot = jnp.where(cell == target, 1.0, 0.0).astype(BF16)
    sums = lax.dot_general(
        onehot, rows_ref[...], (((1,), (1,)), ((), ())), preferred_element_type=F32
    )
    high = sums.astype(BF16).astype(F32)
    sent_ref[...] = jnp.concatenate([high[: CELLS // 2], high[CELLS // 2 :]], axis=1).astype(BF16)
    own_ref[...] = jnp.concatenate([high, sums - high], axis=1).astype(BF16)


def stepped(block, is_before):
    return jnp.where(is_before, pltpu.roll(block, 1, 1), pltpu.roll(block, BAND_LAT_CELLS - 1, 1))


def other_band(own_steps, other_ref, taps_ref, left_ref, is_before, inside):
    row = lax.broadcasted_iota(jnp.int32, own_steps[0].shape, 1)
    edge = row == jnp.where(is_before, 0, BAND_LAT_CELLS - 1)
    others = [doubled(jnp.where(inside, other_ref[slot].astype(F32), 0.0)) for slot in LON_SLOTS]
    steps = [jnp.where(edge, stepped(other, is_before), own) for other, own in zip(others, own_steps)]
    store_pairs([*along_lon(*steps), *others], left_ref)
    depth = taps_ref.shape[0] // 2
    rows = pl.ds(pl.multiple_of(jnp.where(is_before, 0, depth), depth), depth)
    for c in range(taps_ref.shape[1] // BLOCK):
        cols = slice(c * BLOCK, (c + 1) * BLOCK)
        yield cols, jnp.dot(left_ref[...], taps_ref[rows, cols], preferred_element_type=F32)


def is_even():
    return lax.rem(lax.axis_index("lat"), 2) == 0


def pair_kernel(line_ref, other_ref, taps_ref, inner_ref, out_ref, steps_ref, left_ref):
    even = is_even()
    own = [doubled(line_ref[slot].astype(F32)) for slot in LON_SLOTS]
    for i, block in enumerate(own):
        steps_ref[i] = stepped(block, even)
    first = jnp.logical_not(even)
    own_steps = [stepped(block, first) for block in own]
    for cols, added in other_band(own_steps, other_ref, taps_ref, left_ref, first, True):
        out_ref[:, cols] = inner_ref[:, cols] + added


def mix_kernel(steps_ref, other_ref, taps_ref, inner_ref, mix_ref, out_ref, *scratch):
    left_ref, activ_ref, total_ref, state_ref, sems = scratch
    band = lax.axis_index("lat")
    inside = (band > 0) & (band < lax.axis_size("lat") - 1)
    own_steps = [steps_ref[i] for i in range(3)]
    for cols, added in other_band(own_steps, other_ref, taps_ref, left_ref, is_even(), inside):
        total = inner_ref[:, cols] + added
        activ_ref[:, cols] = jax.nn.gelu(total, approximate=True).astype(BF16)
        total_ref[:, cols] = total
    copies = []
    for c in range(mix_ref.shape[1] // BLOCK):
        cols = slice(c * BLOCK, (c + 1) * BLOCK)
        mixed = jnp.dot(activ_ref[...], mix_ref[:, cols], preferred_element_type=F32)
        state_ref[:, cols] = (total_ref[:, cols] + mixed).astype(BF16)
        copies.append(pltpu.make_async_copy(state_ref.at[:, cols], out_ref.at[:, cols], sems.at[c]))
        copies[-1].start()
    for copy in copies:
        copy.wait()


def from_neighbour(value, axis, step):
    count = lax.axis_size(axis)
    return lax.ppermute(value, axis, [((i + step) % count, i) for i in range(count)])


def swapped(value, axis, first):
    count = lax.axis_size(axis)
    pairs = [(i, (i + 1 if i % 2 == first else i - 1) % count) for i in range(count)]
    return lax.ppermute(value, axis, pairs)


def on_device(
    obs_rows, obs_cells, obs_counts, enc_weight, near_kernel_weight, far_kernel_weight, mix_weight
):
    slots, features = obs_rows.shape[2:]
    channels = mix_weight.shape[0]
    params = pltpu.CompilerParams(vmem_limit_bytes=24 << 20)
    in_vmem = pl.BlockSpec(memory_space=pltpu.VMEM)
    early = pl.pallas_call(
        ready_kernel,
        out_shape=pltpu.VMEM((8, 128), F32),
        cost_estimate=pl.CostEstimate(flops=4_000_000_000, bytes_accessed=12_000_000, transcendentals=0),
        compiler_params=params,
        name="ready",
    )()
    count, early = lax.optimization_barrier((obs_counts, early))
    sent, own = pl.pallas_call(
        sums_kernel,
        out_shape=(pltpu.VMEM((CELLS // 2, 2 * features), BF16), pltpu.VMEM((CELLS, 2 * features), BF16)),
        in_specs=[in_vmem, pl.BlockSpec(memory_space=pltpu.SMEM), in_vmem, in_vmem],
        cost_estimate=pl.CostEstimate(flops=4_000_000_000, bytes_accessed=12_000_000, transcendentals=0),
        compiler_params=params,
        name="cell_sums",
    )(early, count, obs_rows.reshape(slots, features).T, obs_cells.reshape(1, slots))
    weights = (enc_weight, near_kernel_weight, far_kernel_weight)
    taps = pl.pallas_call(
        taps_kernel,
        out_shape=pltpu.VMEM((len(OUTER_TAPS) * features, channels), BF16),
        cost_estimate=pl.CostEstimate(flops=1_600_000_000, bytes_accessed=2_500_000, transcendentals=0),
        compiler_params=params,
        name="outer_taps",
    )(*weights)
    line = jnp.stack([sent, from_neighbour(sent, "lon", -1), from_neighbour(sent, "lon", 1)])
    line, taps = lax.optimization_barrier((line, taps))
    inner = pl.pallas_call(
        inner_kernel,
        out_shape=pltpu.VMEM((CELLS, channels), F32),
        scratch_shapes=[pltpu.VMEM((8 * features, channels), BF16), pltpu.VMEM((CELLS, 8 * features), BF16)],
        cost_estimate=pl.CostEstimate(flops=1_000_000_000, bytes_accessed=2_500_000, transcendentals=0),
        compiler_params=params,
        name="inner_taps",
    )(own, line, *weights, mix_weight)
    left = pltpu.VMEM((CELLS, len(INNER_TAPS) * features), BF16)
    paired, steps = pl.pallas_call(
        pair_kernel,
        out_shape=(
            pltpu.VMEM((CELLS, channels), F32),
            pltpu.VMEM((3, SECTOR_LON_CELLS, BAND_LAT_CELLS, 2 * features), F32),
        ),
        scratch_shapes=[left],
        cost_estimate=pl.CostEstimate(flops=1_000_000, bytes_accessed=10_000, transcendentals=0),
        compiler_params=params,
        name="pair_taps",
    )(line, swapped(line, "lat", 0), taps, inner)
    mixed = pl.pallas_call(
        mix_kernel,
        out_shape=jax.ShapeDtypeStruct((CELLS, channels), BF16),
        in_specs=[in_vmem] * 5,
        out_specs=pl.BlockSpec(memory_space=pltpu.HBM),
        scratch_shapes=[
            left,
            pltpu.VMEM((CELLS, channels), BF16),
            pltpu.VMEM((CELLS, channels), F32),
            pltpu.VMEM((CELLS, channels), BF16),
            pltpu.SemaphoreType.DMA((channels // BLOCK,)),
        ],
        compiler_params=params,
        name="filter_and_mix",
    )(steps, swapped(line, "lat", 1), taps, paired, mix_weight)
    return mixed.reshape(SECTOR_LON_CELLS, BAND_LAT_CELLS, channels)


def solution(mesh):
    return jax.shard_map(
        on_device,
        mesh=mesh,
        in_specs=(
            P("lon", "lat", None, None),
            P("lon", "lat", None),
            P("lon", "lat"),
            P(),
            P(),
            P(),
            P(),
        ),
        out_specs=P("lon", "lat", None),
        check_vma=False,
    )
```

```python
import jax
import jax.numpy as jnp
from jax import lax
from jax.experimental import pallas as pl
from jax.experimental.pallas import tpu as pltpu
from jax.sharding import PartitionSpec as P

BAND_LAT_CELLS = 8
SECTOR_LON_CELLS = 8
CELLS = BAND_LAT_CELLS * SECTOR_LON_CELLS
BLOCK = 256
INNER_TAPS = [(far, a, 1) for far in (0, 1) for a in range(3)]
OUTER_TAPS = [(far, a, b) for b in (0, 2) for far in (0, 1) for a in range(3)]
LON_SLOTS = (1, 0, 2)
F32, BF16 = jnp.float32, jnp.bfloat16


def encode(taps, enc_ref, near_ref, far_ref, out_ref):
    features, channels = enc_ref.shape
    width = near_ref.shape[2]
    lane = lax.broadcasted_iota(jnp.int32, (width, BLOCK), 1) // width
    for t, (far, a, b) in enumerate(taps):
        for c in range(channels // BLOCK):
            cols = slice(c * BLOCK, (c + 1) * BLOCK)
            tap = (far_ref if far else near_ref)[a, b, :, cols]
            dense = jnp.concatenate(
                [jnp.where(lane == g, tap, jnp.zeros((), BF16)) for g in range(BLOCK // width)], axis=0
            )
            out_ref[t * features : (t + 1) * features, cols] = jnp.dot(
                enc_ref[:, cols], dense, preferred_element_type=F32
            ).astype(BF16)


def taps_kernel(enc_ref, near_ref, far_ref, out_ref):
    encode(OUTER_TAPS, enc_ref, near_ref, far_ref, out_ref)


def doubled(block):
    rows, wide = block.shape
    packed = (SECTOR_LON_CELLS // 2, BAND_LAT_CELLS, wide)
    half = lax.broadcasted_iota(jnp.int32, packed, 2) < wide // 2
    turned = pltpu.roll(block, wide // 2, 1).reshape(packed)
    block = block.reshape(packed)
    return jnp.concatenate([jnp.where(half, block, turned), jnp.where(half, turned, block)], axis=0)


def along_lon(west, own, east):
    return (
        jnp.concatenate([west[-1:], own[:-1]], axis=0),
        own,
        jnp.concatenate([own[1:], east[:1]], axis=0),
    )


def store_pairs(pieces, left_ref):
    wide = pieces[0].shape[-1]
    low_half = lax.broadcasted_iota(jnp.int32, (CELLS, wide), 1) < wide // 2
    for p in range(len(pieces) // 2):
        first, second = (piece.reshape(CELLS, wide) for piece in pieces[2 * p : 2 * p + 2])
        left_ref[:, p * wide : (p + 1) * wide] = jnp.where(low_half, first, second).astype(BF16)


def inner_kernel(own_ref, line_ref, enc_ref, near_ref, far_ref, mix_ref, out_ref, taps_ref, left_ref):
    del mix_ref
    features, channels = enc_ref.shape
    west, own, east = (doubled(line_ref[slot].astype(F32)) for slot in LON_SLOTS)
    store_pairs([*along_lon(west, own, east), west, own, east], left_ref)
    left_ref[:, 6 * features :] = own_ref[...]
    encode(INNER_TAPS, enc_ref, near_ref, far_ref, taps_ref)
    for t in (6, 7):
        taps_ref[t * features : (t + 1) * features] = enc_ref[...]
    for c in range(channels // BLOCK):
        cols = slice(c * BLOCK, (c + 1) * BLOCK)
        out_ref[:, cols] = jnp.dot(left_ref[...], taps_ref[:, cols], preferred_element_type=F32)


def ready_kernel(out_ref):
    out_ref[...] = jnp.zeros(out_ref.shape, F32)


def mask_kernel(_, count_ref, cells_ref, out_ref):
    slots = cells_ref.shape[1]
    slot = lax.broadcasted_iota(jnp.int32, (1, slots), 1)
    cell = lax.broadcasted_iota(jnp.int32, (CELLS, slots), 0)
    target = jnp.where(slot < count_ref[0, 0], cells_ref[...], -1)
    out_ref[...] = jnp.where(cell == target, 1.0, 0.0).astype(BF16)


def sums_kernel(mask_ref, rows_ref, sent_ref, own_ref):
    sums = lax.dot_general(
        mask_ref[...], rows_ref[...], (((1,), (1,)), ((), ())), preferred_element_type=F32
    )
    high = sums.astype(BF16).astype(F32)
    sent_ref[...] = jnp.concatenate([high[: CELLS // 2], high[CELLS // 2 :]], axis=1).astype(BF16)
    own_ref[...] = jnp.concatenate([high, sums - high], axis=1).astype(BF16)


def other_band(line_ref, other_ref, taps_ref, left_ref, is_before, inside):
    wide = line_ref.shape[2]
    row = lax.broadcasted_iota(jnp.int32, (SECTOR_LON_CELLS, BAND_LAT_CELLS, wide), 1)
    last = BAND_LAT_CELLS - 1
    others, steps = [], []
    for slot in LON_SLOTS:
        own = doubled(line_ref[slot].astype(F32))
        other = doubled(jnp.where(inside, other_ref[slot].astype(F32), 0.0))
        down = jnp.where(row == 0, pltpu.roll(other, 1, 1), pltpu.roll(own, 1, 1))
        up = jnp.where(row == last, pltpu.roll(other, last, 1), pltpu.roll(own, last, 1))
        others.append(other)
        steps.append(jnp.where(is_before, down, up))
    store_pairs([*along_lon(*steps), *others], left_ref)
    depth = taps_ref.shape[0] // 2
    rows = pl.ds(pl.multiple_of(jnp.where(is_before, 0, depth), depth), depth)
    for c in range(taps_ref.shape[1] // BLOCK):
        cols = slice(c * BLOCK, (c + 1) * BLOCK)
        yield cols, jnp.dot(left_ref[...], taps_ref[rows, cols], preferred_element_type=F32)


def is_even():
    return lax.rem(lax.axis_index("lat"), 2) == 0


def pair_kernel(line_ref, other_ref, taps_ref, inner_ref, out_ref, left_ref):
    for cols, added in other_band(line_ref, other_ref, taps_ref, left_ref, jnp.logical_not(is_even()), True):
        out_ref[:, cols] = inner_ref[:, cols] + added


def mix_kernel(line_ref, other_ref, taps_ref, inner_ref, mix_ref, out_ref, *scratch):
    left_ref, activ_ref, total_ref, state_ref, sems = scratch
    band = lax.axis_index("lat")
    inside = (band > 0) & (band < lax.axis_size("lat") - 1)
    for cols, added in other_band(line_ref, other_ref, taps_ref, left_ref, is_even(), inside):
        total = inner_ref[:, cols] + added
        activ_ref[:, cols] = jax.nn.gelu(total, approximate=True).astype(BF16)
        total_ref[:, cols] = total
    copies = []
    for c in range(mix_ref.shape[1] // BLOCK):
        cols = slice(c * BLOCK, (c + 1) * BLOCK)
        mixed = jnp.dot(activ_ref[...], mix_ref[:, cols], preferred_element_type=F32)
        state_ref[:, cols] = (total_ref[:, cols] + mixed).astype(BF16)
        copies.append(pltpu.make_async_copy(state_ref.at[:, cols], out_ref.at[:, cols], sems.at[c]))
        copies[-1].start()
    for copy in copies:
        copy.wait()


def from_neighbour(value, axis, step):
    count = lax.axis_size(axis)
    return lax.ppermute(value, axis, [((i + step) % count, i) for i in range(count)])


def swapped(value, axis, first):
    count = lax.axis_size(axis)
    pairs = [(i, (i + 1 if i % 2 == first else i - 1) % count) for i in range(count)]
    return lax.ppermute(value, axis, pairs)


def on_device(
    obs_rows, obs_cells, obs_counts, enc_weight, near_kernel_weight, far_kernel_weight, mix_weight
):
    slots, features = obs_rows.shape[2:]
    channels = mix_weight.shape[0]
    params = pltpu.CompilerParams(vmem_limit_bytes=24 << 20)
    in_vmem = pl.BlockSpec(memory_space=pltpu.VMEM)
    early = pl.pallas_call(
        ready_kernel,
        out_shape=pltpu.VMEM((8, 128), F32),
        cost_estimate=pl.CostEstimate(flops=4_000_000_000, bytes_accessed=12_000_000, transcendentals=0),
        compiler_params=params,
        name="ready",
    )()
    count, early = lax.optimization_barrier((obs_counts, early))
    mask = pl.pallas_call(
        mask_kernel,
        out_shape=pltpu.VMEM((CELLS, slots), BF16),
        in_specs=[in_vmem, pl.BlockSpec(memory_space=pltpu.SMEM), in_vmem],
        compiler_params=params,
        name="cell_mask",
    )(early, count, obs_cells.reshape(1, slots))
    sent, own = pl.pallas_call(
        sums_kernel,
        out_shape=(pltpu.VMEM((CELLS // 2, 2 * features), BF16), pltpu.VMEM((CELLS, 2 * features), BF16)),
        in_specs=[in_vmem] * 2,
        cost_estimate=pl.CostEstimate(flops=4_000_000_000, bytes_accessed=12_000_000, transcendentals=0),
        compiler_params=params,
        name="cell_sums",
    )(mask, obs_rows.reshape(slots, features).T)
    weights = (enc_weight, near_kernel_weight, far_kernel_weight)
    taps = pl.pallas_call(
        taps_kernel,
        out_shape=pltpu.VMEM((len(OUTER_TAPS) * features, channels), BF16),
        cost_estimate=pl.CostEstimate(flops=1_600_000_000, bytes_accessed=2_500_000, transcendentals=0),
        compiler_params=params,
        name="outer_taps",
    )(*weights)
    line = jnp.stack([sent, from_neighbour(sent, "lon", -1), from_neighbour(sent, "lon", 1)])
    line, taps = lax.optimization_barrier((line, taps))
    inner = pl.pallas_call(
        inner_kernel,
        out_shape=pltpu.VMEM((CELLS, channels), F32),
        scratch_shapes=[pltpu.VMEM((8 * features, channels), BF16), pltpu.VMEM((CELLS, 8 * features), BF16)],
        cost_estimate=pl.CostEstimate(flops=1_000_000_000, bytes_accessed=2_500_000, transcendentals=0),
        compiler_params=params,
        name="inner_taps",
    )(own, line, *weights, mix_weight)
    left = pltpu.VMEM((CELLS, len(INNER_TAPS) * features), BF16)
    paired = pl.pallas_call(
        pair_kernel,
        out_shape=pltpu.VMEM((CELLS, channels), F32),
        scratch_shapes=[left],
        cost_estimate=pl.CostEstimate(flops=1_000_000, bytes_accessed=10_000, transcendentals=0),
        compiler_params=params,
        name="pair_taps",
    )(line, swapped(line, "lat", 0), taps, inner)
    mixed = pl.pallas_call(
        mix_kernel,
        out_shape=jax.ShapeDtypeStruct((CELLS, channels), BF16),
        in_specs=[in_vmem] * 5,
        out_specs=pl.BlockSpec(memory_space=pltpu.HBM),
        scratch_shapes=[
            left,
            pltpu.VMEM((CELLS, channels), BF16),
            pltpu.VMEM((CELLS, channels), F32),
            pltpu.VMEM((CELLS, channels), BF16),
            pltpu.SemaphoreType.DMA((channels // BLOCK,)),
        ],
        compiler_params=params,
        name="filter_and_mix",
    )(line, swapped(line, "lat", 1), taps, paired, mix_weight)
    return mixed.reshape(SECTOR_LON_CELLS, BAND_LAT_CELLS, channels)


def solution(mesh):
    return jax.shard_map(
        on_device,
        mesh=mesh,
        in_specs=(
            P("lon", "lat", None, None),
            P("lon", "lat", None),
            P("lon", "lat"),
            P(),
            P(),
            P(),
            P(),
        ),
        out_specs=P("lon", "lat", None),
        check_vma=False,
    )
```

```python
import jax
import jax.numpy as jnp
from jax import lax
from jax.experimental import pallas as pl
from jax.experimental.pallas import tpu as pltpu
from jax.sharding import PartitionSpec as P

BAND_LAT_CELLS = 8
SECTOR_LON_CELLS = 8
CELLS = BAND_LAT_CELLS * SECTOR_LON_CELLS
BLOCK = 256
INNER_TAPS = [(far, a, 1) for far in (0, 1) for a in range(3)]
OUTER_TAPS = [(far, a, b) for b in (0, 2) for far in (0, 1) for a in range(3)]
LON_SLOTS = (1, 0, 2)
F32, BF16 = jnp.float32, jnp.bfloat16


def encode(taps, enc_ref, near_ref, far_ref, out_ref):
    features, channels = enc_ref.shape
    width = near_ref.shape[2]
    lane = lax.broadcasted_iota(jnp.int32, (width, BLOCK), 1) // width
    for t, (far, a, b) in enumerate(taps):
        for c in range(channels // BLOCK):
            cols = slice(c * BLOCK, (c + 1) * BLOCK)
            tap = (far_ref if far else near_ref)[a, b, :, cols]
            dense = jnp.concatenate(
                [jnp.where(lane == g, tap, jnp.zeros((), BF16)) for g in range(BLOCK // width)], axis=0
            )
            out_ref[t * features : (t + 1) * features, cols] = jnp.dot(
                enc_ref[:, cols], dense, preferred_element_type=F32
            ).astype(BF16)


def taps_kernel(enc_ref, near_ref, far_ref, out_ref):
    encode(OUTER_TAPS, enc_ref, near_ref, far_ref, out_ref)


def doubled(block):
    rows, wide = block.shape
    packed = (SECTOR_LON_CELLS // 2, BAND_LAT_CELLS, wide)
    half = lax.broadcasted_iota(jnp.int32, packed, 2) < wide // 2
    turned = pltpu.roll(block, wide // 2, 1).reshape(packed)
    block = block.reshape(packed)
    return jnp.concatenate([jnp.where(half, block, turned), jnp.where(half, turned, block)], axis=0)


def along_lon(west, own, east):
    return (
        jnp.concatenate([west[-1:], own[:-1]], axis=0),
        own,
        jnp.concatenate([own[1:], east[:1]], axis=0),
    )


def store_pairs(pieces, left_ref):
    wide = pieces[0].shape[-1]
    low_half = lax.broadcasted_iota(jnp.int32, (CELLS, wide), 1) < wide // 2
    for p in range(len(pieces) // 2):
        first, second = (piece.reshape(CELLS, wide) for piece in pieces[2 * p : 2 * p + 2])
        left_ref[:, p * wide : (p + 1) * wide] = jnp.where(low_half, first, second).astype(BF16)


def inner_kernel(own_ref, line_ref, enc_ref, near_ref, far_ref, mix_ref, out_ref, taps_ref, left_ref):
    del mix_ref
    features, channels = enc_ref.shape
    west, own, east = (doubled(line_ref[slot].astype(F32)) for slot in LON_SLOTS)
    store_pairs([*along_lon(west, own, east), west, own, east], left_ref)
    left_ref[:, 6 * features :] = own_ref[...]
    encode(INNER_TAPS, enc_ref, near_ref, far_ref, taps_ref)
    for t in (6, 7):
        taps_ref[t * features : (t + 1) * features] = enc_ref[...]
    for c in range(channels // BLOCK):
        cols = slice(c * BLOCK, (c + 1) * BLOCK)
        out_ref[:, cols] = jnp.dot(left_ref[...], taps_ref[:, cols], preferred_element_type=F32)


def ready_kernel(out_ref):
    out_ref[...] = jnp.zeros(out_ref.shape, F32)


def mask_kernel(_, count_ref, cells_ref, out_ref):
    slots = cells_ref.shape[1]
    slot = lax.broadcasted_iota(jnp.int32, (1, slots), 1)
    cell = lax.broadcasted_iota(jnp.int32, (CELLS, slots), 0)
    target = jnp.where(slot < count_ref[0, 0], cells_ref[...], -1)
    out_ref[...] = jnp.where(cell == target, 1.0, 0.0).T.astype(BF16)


def sums_kernel(mask_ref, rows_ref, sent_ref, own_ref):
    sums = jnp.dot(rows_ref[...], mask_ref[...], preferred_element_type=F32).T
    high = sums.astype(BF16).astype(F32)
    sent_ref[...] = jnp.concatenate([high[: CELLS // 2], high[CELLS // 2 :]], axis=1).astype(BF16)
    own_ref[...] = jnp.concatenate([high, sums - high], axis=1).astype(BF16)


def other_band(line_ref, other_ref, taps_ref, left_ref, is_before, inside):
    wide = line_ref.shape[2]
    row = lax.broadcasted_iota(jnp.int32, (SECTOR_LON_CELLS, BAND_LAT_CELLS, wide), 1)
    last = BAND_LAT_CELLS - 1
    others, steps = [], []
    for slot in LON_SLOTS:
        own = doubled(line_ref[slot].astype(F32))
        other = doubled(jnp.where(inside, other_ref[slot].astype(F32), 0.0))
        down = jnp.where(row == 0, pltpu.roll(other, 1, 1), pltpu.roll(own, 1, 1))
        up = jnp.where(row == last, pltpu.roll(other, last, 1), pltpu.roll(own, last, 1))
        others.append(other)
        steps.append(jnp.where(is_before, down, up))
    store_pairs([*along_lon(*steps), *others], left_ref)
    depth = taps_ref.shape[0] // 2
    rows = pl.ds(pl.multiple_of(jnp.where(is_before, 0, depth), depth), depth)
    for c in range(taps_ref.shape[1] // BLOCK):
        cols = slice(c * BLOCK, (c + 1) * BLOCK)
        yield cols, jnp.dot(left_ref[...], taps_ref[rows, cols], preferred_element_type=F32)


def is_even():
    return lax.rem(lax.axis_index("lat"), 2) == 0


def pair_kernel(line_ref, other_ref, taps_ref, inner_ref, out_ref, left_ref):
    for cols, added in other_band(line_ref, other_ref, taps_ref, left_ref, jnp.logical_not(is_even()), True):
        out_ref[:, cols] = inner_ref[:, cols] + added


def mix_kernel(line_ref, other_ref, taps_ref, inner_ref, mix_ref, out_ref, *scratch):
    left_ref, activ_ref, total_ref, state_ref, sems = scratch
    band = lax.axis_index("lat")
    inside = (band > 0) & (band < lax.axis_size("lat") - 1)
    for cols, added in other_band(line_ref, other_ref, taps_ref, left_ref, is_even(), inside):
        total = inner_ref[:, cols] + added
        activ_ref[:, cols] = jax.nn.gelu(total, approximate=True).astype(BF16)
        total_ref[:, cols] = total
    copies = []
    for c in range(mix_ref.shape[1] // BLOCK):
        cols = slice(c * BLOCK, (c + 1) * BLOCK)
        mixed = jnp.dot(activ_ref[...], mix_ref[:, cols], preferred_element_type=F32)
        state_ref[:, cols] = (total_ref[:, cols] + mixed).astype(BF16)
        copies.append(pltpu.make_async_copy(state_ref.at[:, cols], out_ref.at[:, cols], sems.at[c]))
        copies[-1].start()
    for copy in copies:
        copy.wait()


def from_neighbour(value, axis, step):
    count = lax.axis_size(axis)
    return lax.ppermute(value, axis, [((i + step) % count, i) for i in range(count)])


def swapped(value, axis, first):
    count = lax.axis_size(axis)
    pairs = [(i, (i + 1 if i % 2 == first else i - 1) % count) for i in range(count)]
    return lax.ppermute(value, axis, pairs)


def on_device(
    obs_rows, obs_cells, obs_counts, enc_weight, near_kernel_weight, far_kernel_weight, mix_weight
):
    slots, features = obs_rows.shape[2:]
    channels = mix_weight.shape[0]
    params = pltpu.CompilerParams(vmem_limit_bytes=24 << 20)
    in_vmem = pl.BlockSpec(memory_space=pltpu.VMEM)
    early = pl.pallas_call(
        ready_kernel,
        out_shape=pltpu.VMEM((8, 128), F32),
        cost_estimate=pl.CostEstimate(flops=4_000_000_000, bytes_accessed=12_000_000, transcendentals=0),
        compiler_params=params,
        name="ready",
    )()
    count, early = lax.optimization_barrier((obs_counts, early))
    mask = pl.pallas_call(
        mask_kernel,
        out_shape=pltpu.VMEM((slots, CELLS), BF16),
        in_specs=[in_vmem, pl.BlockSpec(memory_space=pltpu.SMEM), in_vmem],
        compiler_params=params,
        name="cell_mask",
    )(early, count, obs_cells.reshape(1, slots))
    sent, own = pl.pallas_call(
        sums_kernel,
        out_shape=(pltpu.VMEM((CELLS // 2, 2 * features), BF16), pltpu.VMEM((CELLS, 2 * features), BF16)),
        in_specs=[in_vmem] * 2,
        cost_estimate=pl.CostEstimate(flops=4_000_000_000, bytes_accessed=12_000_000, transcendentals=0),
        compiler_params=params,
        name="cell_sums",
    )(mask, obs_rows.reshape(slots, features).T)
    weights = (enc_weight, near_kernel_weight, far_kernel_weight)
    taps = pl.pallas_call(
        taps_kernel,
        out_shape=pltpu.VMEM((len(OUTER_TAPS) * features, channels), BF16),
        cost_estimate=pl.CostEstimate(flops=1_600_000_000, bytes_accessed=2_500_000, transcendentals=0),
        compiler_params=params,
        name="outer_taps",
    )(*weights)
    line = jnp.stack([sent, from_neighbour(sent, "lon", -1), from_neighbour(sent, "lon", 1)])
    line, taps = lax.optimization_barrier((line, taps))
    inner = pl.pallas_call(
        inner_kernel,
        out_shape=pltpu.VMEM((CELLS, channels), F32),
        scratch_shapes=[pltpu.VMEM((8 * features, channels), BF16), pltpu.VMEM((CELLS, 8 * features), BF16)],
        cost_estimate=pl.CostEstimate(flops=1_000_000_000, bytes_accessed=2_500_000, transcendentals=0),
        compiler_params=params,
        name="inner_taps",
    )(own, line, *weights, mix_weight)
    left = pltpu.VMEM((CELLS, len(INNER_TAPS) * features), BF16)
    paired = pl.pallas_call(
        pair_kernel,
        out_shape=pltpu.VMEM((CELLS, channels), F32),
        scratch_shapes=[left],
        cost_estimate=pl.CostEstimate(flops=1_000_000, bytes_accessed=10_000, transcendentals=0),
        compiler_params=params,
        name="pair_taps",
    )(line, swapped(line, "lat", 0), taps, inner)
    mixed = pl.pallas_call(
        mix_kernel,
        out_shape=jax.ShapeDtypeStruct((CELLS, channels), BF16),
        in_specs=[in_vmem] * 5,
        out_specs=pl.BlockSpec(memory_space=pltpu.HBM),
        scratch_shapes=[
            left,
            pltpu.VMEM((CELLS, channels), BF16),
            pltpu.VMEM((CELLS, channels), F32),
            pltpu.VMEM((CELLS, channels), BF16),
            pltpu.SemaphoreType.DMA((channels // BLOCK,)),
        ],
        compiler_params=params,
        name="filter_and_mix",
    )(line, swapped(line, "lat", 1), taps, paired, mix_weight)
    return mixed.reshape(SECTOR_LON_CELLS, BAND_LAT_CELLS, channels)


def solution(mesh):
    return jax.shard_map(
        on_device,
        mesh=mesh,
        in_specs=(
            P("lon", "lat", None, None),
            P("lon", "lat", None),
            P("lon", "lat"),
            P(),
            P(),
            P(),
            P(),
        ),
        out_specs=P("lon", "lat", None),
        check_vma=False,
    )
```

```python
import jax
import jax.numpy as jnp
from jax import lax
from jax.experimental import pallas as pl
from jax.experimental.pallas import tpu as pltpu
from jax.sharding import PartitionSpec as P

BAND_LAT_CELLS = 8
SECTOR_LON_CELLS = 8
CELLS = BAND_LAT_CELLS * SECTOR_LON_CELLS
BLOCK = 256
INNER_TAPS = [(far, a, 1) for far in (0, 1) for a in range(3)]
OUTER_TAPS = [(far, a, b) for b in (0, 2) for far in (0, 1) for a in range(3)]
LON_SLOTS = (1, 0, 2)
F32, BF16 = jnp.float32, jnp.bfloat16


def encode(taps, enc_ref, near_ref, far_ref, out_ref):
    features, channels = enc_ref.shape
    width = near_ref.shape[2]
    lane = lax.broadcasted_iota(jnp.int32, (width, BLOCK), 1) // width
    for t, (far, a, b) in enumerate(taps):
        for c in range(channels // BLOCK):
            cols = slice(c * BLOCK, (c + 1) * BLOCK)
            tap = (far_ref if far else near_ref)[a, b, :, cols]
            dense = jnp.concatenate(
                [jnp.where(lane == g, tap, jnp.zeros((), BF16)) for g in range(BLOCK // width)], axis=0
            )
            out_ref[t * features : (t + 1) * features, cols] = jnp.dot(
                enc_ref[:, cols], dense, preferred_element_type=F32
            ).astype(BF16)


def taps_kernel(enc_ref, near_ref, far_ref, out_ref):
    encode(OUTER_TAPS, enc_ref, near_ref, far_ref, out_ref)


def doubled(block):
    rows, wide = block.shape
    packed = (SECTOR_LON_CELLS // 2, BAND_LAT_CELLS, wide)
    half = lax.broadcasted_iota(jnp.int32, packed, 2) < wide // 2
    turned = pltpu.roll(block, wide // 2, 1).reshape(packed)
    block = block.reshape(packed)
    return jnp.concatenate([jnp.where(half, block, turned), jnp.where(half, turned, block)], axis=0)


def along_lon(west, own, east):
    return (
        jnp.concatenate([west[-1:], own[:-1]], axis=0),
        own,
        jnp.concatenate([own[1:], east[:1]], axis=0),
    )


def store_pairs(pieces, left_ref):
    wide = pieces[0].shape[-1]
    low_half = lax.broadcasted_iota(jnp.int32, (CELLS, wide), 1) < wide // 2
    for p in range(len(pieces) // 2):
        first, second = (piece.reshape(CELLS, wide) for piece in pieces[2 * p : 2 * p + 2])
        left_ref[:, p * wide : (p + 1) * wide] = jnp.where(low_half, first, second).astype(BF16)


def inner_kernel(own_ref, line_ref, enc_ref, near_ref, far_ref, mix_ref, out_ref, taps_ref, left_ref):
    del mix_ref
    features, channels = enc_ref.shape
    west, own, east = (doubled(line_ref[slot].astype(F32)) for slot in LON_SLOTS)
    store_pairs([*along_lon(west, own, east), west, own, east], left_ref)
    left_ref[:, 6 * features :] = own_ref[...]
    encode(INNER_TAPS, enc_ref, near_ref, far_ref, taps_ref)
    for t in (6, 7):
        taps_ref[t * features : (t + 1) * features] = enc_ref[...]
    for c in range(channels // BLOCK):
        cols = slice(c * BLOCK, (c + 1) * BLOCK)
        out_ref[:, cols] = jnp.dot(left_ref[...], taps_ref[:, cols], preferred_element_type=F32)


def ready_kernel(out_ref):
    out_ref[...] = jnp.zeros(out_ref.shape, F32)


def mask_kernel(_, count_ref, cells_ref, out_ref):
    slots = cells_ref.shape[1]
    slot = lax.broadcasted_iota(jnp.int32, (1, slots), 1)
    cell = lax.broadcasted_iota(jnp.int32, (CELLS, slots), 0)
    target = jnp.where(slot < count_ref[0, 0], cells_ref[...], -1)
    out_ref[...] = jnp.where(cell == target, 1.0, 0.0).astype(BF16)


def sums_kernel(mask_ref, rows_ref, sent_ref, own_ref):
    part = rows_ref.shape[1] // 4
    one, two, three, four = (
        lax.dot_general(
            mask_ref[:, i * part : (i + 1) * part],
            rows_ref[:, i * part : (i + 1) * part],
            (((1,), (1,)), ((), ())),
            preferred_element_type=F32,
        )
        for i in range(4)
    )
    sums = (one + two) + (three + four)
    high = sums.astype(BF16).astype(F32)
    sent_ref[...] = jnp.concatenate([high[: CELLS // 2], high[CELLS // 2 :]], axis=1).astype(BF16)
    own_ref[...] = jnp.concatenate([high, sums - high], axis=1).astype(BF16)


def other_band(line_ref, other_ref, taps_ref, left_ref, is_before, inside):
    wide = line_ref.shape[2]
    row = lax.broadcasted_iota(jnp.int32, (SECTOR_LON_CELLS, BAND_LAT_CELLS, wide), 1)
    last = BAND_LAT_CELLS - 1
    others, steps = [], []
    for slot in LON_SLOTS:
        own = doubled(line_ref[slot].astype(F32))
        other = doubled(jnp.where(inside, other_ref[slot].astype(F32), 0.0))
        down = jnp.where(row == 0, pltpu.roll(other, 1, 1), pltpu.roll(own, 1, 1))
        up = jnp.where(row == last, pltpu.roll(other, last, 1), pltpu.roll(own, last, 1))
        others.append(other)
        steps.append(jnp.where(is_before, down, up))
    store_pairs([*along_lon(*steps), *others], left_ref)
    depth = taps_ref.shape[0] // 2
    rows = pl.ds(pl.multiple_of(jnp.where(is_before, 0, depth), depth), depth)
    for c in range(taps_ref.shape[1] // BLOCK):
        cols = slice(c * BLOCK, (c + 1) * BLOCK)
        yield cols, jnp.dot(left_ref[...], taps_ref[rows, cols], preferred_element_type=F32)


def is_even():
    return lax.rem(lax.axis_index("lat"), 2) == 0


def pair_kernel(line_ref, other_ref, taps_ref, inner_ref, out_ref, left_ref):
    for cols, added in other_band(line_ref, other_ref, taps_ref, left_ref, jnp.logical_not(is_even()), True):
        out_ref[:, cols] = inner_ref[:, cols] + added


def mix_kernel(line_ref, other_ref, taps_ref, inner_ref, mix_ref, out_ref, *scratch):
    left_ref, activ_ref, total_ref, state_ref, sems = scratch
    band = lax.axis_index("lat")
    inside = (band > 0) & (band < lax.axis_size("lat") - 1)
    for cols, added in other_band(line_ref, other_ref, taps_ref, left_ref, is_even(), inside):
        total = inner_ref[:, cols] + added
        activ_ref[:, cols] = jax.nn.gelu(total, approximate=True).astype(BF16)
        total_ref[:, cols] = total
    copies = []
    for c in range(mix_ref.shape[1] // BLOCK):
        cols = slice(c * BLOCK, (c + 1) * BLOCK)
        mixed = jnp.dot(activ_ref[...], mix_ref[:, cols], preferred_element_type=F32)
        state_ref[:, cols] = (total_ref[:, cols] + mixed).astype(BF16)
        copies.append(pltpu.make_async_copy(state_ref.at[:, cols], out_ref.at[:, cols], sems.at[c]))
        copies[-1].start()
    for copy in copies:
        copy.wait()


def from_neighbour(value, axis, step):
    count = lax.axis_size(axis)
    return lax.ppermute(value, axis, [((i + step) % count, i) for i in range(count)])


def swapped(value, axis, first):
    count = lax.axis_size(axis)
    pairs = [(i, (i + 1 if i % 2 == first else i - 1) % count) for i in range(count)]
    return lax.ppermute(value, axis, pairs)


def on_device(
    obs_rows, obs_cells, obs_counts, enc_weight, near_kernel_weight, far_kernel_weight, mix_weight
):
    slots, features = obs_rows.shape[2:]
    channels = mix_weight.shape[0]
    params = pltpu.CompilerParams(vmem_limit_bytes=24 << 20)
    in_vmem = pl.BlockSpec(memory_space=pltpu.VMEM)
    early = pl.pallas_call(
        ready_kernel,
        out_shape=pltpu.VMEM((8, 128), F32),
        cost_estimate=pl.CostEstimate(flops=4_000_000_000, bytes_accessed=12_000_000, transcendentals=0),
        compiler_params=params,
        name="ready",
    )()
    count, early = lax.optimization_barrier((obs_counts, early))
    mask = pl.pallas_call(
        mask_kernel,
        out_shape=pltpu.VMEM((CELLS, slots), BF16),
        in_specs=[in_vmem, pl.BlockSpec(memory_space=pltpu.SMEM), in_vmem],
        compiler_params=params,
        name="cell_mask",
    )(early, count, obs_cells.reshape(1, slots))
    sent, own = pl.pallas_call(
        sums_kernel,
        out_shape=(pltpu.VMEM((CELLS // 2, 2 * features), BF16), pltpu.VMEM((CELLS, 2 * features), BF16)),
        in_specs=[in_vmem] * 2,
        cost_estimate=pl.CostEstimate(flops=4_000_000_000, bytes_accessed=12_000_000, transcendentals=0),
        compiler_params=params,
        name="cell_sums",
    )(mask, obs_rows.reshape(slots, features).T)
    weights = (enc_weight, near_kernel_weight, far_kernel_weight)
    taps = pl.pallas_call(
        taps_kernel,
        out_shape=pltpu.VMEM((len(OUTER_TAPS) * features, channels), BF16),
        cost_estimate=pl.CostEstimate(flops=1_600_000_000, bytes_accessed=2_500_000, transcendentals=0),
        compiler_params=params,
        name="outer_taps",
    )(*weights)
    line = jnp.stack([sent, from_neighbour(sent, "lon", -1), from_neighbour(sent, "lon", 1)])
    line, taps = lax.optimization_barrier((line, taps))
    inner = pl.pallas_call(
        inner_kernel,
        out_shape=pltpu.VMEM((CELLS, channels), F32),
        scratch_shapes=[pltpu.VMEM((8 * features, channels), BF16), pltpu.VMEM((CELLS, 8 * features), BF16)],
        cost_estimate=pl.CostEstimate(flops=1_000_000_000, bytes_accessed=2_500_000, transcendentals=0),
        compiler_params=params,
        name="inner_taps",
    )(own, line, *weights, mix_weight)
    left = pltpu.VMEM((CELLS, len(INNER_TAPS) * features), BF16)
    paired = pl.pallas_call(
        pair_kernel,
        out_shape=pltpu.VMEM((CELLS, channels), F32),
        scratch_shapes=[left],
        cost_estimate=pl.CostEstimate(flops=1_000_000, bytes_accessed=10_000, transcendentals=0),
        compiler_params=params,
        name="pair_taps",
    )(line, swapped(line, "lat", 0), taps, inner)
    mixed = pl.pallas_call(
        mix_kernel,
        out_shape=jax.ShapeDtypeStruct((CELLS, channels), BF16),
        in_specs=[in_vmem] * 5,
        out_specs=pl.BlockSpec(memory_space=pltpu.HBM),
        scratch_shapes=[
            left,
            pltpu.VMEM((CELLS, channels), BF16),
            pltpu.VMEM((CELLS, channels), F32),
            pltpu.VMEM((CELLS, channels), BF16),
            pltpu.SemaphoreType.DMA((channels // BLOCK,)),
        ],
        compiler_params=params,
        name="filter_and_mix",
    )(line, swapped(line, "lat", 1), taps, paired, mix_weight)
    return mixed.reshape(SECTOR_LON_CELLS, BAND_LAT_CELLS, channels)


def solution(mesh):
    return jax.shard_map(
        on_device,
        mesh=mesh,
        in_specs=(
            P("lon", "lat", None, None),
            P("lon", "lat", None),
            P("lon", "lat"),
            P(),
            P(),
            P(),
            P(),
        ),
        out_specs=P("lon", "lat", None),
        check_vma=False,
    )
```

```python
import jax
import jax.numpy as jnp
from jax import lax
from jax.experimental import pallas as pl
from jax.experimental.pallas import tpu as pltpu
from jax.sharding import PartitionSpec as P

BAND_LAT_CELLS = 8
SECTOR_LON_CELLS = 8
CELLS = BAND_LAT_CELLS * SECTOR_LON_CELLS
BLOCK = 256
INNER_TAPS = [(far, a, 1) for far in (0, 1) for a in range(3)]
OUTER_TAPS = [(far, a, b) for b in (0, 2) for far in (0, 1) for a in range(3)]
LON_SLOTS = (1, 0, 2)
F32, BF16 = jnp.float32, jnp.bfloat16


def encode(taps, enc_ref, near_ref, far_ref, out_ref):
    features, channels = enc_ref.shape
    width = near_ref.shape[2]
    lane = lax.broadcasted_iota(jnp.int32, (width, BLOCK), 1) // width
    for t, (far, a, b) in enumerate(taps):
        for c in range(channels // BLOCK):
            cols = slice(c * BLOCK, (c + 1) * BLOCK)
            tap = (far_ref if far else near_ref)[a, b, :, cols]
            dense = jnp.concatenate(
                [jnp.where(lane == g, tap, jnp.zeros((), BF16)) for g in range(BLOCK // width)], axis=0
            )
            out_ref[t * features : (t + 1) * features, cols] = jnp.dot(
                enc_ref[:, cols], dense, preferred_element_type=F32
            ).astype(BF16)


def taps_kernel(enc_ref, near_ref, far_ref, out_ref):
    encode(OUTER_TAPS, enc_ref, near_ref, far_ref, out_ref)


def doubled(block):
    rows, wide = block.shape
    packed = (SECTOR_LON_CELLS // 2, BAND_LAT_CELLS, wide)
    half = lax.broadcasted_iota(jnp.int32, packed, 2) < wide // 2
    turned = pltpu.roll(block, wide // 2, 1).reshape(packed)
    block = block.reshape(packed)
    return jnp.concatenate([jnp.where(half, block, turned), jnp.where(half, turned, block)], axis=0)


def along_lon(west, own, east):
    return (
        jnp.concatenate([west[-1:], own[:-1]], axis=0),
        own,
        jnp.concatenate([own[1:], east[:1]], axis=0),
    )


def store_pairs(pieces, left_ref):
    wide = pieces[0].shape[-1]
    low_half = lax.broadcasted_iota(jnp.int32, (CELLS, wide), 1) < wide // 2
    for p in range(len(pieces) // 2):
        first, second = (piece.reshape(CELLS, wide) for piece in pieces[2 * p : 2 * p + 2])
        left_ref[:, p * wide : (p + 1) * wide] = jnp.where(low_half, first, second).astype(BF16)


def inner_kernel(own_ref, line_ref, enc_ref, near_ref, far_ref, mix_ref, out_ref, taps_ref, left_ref):
    del mix_ref
    features, channels = enc_ref.shape
    west, own, east = (doubled(line_ref[slot].astype(F32)) for slot in LON_SLOTS)
    store_pairs([*along_lon(west, own, east), west, own, east], left_ref)
    left_ref[:, 6 * features :] = own_ref[...]
    encode(INNER_TAPS, enc_ref, near_ref, far_ref, taps_ref)
    for t in (6, 7):
        taps_ref[t * features : (t + 1) * features] = enc_ref[...]
    for c in range(channels // BLOCK):
        cols = slice(c * BLOCK, (c + 1) * BLOCK)
        out_ref[:, cols] = jnp.dot(left_ref[...], taps_ref[:, cols], preferred_element_type=F32)


def ready_kernel(out_ref):
    out_ref[...] = jnp.zeros(out_ref.shape, F32)


def sums_kernel(_, count_ref, rows_ref, cells_ref, sent_ref, own_ref):
    slots = rows_ref.shape[1]
    slot = lax.broadcasted_iota(jnp.int32, (1, slots), 1)
    cell = lax.broadcasted_iota(jnp.int32, (CELLS, slots), 0)
    target = jnp.where(slot < count_ref[0, 0], cells_ref[...], -1)
    onehot = jnp.where(cell == target, 1.0, 0.0).astype(BF16)
    sums = lax.dot_general(
        onehot, rows_ref[...], (((1,), (1,)), ((), ())), preferred_element_type=F32
    )
    high = sums.astype(BF16).astype(F32)
    sent_ref[...] = jnp.concatenate([high[: CELLS // 2], high[CELLS // 2 :]], axis=1).astype(BF16)
    own_ref[...] = jnp.concatenate([high, sums - high], axis=1).astype(BF16)


def other_band(line_ref, other_ref, taps_ref, left_ref, is_before, inside):
    wide = line_ref.shape[2]
    row = lax.broadcasted_iota(jnp.int32, (SECTOR_LON_CELLS, BAND_LAT_CELLS, wide), 1)
    last = BAND_LAT_CELLS - 1
    others, steps = [], []
    for slot in LON_SLOTS:
        own = doubled(line_ref[slot].astype(F32))
        other = doubled(jnp.where(inside, other_ref[slot].astype(F32), 0.0))
        down = jnp.where(row == 0, pltpu.roll(other, 1, 1), pltpu.roll(own, 1, 1))
        up = jnp.where(row == last, pltpu.roll(other, last, 1), pltpu.roll(own, last, 1))
        others.append(other)
        steps.append(jnp.where(is_before, down, up))
    store_pairs([*along_lon(*steps), *others], left_ref)
    depth = taps_ref.shape[0] // 2
    rows = pl.ds(pl.multiple_of(jnp.where(is_before, 0, depth), depth), depth)
    for c in range(taps_ref.shape[1] // BLOCK):
        cols = slice(c * BLOCK, (c + 1) * BLOCK)
        yield cols, jnp.dot(left_ref[...], taps_ref[rows, cols], preferred_element_type=F32)


def is_even():
    return lax.rem(lax.axis_index("lat"), 2) == 0


def pair_kernel(line_ref, other_ref, taps_ref, inner_ref, out_ref, left_ref):
    for cols, added in other_band(line_ref, other_ref, taps_ref, left_ref, jnp.logical_not(is_even()), True):
        out_ref[:, cols] = inner_ref[:, cols] + added


def mix_kernel(line_ref, other_ref, taps_ref, inner_ref, mix_ref, out_ref, *scratch):
    left_ref, activ_ref, total_ref, state_ref, sems = scratch
    band = lax.axis_index("lat")
    inside = (band > 0) & (band < lax.axis_size("lat") - 1)
    for cols, added in other_band(line_ref, other_ref, taps_ref, left_ref, is_even(), inside):
        total = inner_ref[:, cols] + added
        activ_ref[:, cols] = jax.nn.gelu(total, approximate=True).astype(BF16)
        total_ref[:, cols] = total
    copies = []
    for c in range(mix_ref.shape[1] // BLOCK):
        cols = slice(c * BLOCK, (c + 1) * BLOCK)
        mixed = jnp.dot(activ_ref[...], mix_ref[:, cols], preferred_element_type=F32)
        state_ref[c] = (total_ref[:, cols] + mixed).astype(BF16)
        copies.append(pltpu.make_async_copy(state_ref.at[c], out_ref.at[:, cols], sems.at[c]))
        copies[-1].start()
    for copy in copies:
        copy.wait()


def from_neighbour(value, axis, step):
    count = lax.axis_size(axis)
    return lax.ppermute(value, axis, [((i + step) % count, i) for i in range(count)])


def swapped(value, axis, first):
    count = lax.axis_size(axis)
    pairs = [(i, (i + 1 if i % 2 == first else i - 1) % count) for i in range(count)]
    return lax.ppermute(value, axis, pairs)


def on_device(
    obs_rows, obs_cells, obs_counts, enc_weight, near_kernel_weight, far_kernel_weight, mix_weight
):
    slots, features = obs_rows.shape[2:]
    channels = mix_weight.shape[0]
    params = pltpu.CompilerParams(vmem_limit_bytes=24 << 20)
    in_vmem = pl.BlockSpec(memory_space=pltpu.VMEM)
    early = pl.pallas_call(
        ready_kernel,
        out_shape=pltpu.VMEM((8, 128), F32),
        cost_estimate=pl.CostEstimate(flops=4_000_000_000, bytes_accessed=12_000_000, transcendentals=0),
        compiler_params=params,
        name="ready",
    )()
    count, early = lax.optimization_barrier((obs_counts, early))
    sent, own = pl.pallas_call(
        sums_kernel,
        out_shape=(pltpu.VMEM((CELLS // 2, 2 * features), BF16), pltpu.VMEM((CELLS, 2 * features), BF16)),
        in_specs=[in_vmem, pl.BlockSpec(memory_space=pltpu.SMEM), in_vmem, in_vmem],
        cost_estimate=pl.CostEstimate(flops=4_000_000_000, bytes_accessed=12_000_000, transcendentals=0),
        compiler_params=params,
        name="cell_sums",
    )(early, count, obs_rows.reshape(slots, features).T, obs_cells.reshape(1, slots))
    weights = (enc_weight, near_kernel_weight, far_kernel_weight)
    taps = pl.pallas_call(
        taps_kernel,
        out_shape=pltpu.VMEM((len(OUTER_TAPS) * features, channels), BF16),
        cost_estimate=pl.CostEstimate(flops=1_600_000_000, bytes_accessed=2_500_000, transcendentals=0),
        compiler_params=params,
        name="outer_taps",
    )(*weights)
    line = jnp.stack([sent, from_neighbour(sent, "lon", -1), from_neighbour(sent, "lon", 1)])
    line, taps = lax.optimization_barrier((line, taps))
    inner = pl.pallas_call(
        inner_kernel,
        out_shape=pltpu.VMEM((CELLS, channels), F32),
        scratch_shapes=[pltpu.VMEM((8 * features, channels), BF16), pltpu.VMEM((CELLS, 8 * features), BF16)],
        cost_estimate=pl.CostEstimate(flops=1_000_000_000, bytes_accessed=2_500_000, transcendentals=0),
        compiler_params=params,
        name="inner_taps",
    )(own, line, *weights, mix_weight)
    left = pltpu.VMEM((CELLS, len(INNER_TAPS) * features), BF16)
    paired = pl.pallas_call(
        pair_kernel,
        out_shape=pltpu.VMEM((CELLS, channels), F32),
        scratch_shapes=[left],
        cost_estimate=pl.CostEstimate(flops=1_000_000, bytes_accessed=10_000, transcendentals=0),
        compiler_params=params,
        name="pair_taps",
    )(line, swapped(line, "lat", 0), taps, inner)
    mixed = pl.pallas_call(
        mix_kernel,
        out_shape=jax.ShapeDtypeStruct((CELLS, channels), BF16),
        in_specs=[in_vmem] * 5,
        out_specs=pl.BlockSpec(memory_space=pltpu.HBM),
        scratch_shapes=[
            left,
            pltpu.VMEM((CELLS, channels), BF16),
            pltpu.VMEM((CELLS, channels), F32),
            pltpu.VMEM((channels // BLOCK, CELLS, BLOCK), BF16),
            pltpu.SemaphoreType.DMA((channels // BLOCK,)),
        ],
        compiler_params=params,
        name="filter_and_mix",
    )(line, swapped(line, "lat", 1), taps, paired, mix_weight)
    return mixed.reshape(SECTOR_LON_CELLS, BAND_LAT_CELLS, channels)


def solution(mesh):
    return jax.shard_map(
        on_device,
        mesh=mesh,
        in_specs=(
            P("lon", "lat", None, None),
            P("lon", "lat", None),
            P("lon", "lat"),
            P(),
            P(),
            P(),
            P(),
        ),
        out_specs=P("lon", "lat", None),
        check_vma=False,
    )
```

```python
import jax
import jax.numpy as jnp
from jax import lax
from jax.experimental import pallas as pl
from jax.experimental.pallas import tpu as pltpu
from jax.sharding import PartitionSpec as P

BAND_LAT_CELLS = 8
SECTOR_LON_CELLS = 8
CELLS = BAND_LAT_CELLS * SECTOR_LON_CELLS
BLOCK = 256
INNER_TAPS = [(far, a, 1) for far in (0, 1) for a in range(3)]
OUTER_TAPS = [(far, a, b) for b in (0, 2) for far in (0, 1) for a in range(3)]
LON_SLOTS = (1, 0, 2)
F32, BF16 = jnp.float32, jnp.bfloat16


def encode(taps, enc_ref, near_ref, far_ref, out_ref):
    features, channels = enc_ref.shape
    width = near_ref.shape[2]
    lane = lax.broadcasted_iota(jnp.int32, (width, BLOCK), 1) // width
    for t, (far, a, b) in enumerate(taps):
        for c in range(channels // BLOCK):
            cols = slice(c * BLOCK, (c + 1) * BLOCK)
            tap = (far_ref if far else near_ref)[a, b, :, cols]
            dense = jnp.concatenate(
                [jnp.where(lane == g, tap, jnp.zeros((), BF16)) for g in range(BLOCK // width)], axis=0
            )
            out_ref[t * features : (t + 1) * features, cols] = jnp.dot(
                enc_ref[:, cols], dense, preferred_element_type=F32
            ).astype(BF16)


def taps_kernel(enc_ref, near_ref, far_ref, out_ref):
    encode(OUTER_TAPS, enc_ref, near_ref, far_ref, out_ref)


def doubled(block):
    rows, wide = block.shape
    packed = (SECTOR_LON_CELLS // 2, BAND_LAT_CELLS, wide)
    half = lax.broadcasted_iota(jnp.int32, packed, 2) < wide // 2
    turned = pltpu.roll(block, wide // 2, 1).reshape(packed)
    block = block.reshape(packed)
    return jnp.concatenate([jnp.where(half, block, turned), jnp.where(half, turned, block)], axis=0)


def along_lon(west, own, east):
    return (
        jnp.concatenate([west[-1:], own[:-1]], axis=0),
        own,
        jnp.concatenate([own[1:], east[:1]], axis=0),
    )


def store_pairs(pieces, left_ref):
    wide = pieces[0].shape[-1]
    low_half = lax.broadcasted_iota(jnp.int32, (CELLS, wide), 1) < wide // 2
    for p in range(len(pieces) // 2):
        first, second = (piece.reshape(CELLS, wide) for piece in pieces[2 * p : 2 * p + 2])
        left_ref[:, p * wide : (p + 1) * wide] = jnp.where(low_half, first, second).astype(BF16)


def inner_kernel(own_ref, line_ref, enc_ref, near_ref, far_ref, mix_ref, out_ref, taps_ref, left_ref):
    del mix_ref
    features, channels = enc_ref.shape
    west, own, east = (doubled(line_ref[slot].astype(F32)) for slot in LON_SLOTS)
    store_pairs([*along_lon(west, own, east), west, own, east], left_ref)
    left_ref[:, 6 * features :] = own_ref[...]
    encode(INNER_TAPS, enc_ref, near_ref, far_ref, taps_ref)
    for t in (6, 7):
        taps_ref[t * features : (t + 1) * features] = enc_ref[...]
    for c in range(channels // BLOCK):
        cols = slice(c * BLOCK, (c + 1) * BLOCK)
        out_ref[:, cols] = jnp.dot(left_ref[...], taps_ref[:, cols], preferred_element_type=F32)


def ready_kernel(out_ref):
    out_ref[...] = jnp.zeros(out_ref.shape, F32)


def sums_kernel(_, count_ref, rows_ref, cells_ref, sent_ref, own_ref):
    slots = rows_ref.shape[1]
    slot = lax.broadcasted_iota(jnp.int32, (1, slots), 1)
    cell = lax.broadcasted_iota(jnp.int32, (CELLS, slots), 0)
    target = jnp.where(slot < count_ref[0, 0], cells_ref[...], -1)
    onehot = jnp.where(cell == target, 1.0, 0.0).astype(BF16)
    sums = lax.dot_general(
        onehot, rows_ref[...], (((1,), (1,)), ((), ())), preferred_element_type=F32
    )
    high = sums.astype(BF16).astype(F32)
    sent_ref[...] = jnp.concatenate([high[: CELLS // 2], high[CELLS // 2 :]], axis=1).astype(BF16)
    own_ref[...] = jnp.concatenate([high, sums - high], axis=1).astype(BF16)


def other_band(line_ref, other_ref, taps_ref, left_ref, is_before, inside):
    wide = line_ref.shape[2]
    row = lax.broadcasted_iota(jnp.int32, (SECTOR_LON_CELLS, BAND_LAT_CELLS, wide), 1)
    last = BAND_LAT_CELLS - 1
    others, steps = [], []
    for slot in LON_SLOTS:
        own = doubled(line_ref[slot].astype(F32))
        other = doubled(jnp.where(inside, other_ref[slot].astype(F32), 0.0))
        down = jnp.where(row == 0, pltpu.roll(other, 1, 1), pltpu.roll(own, 1, 1))
        up = jnp.where(row == last, pltpu.roll(other, last, 1), pltpu.roll(own, last, 1))
        others.append(other)
        steps.append(jnp.where(is_before, down, up))
    store_pairs([*along_lon(*steps), *others], left_ref)
    depth = taps_ref.shape[0] // 2
    rows = pl.ds(pl.multiple_of(jnp.where(is_before, 0, depth), depth), depth)
    for c in range(taps_ref.shape[1] // (2 * BLOCK)):
        cols = slice(2 * c * BLOCK, 2 * (c + 1) * BLOCK)
        yield cols, jnp.dot(left_ref[...], taps_ref[rows, cols], preferred_element_type=F32)


def is_even():
    return lax.rem(lax.axis_index("lat"), 2) == 0


def pair_kernel(line_ref, other_ref, taps_ref, inner_ref, out_ref, left_ref):
    for cols, added in other_band(line_ref, other_ref, taps_ref, left_ref, jnp.logical_not(is_even()), True):
        out_ref[:, cols] = inner_ref[:, cols] + added


def mix_kernel(line_ref, other_ref, taps_ref, inner_ref, mix_ref, out_ref, *scratch):
    left_ref, activ_ref, total_ref, state_ref, sems = scratch
    band = lax.axis_index("lat")
    inside = (band > 0) & (band < lax.axis_size("lat") - 1)
    for cols, added in other_band(line_ref, other_ref, taps_ref, left_ref, is_even(), inside):
        total = inner_ref[:, cols] + added
        activ_ref[:, cols] = jax.nn.gelu(total, approximate=True).astype(BF16)
        total_ref[:, cols] = total
    copies = []
    for c in range(mix_ref.shape[1] // BLOCK):
        cols = slice(c * BLOCK, (c + 1) * BLOCK)
        mixed = jnp.dot(activ_ref[...], mix_ref[:, cols], preferred_element_type=F32)
        state_ref[:, cols] = (total_ref[:, cols] + mixed).astype(BF16)
        copies.append(pltpu.make_async_copy(state_ref.at[:, cols], out_ref.at[:, cols], sems.at[c]))
        copies[-1].start()
    for copy in copies:
        copy.wait()


def from_neighbour(value, axis, step):
    count = lax.axis_size(axis)
    return lax.ppermute(value, axis, [((i + step) % count, i) for i in range(count)])


def swapped(value, axis, first):
    count = lax.axis_size(axis)
    pairs = [(i, (i + 1 if i % 2 == first else i - 1) % count) for i in range(count)]
    return lax.ppermute(value, axis, pairs)


def on_device(
    obs_rows, obs_cells, obs_counts, enc_weight, near_kernel_weight, far_kernel_weight, mix_weight
):
    slots, features = obs_rows.shape[2:]
    channels = mix_weight.shape[0]
    params = pltpu.CompilerParams(vmem_limit_bytes=24 << 20)
    in_vmem = pl.BlockSpec(memory_space=pltpu.VMEM)
    early = pl.pallas_call(
        ready_kernel,
        out_shape=pltpu.VMEM((8, 128), F32),
        cost_estimate=pl.CostEstimate(flops=4_000_000_000, bytes_accessed=12_000_000, transcendentals=0),
        compiler_params=params,
        name="ready",
    )()
    count, early = lax.optimization_barrier((obs_counts, early))
    sent, own = pl.pallas_call(
        sums_kernel,
        out_shape=(pltpu.VMEM((CELLS // 2, 2 * features), BF16), pltpu.VMEM((CELLS, 2 * features), BF16)),
        in_specs=[in_vmem, pl.BlockSpec(memory_space=pltpu.SMEM), in_vmem, in_vmem],
        cost_estimate=pl.CostEstimate(flops=4_000_000_000, bytes_accessed=12_000_000, transcendentals=0),
        compiler_params=params,
        name="cell_sums",
    )(early, count, obs_rows.reshape(slots, features).T, obs_cells.reshape(1, slots))
    weights = (enc_weight, near_kernel_weight, far_kernel_weight)
    taps = pl.pallas_call(
        taps_kernel,
        out_shape=pltpu.VMEM((len(OUTER_TAPS) * features, channels), BF16),
        cost_estimate=pl.CostEstimate(flops=1_600_000_000, bytes_accessed=2_500_000, transcendentals=0),
        compiler_params=params,
        name="outer_taps",
    )(*weights)
    line = jnp.stack([sent, from_neighbour(sent, "lon", -1), from_neighbour(sent, "lon", 1)])
    line, taps = lax.optimization_barrier((line, taps))
    inner = pl.pallas_call(
        inner_kernel,
        out_shape=pltpu.VMEM((CELLS, channels), F32),
        scratch_shapes=[pltpu.VMEM((8 * features, channels), BF16), pltpu.VMEM((CELLS, 8 * features), BF16)],
        cost_estimate=pl.CostEstimate(flops=1_000_000_000, bytes_accessed=2_500_000, transcendentals=0),
        compiler_params=params,
        name="inner_taps",
    )(own, line, *weights, mix_weight)
    left = pltpu.VMEM((CELLS, len(INNER_TAPS) * features), BF16)
    paired = pl.pallas_call(
        pair_kernel,
        out_shape=pltpu.VMEM((CELLS, channels), F32),
        scratch_shapes=[left],
        cost_estimate=pl.CostEstimate(flops=1_000_000, bytes_accessed=10_000, transcendentals=0),
        compiler_params=params,
        name="pair_taps",
    )(line, swapped(line, "lat", 0), taps, inner)
    mixed = pl.pallas_call(
        mix_kernel,
        out_shape=jax.ShapeDtypeStruct((CELLS, channels), BF16),
        in_specs=[in_vmem] * 5,
        out_specs=pl.BlockSpec(memory_space=pltpu.HBM),
        scratch_shapes=[
            left,
            pltpu.VMEM((CELLS, channels), BF16),
            pltpu.VMEM((CELLS, channels), F32),
            pltpu.VMEM((CELLS, channels), BF16),
            pltpu.SemaphoreType.DMA((channels // BLOCK,)),
        ],
        compiler_params=params,
        name="filter_and_mix",
    )(line, swapped(line, "lat", 1), taps, paired, mix_weight)
    return mixed.reshape(SECTOR_LON_CELLS, BAND_LAT_CELLS, channels)


def solution(mesh):
    return jax.shard_map(
        on_device,
        mesh=mesh,
        in_specs=(
            P("lon", "lat", None, None),
            P("lon", "lat", None),
            P("lon", "lat"),
            P(),
            P(),
            P(),
            P(),
        ),
        out_specs=P("lon", "lat", None),
        check_vma=False,
    )
```
